128 devices in a mesh: exp: 32 (over x_hi, z, y), fsdp: 4 (over x_lo, core).
Axes of the slice: x: 4 (x_hi: 2, x_lo: 2; x = x_hi * 2 + x_lo), y: 4, z: 4, core: 2. Of those that a mesh axis runs over, the one named last changes fastest.
Arguments:
- residual: bfloat16 [128, 4, 7168], P(('fsdp', 'exp')), may hold values from -6 to 6
- gain: float32 [7168], replicated, may hold values from 0.1 to 1.9
- queries: bfloat16 [128, 4, 32, 576], P('fsdp', None, 'exp'), may hold values from -72 to 72
- new_keys: bfloat16 [128, 4, 576], P('fsdp'), may hold values from -6 to 6
- cache: bfloat16 [128, 576, 256], P('fsdp'), may hold values from -6 to 6
- lengths: int32 [128], P('fsdp'), may hold values from 2 to 256, as said below
- w_value: bfloat16 [32, 512, 128], P('exp'), may hold values from -0.25 to 0.25
- w_out: bfloat16 [32, 128, 7168], P('exp'), may hold values from -0.5 to 0.5
- w_gate: bfloat16 [32, 7168, 1024], P(None, 'exp', 'fsdp'), may hold values from -0.0625 to 0.0625
- w_up: bfloat16 [32, 7168, 1024], P(None, 'exp', 'fsdp'), may hold values from -0.0625 to 0.0625
- w_down: bfloat16 [32, 7168, 1024], P(None, 'exp', 'fsdp'), may hold values from -0.1875 to 0.1875
- expert_ids: int32 [128, 4, 8], P(('fsdp', 'exp')), may hold values from 0 to 31, all different within a row; in each aligned block of 4 rows (0 to 3, 4 to 7, ..., all dimensions but the last counted through in order) at most 2 rows name the same one
- gates: float32 [128, 4, 8], P(('fsdp', 'exp')), may hold values from 0.1 to 1
Outputs:
- mixed: float32 [128, 4, 7168], P(('fsdp', 'exp'))
The draws below stay inside these ranges and needn't reach their ends.
Inputs may be any that keep to these rules, and one draw needn't show every extreme that they name: `expert_ids`: in the 4 rows of one device (aligned blocks of rows and steps in order), no expert is named more than 2 times. `lengths`: some row has exactly 256 cached tokens.
All inputs are finite; a program needn't handle non-finite values.
Results may differ from the reference program's by a relative error of at most 0.006.
Values may be sent and summed in bfloat16 or wider, within the bound.
A program may use at most 128 MiB of HBM per device.

```python
import math
import jax
import jax.numpy as jnp
import numpy as np
from jax import lax

D = 7168
F = 1024
LAT = 512
ROPE = 64
VH = 128
TOP = 8
STEPS = 4
ROW_DEV = 1
CACHE = 256
KD = 576
HEADS = 32
EXPERTS = 32
ROWS = 128
CAP = 2
N_EXP = 32
N_FSDP = 4


def shared_cache(key):
    return jnp.clip(jax.random.normal(key, (ROWS, LAT + ROPE, CACHE), jnp.float32), -6.0, 6.0)


def draw_cache(key, part):
    base = shared_cache(key)
    return base.astype(jnp.bfloat16)


def draw_queries(key, part):
    key = jax.random.fold_in(key, 5)
    drawn = jnp.clip(jax.random.normal(key, (ROWS, STEPS, HEADS, LAT + ROPE), jnp.float32), -6.0, 6.0)
    return drawn.astype(jnp.bfloat16)


def draw_lengths(key, part):
    key = jax.random.fold_in(key, 7)
    first_key, second_key = jax.random.split(key)
    drawn = jax.random.randint(first_key, (ROWS,), 2, CACHE + 1)
    picked = jax.random.randint(second_key, (), 0, ROWS)
    return jnp.where(jnp.arange(ROWS) == picked, CACHE, drawn).astype(jnp.int32)


def shard_levels(own_key, extent, pieces, smallest, largest):
    factor_of, own = 1.0, jax.random.fold_in(own_key, 6)
    for position, blocks in pieces:
        steps = jnp.exp(jax.random.uniform(jax.random.fold_in(own, position), (blocks,), jnp.float32, smallest / len(pieces), largest / len(pieces)))
        factor_of = factor_of * jnp.repeat(steps, extent[position] // blocks).reshape([-1 if axis == position else 1 for axis in range(len(extent))])
    return factor_of


def routed_block(rng, own, number, rows, count, top, most, slope):
    order = jax.random.permutation(rng, count)
    crowded, ordinary = portions_of(count, rows * top, most, slope, True), portions_of(count, rows * top, most, slope, False)
    places = jnp.arange(count)

    def named(sizes, offset_by):
        used = int((sizes > 0).sum())
        fixed = max(1, used // 4)
        passed = fixed + (places - fixed + offset_by * (used - fixed)) % max(1, count - fixed)
        return jnp.zeros((count,), jnp.int32).at[order[jnp.where(places < fixed, places, passed)]].set(jnp.asarray(sizes, jnp.int32))

    sizes = jnp.where(number % 4 == 0, named(crowded, number // 4), named(ordinary, number - number // 4 - 1))
    mixed = jax.random.permutation(jax.random.fold_in(own, 3), count)
    giver, sink = mixed[0:count // 2 * 2:2], mixed[1:count // 2 * 2:2]
    slack = jnp.minimum(sizes[giver] - 1, most - sizes[sink]) // 2
    slack = jnp.where((giver == order[0]) | (sink == order[0]) | (sizes[sink] == 0), 0, jnp.maximum(slack, 0))
    passed = jax.random.randint(jax.random.fold_in(own, 4), (count // 2,), 0, 1 << 20) % (slack + 1)
    sizes = sizes.at[giver].add(-passed).at[sink].add(passed)
    labels = jnp.searchsorted(jnp.cumsum(sizes), jnp.arange(rows * top), side="right").astype(jnp.int32)
    grid = labels.reshape(top, rows).T
    grid = grid[jax.random.permutation(jax.random.fold_in(own, 1), rows)]
    offset_by = jax.random.randint(jax.random.fold_in(own, 2), (rows, 1), 0, top)
    return jnp.take_along_axis(grid, (jnp.arange(top)[None, :] + offset_by) % top, axis=1)


def portions_of(number_of, total, most, skew, full):
    portions = [(1 << 20) // math.isqrt(rank ** skew) + 1 for rank in range(1, number_of + 1)]
    largest = most if full else min(most, max(-(-total // number_of), total * portions[0] // sum(portions)))
    least = 1 if total - largest >= number_of - 1 else 0
    counts, rest = [largest] + [least] * (number_of - 1), total - largest - least * (number_of - 1)
    while rest > 0:
        free = [i for i in range(1, number_of) if counts[i] < largest] or [i for i in range(1, number_of) if counts[i] < most]
        mass, left = sum([portions[i] for i in free]), rest
        for i in free:
            extra = min(most - counts[i], max(1, left * portions[i] // mass), rest)
            counts[i] = counts[i] + extra
            rest = rest - extra
    return np.array(counts)


def normal_values(own_key, shape, spread, most, shards=(), held_as=jnp.bfloat16):
    array = jax.random.normal(own_key, shape, jnp.float32) * spread
    if len(shards) > 0:
        array = shard_levels(own_key, shape, shards, -0.22, 0.18) * array
    return jnp.clip(array, min=-most, max=most).astype(held_as)


def setup_inputs(seed: int = 0) -> dict:
    streams_of = jax.random.split(jax.random.key(seed), 14)
    residual = normal_values(streams_of[0], (ROWS, STEPS, D), 1.0, 6.0, ((0, 128),))
    gain = jnp.clip(1.0 + 0.18 * jax.random.normal(streams_of[1], (D,), jnp.float32), 0.1, 1.9)
    queries = draw_queries(jax.random.fold_in(streams_of[13], 71), 0)
    new_keys = normal_values(streams_of[3], (ROWS, STEPS, KD), 1.0, 6.0, ((0, 4),))
    cache = draw_cache(jax.random.fold_in(streams_of[13], 71), 0)
    lengths = draw_lengths(jax.random.fold_in(streams_of[13], 71), 0)
    w_value = normal_values(streams_of[6], (HEADS, LAT, VH), LAT ** -0.5, 0.25, ((0, 32),))
    w_out = normal_values(streams_of[7], (HEADS, VH, D), VH ** -0.5, 0.5, ((0, 32),))
    w_gate = normal_values(streams_of[8], (EXPERTS, D, F), D ** -0.5, 0.0625, ((1, 32), (2, 4)))
    w_up = normal_values(streams_of[9], (EXPERTS, D, F), D ** -0.5, 0.0625, ((1, 32), (2, 4)))
    w_down = normal_values(streams_of[10], (EXPERTS, D, F), F ** -0.5, 0.1875, ((1, 32), (2, 4)))
    expert_ids_keys = jax.random.split(jax.random.fold_in(streams_of[11], 1), ROWS * STEPS // (ROW_DEV * STEPS))
    expert_ids_turns = jax.random.permutation(jax.random.fold_in(streams_of[11], 3), ROWS * STEPS // (ROW_DEV * STEPS))
    expert_ids = jax.vmap(lambda own, number: routed_block(jax.random.fold_in(streams_of[11], 2), own, number, ROW_DEV * STEPS, EXPERTS, TOP, CAP, 2))(expert_ids_keys, expert_ids_turns).reshape((ROWS, STEPS, TOP))
    gates = jnp.clip(0.1 + 0.9 * jax.random.uniform(streams_of[12], (ROWS, STEPS, TOP), jnp.float32) ** shard_levels(streams_of[12], (ROWS, STEPS, TOP), ((0, 128),), -0.2, 0.2), 0.1, 1.0)
    return {"residual": residual, "gain": gain, "queries": queries, "new_keys": new_keys, "cache": cache, "lengths": lengths, "w_value": w_value, "w_out": w_out, "w_gate": w_gate, "w_up": w_up, "w_down": w_down, "expert_ids": expert_ids, "gates": gates}


score_scale = 0.07216878364870322

def reference(residual, gain, queries, new_keys, cache, lengths, w_value, w_out, w_gate, w_up, w_down, expert_ids, gates):
    query_f = queries.astype(jnp.float32)
    cache_f = cache.astype(jnp.float32)
    fresh_f = new_keys.astype(jnp.float32)
    cache_scores = jnp.einsum('rthc,rcl->rthl', query_f, cache_f) * score_scale
    cache_valid = jnp.arange(CACHE, dtype=jnp.int32)[None, :] < lengths[:, None]
    cache_scores = jnp.where(cache_valid[:, None, None, :], cache_scores, -1e+30)
    new_scores = jnp.einsum('rthc,ruc->rthu', query_f, fresh_f) * score_scale
    step_index = jnp.arange(STEPS, dtype=jnp.int32)
    new_valid = step_index[None, :] <= step_index[:, None]
    new_scores = jnp.where(new_valid[None, :, None, :], new_scores, -1e+30)
    highest = jnp.maximum(lax.optimization_barrier(jnp.max(cache_scores, -1)), lax.optimization_barrier(jnp.max(new_scores, -1)))[..., None]
    cache_exp = jnp.exp(cache_scores - highest)
    new_exp = jnp.exp(new_scores - highest)
    total = (lax.optimization_barrier(jnp.sum(cache_exp, -1)) + lax.optimization_barrier(jnp.sum(new_exp, -1)))[..., None]
    cache_weights = (cache_exp / total).astype(jnp.bfloat16)
    new_weights = (new_exp / total).astype(jnp.bfloat16)
    context = jnp.einsum('rthl,rcl->rthc', cache_weights.astype(jnp.float32), cache_f[:, :LAT, :])
    context = context + jnp.einsum('rthu,ruc->rthc', new_weights.astype(jnp.float32), fresh_f[:, :, :LAT])
    context = context.astype(jnp.bfloat16)
    values = jnp.einsum('rthc,hcv->rthv', context.astype(jnp.float32), w_value.astype(jnp.float32)).astype(jnp.bfloat16)
    attention = jnp.einsum('rthv,hvd->rtd', values.astype(jnp.float32), w_out.astype(jnp.float32))
    attended = residual.astype(jnp.float32) + attention
    meansq = lax.optimization_barrier(jnp.mean(attended * attended, -1, keepdims=True))
    normed = (attended * lax.rsqrt(meansq + 1e-06) * gain).astype(jnp.bfloat16)
    row_inputs = normed.reshape(ROWS * STEPS, D)
    flat_ids = expert_ids.reshape(-1)
    flat_gates = gates.reshape(-1)
    most = N_EXP * N_FSDP * CAP
    quarter_width = F // N_FSDP

    def one_expert(expert):
        order = jnp.argsort((flat_ids != expert).astype(jnp.int32), stable=True)[:most].astype(jnp.int32)
        valid = flat_ids[order] == expert
        picked = row_inputs[order // TOP]
        gate_mat = lax.dynamic_index_in_dim(w_gate, expert, 0, False)
        up_mat = lax.dynamic_index_in_dim(w_up, expert, 0, False)
        down_mat = lax.dynamic_index_in_dim(w_down, expert, 0, False)
        summed = jnp.zeros((most, D), jnp.float32)
        for quarter in range(N_FSDP):
            lower = quarter * quarter_width
            upper = lower + quarter_width
            gate_part = jnp.dot(picked, gate_mat[:, lower:upper], preferred_element_type=jnp.float32)
            up_part = jnp.dot(picked, up_mat[:, lower:upper], preferred_element_type=jnp.float32)
            hidden = (jax.nn.silu(gate_part) * up_part).astype(jnp.bfloat16)
            share = jnp.dot(hidden, down_mat[:, lower:upper].T, preferred_element_type=jnp.float32)
            share = lax.optimization_barrier(share.astype(jnp.bfloat16))
            summed = summed + share.astype(jnp.float32)
        weighted = jnp.where(valid[:, None], summed * flat_gates[order][:, None], 0.0)
        return (order, weighted)
    orders, contribs = lax.map(one_expert, jnp.arange(EXPERTS, dtype=jnp.int32))
    routed = jnp.zeros((ROWS * STEPS, D), jnp.float32).at[(orders // TOP).reshape(-1)].add(contribs.reshape(-1, D))
    mixed = attended + routed.reshape(ROWS, STEPS, D)
    return mixed
```

```python
import functools

import jax
import jax.numpy as jnp
from jax import lax
from jax.experimental import pallas as pl
from jax.experimental.pallas import tpu as pltpu
from jax.sharding import PartitionSpec as P

TOP = 8
score_scale = 0.07216878364870322
MESH = pl.DeviceIdType.MESH
BF = jnp.bfloat16
F32 = jnp.float32
WIDE = 256
HIGH = 56 * 1024 * 1024

NT = (((1,), (1,)), ((), ()))
TN = (((0,), (0,)), ((), ()))


def matmul(a, b):
    return jnp.dot(a, b, preferred_element_type=F32)


def vmem():
    return pl.BlockSpec(memory_space=pltpu.VMEM)


def anywhere():
    return pl.BlockSpec(memory_space=pl.ANY)


def greet(barrier, axis, me, size):
    def one(d, carry):
        pl.semaphore_signal(
            barrier, inc=1, device_id={axis: lax.rem(me + d, size)}, device_id_type=MESH
        )
        return carry

    lax.fori_loop(1, size, one, 0)


def each(lower, upper, body):
    def step(i, carry):
        body(i)
        return carry

    lax.fori_loop(lower, upper, step, 0)


def attend_kernel(
    peers,
    groups,
    q_ref,
    nk_ref,
    cache_ref,
    len_ref,
    wv_ref,
    wo_ref,
    res_ref,
    gain_ref,
    xall_ref,
    att_ref,
    cache_v,
    wo_s,
    new_s,
    ctx_s,
    send_v,
    recv_v,
    ssq_s,
    ssq_r,
    nrm_v,
    cache_sem,
    send_sem,
    recv_sem,
    ssq_send,
    ssq_recv,
    f_send,
    f_recv,
    own_sem,
):
    me = lax.axis_index("exp")
    fs = lax.axis_index("fsdp")
    tokens = q_ref.shape[0]
    latent = wv_ref.shape[0]
    chunks = cache_sem.shape[0]
    per = tokens // chunks
    cache_per = cache_ref.shape[0] // chunks
    width = wo_ref.shape[1] // peers
    barrier = pltpu.get_barrier_semaphore()
    greet(barrier, "exp", me, peers)
    greet(barrier, "fsdp", fs, groups)

    def cache_copy(c):
        rows = pl.ds(c * cache_per, cache_per)
        return pltpu.make_async_copy(cache_ref.at[rows], cache_v.at[rows], cache_sem.at[c])

    for c in range(chunks):
        cache_copy(c).start()

    pad = jnp.zeros((wo_ref.shape[0], WIDE - width), BF)
    for j in range(peers):
        wo_s[j] = jnp.concatenate([wo_ref[:, j * width : (j + 1) * width], pad], axis=1)

    token_r = lax.broadcasted_iota(jnp.int32, (tokens, tokens), 0)
    token_c = lax.broadcasted_iota(jnp.int32, (tokens, tokens), 1)
    same = (token_r // 4 == token_c // 4) & (token_c <= token_r)
    fresh = lax.dot_general(q_ref[...], nk_ref[...], NT, preferred_element_type=F32)
    new_s[...] = jnp.where(same, fresh * score_scale, -1e30)

    def send_copy(c, d):
        peer = lax.rem(me + d, peers)
        rows = pl.ds(pl.multiple_of(c * per, 16), per)
        return pltpu.make_async_remote_copy(
            src_ref=send_v.at[peer, rows],
            dst_ref=recv_v.at[me, rows],
            send_sem=send_sem.at[c, d],
            recv_sem=recv_sem.at[c, me],
            device_id={"exp": peer},
            device_id_type=MESH,
        )

    def recv_copy(c, d):
        peer = lax.rem(me + d, peers)
        rows = pl.ds(pl.multiple_of(c * per, 16), per)
        return pltpu.make_async_remote_copy(
            src_ref=send_v.at[peer, rows],
            dst_ref=recv_v.at[peer, rows],
            send_sem=send_sem.at[c, d],
            recv_sem=recv_sem.at[c, peer],
            device_id={"exp": peer},
            device_id_type=MESH,
        )

    which = lax.broadcasted_iota(jnp.int32, (16, 1), 0) // 4
    lane = lax.broadcasted_iota(jnp.int32, (16, cache_ref.shape[2]), 1)
    mine = (lax.broadcasted_iota(jnp.int32, (per, 1), 0) // 4) + 0

    for c in range(chunks):
        cache_copy(c).wait()

        def block(g, c=c):
            rows = pl.ds(pl.multiple_of(c * per + g * 16, 16), 16)
            first = c * cache_per + g * 4
            q16 = q_ref[rows, :]
            scores = matmul(q16, cache_v[first])
            for i in range(1, 4):
                scores = jnp.where(which == i, matmul(q16, cache_v[first + i]), scores)
            scores = jnp.where(lane < len_ref[rows, :], scores * score_scale, -1e30)
            new = new_s[rows, :]
            highest = jnp.maximum(
                jnp.max(scores, -1, keepdims=True), jnp.max(new, -1, keepdims=True)
            )
            cache_exp = jnp.exp(scores - highest)
            new_exp = jnp.exp(new - highest)
            total = jnp.sum(cache_exp, -1, keepdims=True) + jnp.sum(new_exp, -1, keepdims=True)
            cache_w = (cache_exp / total).astype(BF)
            new_w = (new_exp / total).astype(BF)
            context = lax.dot_general(
                cache_w, cache_v[first, :latent, :], NT, preferred_element_type=F32
            )
            for i in range(1, 4):
                part = lax.dot_general(
                    cache_w, cache_v[first + i, :latent, :], NT, preferred_element_type=F32
                )
                context = jnp.where(which == i, part, context)
            context = context + matmul(new_w, nk_ref[:, :latent])
            ctx_s[pl.ds(pl.multiple_of(g * 16, 16), 16), :] = context.astype(BF)

        each(0, per // 16, block)
        values = matmul(ctx_s[...], wv_ref[...]).astype(BF)
        own_rows = mine + c * (per // 4) == me

        def project(j, c=c, values=values, own_rows=own_rows):
            part = matmul(values, wo_s[j])
            res = jnp.concatenate([res_ref[j]] * (per // 16), axis=0).astype(F32)
            part = part + jnp.where(own_rows, res, 0.0)
            send_v[j, c * per : (c + 1) * per, :] = part.astype(BF)

        each(0, peers, project)
        if c == 0:
            pl.semaphore_wait(barrier, peers - 1 + groups - 1)
        each(1, peers, lambda d, c=c: send_copy(c, d).start())

    def add(d, acc):
        for c in range(chunks):
            recv_copy(c, d).wait_recv()
        return acc + recv_v[lax.rem(me + d, peers)].astype(F32)

    attended = lax.fori_loop(1, peers, add, send_v[me].astype(F32))
    att_ref[...] = attended

    diagonal = token_r == token_c
    column = jnp.sum(attended * attended, -1, keepdims=True)
    row = jnp.sum(jnp.where(diagonal, column, 0.0), 0, keepdims=True)
    ssq_s[...] = jnp.broadcast_to(row, ssq_s.shape)

    def ssq_copy(d, slot):
        peer = lax.rem(me + d, peers)
        return pltpu.make_async_remote_copy(
            src_ref=ssq_s,
            dst_ref=ssq_r.at[slot],
            send_sem=ssq_send.at[d],
            recv_sem=ssq_recv.at[slot],
            device_id={"exp": peer},
            device_id_type=MESH,
        )

    each(1, peers, lambda d: ssq_copy(d, me).start())

    def add_ssq(d, acc):
        slot = lax.rem(me + d, peers)
        ssq_copy(d, slot).wait_recv()
        return acc + ssq_r[slot]

    total = lax.fori_loop(1, peers, add_ssq, ssq_s[...])[:1, :]
    column = jnp.sum(jnp.where(diagonal, total, 0.0), 1, keepdims=True)
    scale = lax.rsqrt(column / (width * peers) + 1e-06)
    nrm_v[...] = (attended * scale * gain_ref[...]).astype(BF)

    own = pltpu.make_async_copy(nrm_v, xall_ref.at[fs], own_sem)
    own.start()

    def group_copy(d, slot):
        return pltpu.make_async_remote_copy(
            src_ref=nrm_v,
            dst_ref=xall_ref.at[slot],
            send_sem=f_send.at[d],
            recv_sem=f_recv.at[slot],
            device_id={"fsdp": lax.rem(fs + d, groups)},
            device_id_type=MESH,
        )

    for d in range(1, groups):
        group_copy(d, fs).start()
    for d in range(1, groups):
        group_copy(d, lax.rem(fs + d, groups)).wait_recv()
    own.wait()

    def finish(d):
        for c in range(chunks):
            send_copy(c, d).wait_send()
        ssq_copy(d, me).wait_send()

    each(1, peers, finish)
    for d in range(1, groups):
        group_copy(d, fs).wait_send()


def attend(q, nk, cache, lens, wv, wo, res, gain, peers, groups):
    tokens = q.shape[0]
    chunks = 4
    per = tokens // chunks
    return pl.pallas_call(
        functools.partial(attend_kernel, peers, groups),
        out_shape=(
            jax.ShapeDtypeStruct((groups, tokens, WIDE), BF),
            jax.ShapeDtypeStruct((tokens, WIDE), F32),
        ),
        in_specs=[vmem(), vmem(), anywhere()] + [vmem()] * 5,
        out_specs=(anywhere(), vmem()),
        scratch_shapes=[
            pltpu.VMEM(cache.shape, BF),
            pltpu.VMEM((peers, wo.shape[0], WIDE), BF),
            pltpu.VMEM((tokens, tokens), F32),
            pltpu.VMEM((per, wv.shape[0]), BF),
            pltpu.VMEM((peers, tokens, WIDE), BF),
            pltpu.VMEM((peers, tokens, WIDE), BF),
            pltpu.VMEM((8, tokens), F32),
            pltpu.VMEM((peers, 8, tokens), F32),
            pltpu.VMEM((tokens, WIDE), BF),
            pltpu.SemaphoreType.DMA((chunks,)),
            pltpu.SemaphoreType.DMA((chunks, peers)),
            pltpu.SemaphoreType.DMA((chunks, peers)),
            pltpu.SemaphoreType.DMA((peers,)),
            pltpu.SemaphoreType.DMA((peers,)),
            pltpu.SemaphoreType.DMA((groups,)),
            pltpu.SemaphoreType.DMA((groups,)),
            pltpu.SemaphoreType.DMA,
        ],
        compiler_params=pltpu.CompilerParams(
            collective_id=0, has_side_effects=True, vmem_limit_bytes=HIGH
        ),
        name="attend",
    )(q, nk, cache, lens, wv, wo, res, gain)


def gate_up_kernel(lo_ref, hi_ref, x_ref, pos_ref, wg_ref, wu_ref, out_ref, acc):
    tiles, rows, wide = out_ref.shape
    half = wide // 2
    tokens = x_ref.shape[0]
    depth = wg_ref.shape[1]
    line = lax.broadcasted_iota(jnp.int32, (rows, tokens), 0)

    def tile(t):
        acc[...] = jnp.zeros_like(acc)

        def visit(e):
            place = (pos_ref[e] - t * rows == line).astype(F32).astype(BF)
            picked = matmul(place, x_ref[...]).astype(BF)[:, :depth]
            acc[:, :half] += matmul(picked, wg_ref[e])
            acc[:, half:] += matmul(picked, wu_ref[e])

        each(lo_ref[t], hi_ref[t], visit)
        out_ref[t] = acc[...].astype(BF)

    each(0, tiles, tile)


def gate_up(lo, hi, x, pos, wg, wu, tiles, rows):
    smem = pl.BlockSpec(memory_space=pltpu.SMEM)
    return pl.pallas_call(
        gate_up_kernel,
        out_shape=jax.ShapeDtypeStruct((tiles, rows, 2 * wg.shape[2]), BF),
        in_specs=[smem, smem] + [vmem()] * 4,
        out_specs=vmem(),
        scratch_shapes=[pltpu.VMEM((rows, 2 * wg.shape[2]), F32)],
        compiler_params=pltpu.CompilerParams(vmem_limit_bytes=HIGH),
        name="gate_up",
    )(lo, hi, x, pos, wg, wu)


def hidden_kernel(peers, part_ref, hid_ref, recv_v, acc, hid_v, r_send, r_recv, g_send, g_recv, own_sem):
    me = lax.axis_index("exp")
    half = hid_v.shape[1]
    barrier = pltpu.get_barrier_semaphore()
    greet(barrier, "exp", me, peers)
    own = pltpu.make_async_copy(part_ref.at[me], recv_v.at[me], own_sem.at[0])
    own.start()
    pl.semaphore_wait(barrier, peers - 1)

    def part_copy(d, slot):
        peer = lax.rem(me + d, peers)
        return pltpu.make_async_remote_copy(
            src_ref=part_ref.at[peer],
            dst_ref=recv_v.at[slot],
            send_sem=r_send.at[d],
            recv_sem=r_recv.at[slot],
            device_id={"exp": peer},
            device_id_type=MESH,
        )

    each(1, peers, lambda d: part_copy(d, me).start())
    own.wait()
    acc[...] = recv_v[me].astype(F32)

    def add(d):
        slot = lax.rem(me + peers - d, peers)
        part_copy(d, slot).wait_recv()
        acc[...] += recv_v[slot].astype(F32)

    each(1, peers, add)
    gate = acc[:, :half]
    hid_v[...] = (gate / (1.0 + jnp.exp(-gate)) * acc[:, half:]).astype(BF)

    def hid_copy(d, slot):
        peer = lax.rem(me + d, peers)
        return pltpu.make_async_remote_copy(
            src_ref=hid_v,
            dst_ref=hid_ref.at[slot],
            send_sem=g_send.at[d],
            recv_sem=g_recv.at[slot],
            device_id={"exp": peer},
            device_id_type=MESH,
        )

    own = pltpu.make_async_copy(hid_v, hid_ref.at[me], own_sem.at[1])
    own.start()
    each(1, peers, lambda d: hid_copy(d, me).start())
    own.wait()

    def finish(d):
        part_copy(d, me).wait_send()
        hid_copy(d, lax.rem(me + peers - d, peers)).wait_recv()
        hid_copy(d, me).wait_send()

    each(1, peers, finish)


def hidden(part, peers):
    tiles, rows, wide = part.shape
    return pl.pallas_call(
        functools.partial(hidden_kernel, peers),
        out_shape=jax.ShapeDtypeStruct((tiles, rows, wide // 2), BF),
        in_specs=[anywhere()],
        out_specs=anywhere(),
        scratch_shapes=[
            pltpu.VMEM((peers, rows, wide), BF),
            pltpu.VMEM((rows, wide), F32),
            pltpu.VMEM((rows, wide // 2), BF),
            pltpu.SemaphoreType.DMA((peers,)),
            pltpu.SemaphoreType.DMA((peers,)),
            pltpu.SemaphoreType.DMA((peers,)),
            pltpu.SemaphoreType.DMA((peers,)),
            pltpu.SemaphoreType.DMA((2,)),
        ],
        compiler_params=pltpu.CompilerParams(
            collective_id=1, has_side_effects=True, vmem_limit_bytes=HIGH
        ),
        name="hidden",
    )(part)


def down_kernel(lo_ref, hi_ref, hid_ref, pos_ref, gate_ref, wd_ref, out_ref, acc):
    tiles, rows, _ = hid_ref.shape
    tokens = pos_ref.shape[2]
    depth = wd_ref.shape[1]
    line = lax.broadcasted_iota(jnp.int32, (rows, tokens), 0)
    acc[...] = jnp.zeros_like(acc)

    def tile(t):
        def visit(e):
            hit = pos_ref[e] - t * rows == line
            share = lax.dot_general(hid_ref[t], wd_ref[e], NT, preferred_element_type=F32)
            weight = jnp.sum(jnp.where(hit, gate_ref[e], 0.0), 1, keepdims=True)
            share = (share * weight).astype(BF)
            acc[:, :depth] += lax.dot_general(
                hit.astype(F32).astype(BF), share, TN, preferred_element_type=F32
            )

        each(lo_ref[t], hi_ref[t], visit)

    each(0, tiles, tile)
    out_ref[...] = acc[...].astype(BF)


def down(lo, hi, hid, pos, gate, wd):
    smem = pl.BlockSpec(memory_space=pltpu.SMEM)
    tokens = pos.shape[2]
    return pl.pallas_call(
        down_kernel,
        out_shape=jax.ShapeDtypeStruct((tokens, WIDE), BF),
        in_specs=[smem, smem] + [vmem()] * 4,
        out_specs=vmem(),
        scratch_shapes=[pltpu.VMEM((tokens, WIDE), F32)],
        compiler_params=pltpu.CompilerParams(vmem_limit_bytes=HIGH),
        name="down",
    )(lo, hi, hid, pos, gate, wd)


def finish_kernel(
    peers, groups, routed_ref, att_ref, out_ref, recv_v, send_v, f_send, f_recv, o_send, o_recv, own_sem
):
    me = lax.axis_index("exp")
    fs = lax.axis_index("fsdp")
    own_rows = send_v.shape[1]
    barrier = pltpu.get_barrier_semaphore()
    greet(barrier, "exp", me, peers)
    greet(barrier, "fsdp", fs, groups)
    pl.semaphore_wait(barrier, peers - 1 + groups - 1)

    def group_copy(d, slot):
        peer = lax.rem(fs + d, groups)
        return pltpu.make_async_remote_copy(
            src_ref=routed_ref.at[peer],
            dst_ref=recv_v.at[slot],
            send_sem=f_send.at[d],
            recv_sem=f_recv.at[slot],
            device_id={"fsdp": peer},
            device_id_type=MESH,
        )

    for d in range(1, groups):
        group_copy(d, fs).start()
    mixed = att_ref[...] + routed_ref[fs].astype(F32)
    for d in range(1, groups):
        slot = lax.rem(fs + d, groups)
        group_copy(d, slot).wait_recv()
        mixed = mixed + recv_v[slot].astype(F32)
    for j in range(peers):
        send_v[j] = mixed[j * own_rows : (j + 1) * own_rows, :]

    def out_copy(d, slot):
        peer = lax.rem(me + d, peers)
        return pltpu.make_async_remote_copy(
            src_ref=send_v.at[peer],
            dst_ref=out_ref.at[slot],
            send_sem=o_send.at[d],
            recv_sem=o_recv.at[slot],
            device_id={"exp": peer},
            device_id_type=MESH,
        )

    own = pltpu.make_async_copy(send_v.at[me], out_ref.at[me], own_sem)
    own.start()
    each(1, peers, lambda d: out_copy(d, me).start())
    own.wait()

    def close(d):
        out_copy(d, lax.rem(me + peers - d, peers)).wait_recv()
        out_copy(d, me).wait_send()

    each(1, peers, close)
    for d in range(1, groups):
        group_copy(d, fs).wait_send()


def finish(routed, att, peers, groups):
    tokens = att.shape[0]
    return pl.pallas_call(
        functools.partial(finish_kernel, peers, groups),
        out_shape=jax.ShapeDtypeStruct((peers, tokens // peers, WIDE), F32),
        in_specs=[vmem(), vmem()],
        out_specs=anywhere(),
        scratch_shapes=[
            pltpu.VMEM((groups, tokens, WIDE), BF),
            pltpu.VMEM((peers, tokens // peers, WIDE), F32),
            pltpu.SemaphoreType.DMA((groups,)),
            pltpu.SemaphoreType.DMA((groups,)),
            pltpu.SemaphoreType.DMA((peers,)),
            pltpu.SemaphoreType.DMA((peers,)),
            pltpu.SemaphoreType.DMA,
        ],
        compiler_params=pltpu.CompilerParams(
            collective_id=2, has_side_effects=True, vmem_limit_bytes=HIGH
        ),
        name="finish",
    )(routed, att)


def routing(expert_ids, gates, experts, tiles, rows):
    ids = expert_ids.reshape(-1, TOP)
    flat = jnp.concatenate([ids.astype(F32), gates.reshape(-1, TOP)], axis=1)
    everyone = lax.all_gather(flat, ("fsdp", "exp"), axis=0, tiled=True)
    ids = everyone[:, :TOP].astype(jnp.int32)
    chosen = ids[:, :, None] == jnp.arange(experts, dtype=jnp.int32)[None, None, :]
    gate = jnp.sum(jnp.where(chosen, everyone[:, TOP:, None], 0.0), 1)
    hits = jnp.any(chosen, 1)
    tokens = ids.shape[0]
    order = jnp.arange(tokens, dtype=jnp.int32)
    before = (order[None, :] < order[:, None]).astype(BF)
    rank = matmul(before, hits.astype(BF)).astype(jnp.int32)
    counts = jnp.sum(hits.astype(jnp.int32), 0)
    numbers = jnp.arange(experts, dtype=jnp.int32)
    starts = jnp.sum(jnp.where(numbers[None, :] < numbers[:, None], counts[None, :], 0), 1)
    ends = starts + counts
    pos = jnp.where(hits, rank + starts[None, :], -1)
    edge = jnp.arange(tiles, dtype=jnp.int32) * rows
    lo = jnp.sum((ends[None, :] <= edge[:, None]).astype(jnp.int32), 1)
    hi = jnp.sum((starts[None, :] < edge[:, None] + rows).astype(jnp.int32), 1)
    return lo, hi, pos.T.reshape(experts, 1, tokens), gate.T.reshape(experts, 1, tokens)


def shards(
    residual,
    gain,
    queries,
    new_keys,
    cache,
    lengths,
    w_value,
    w_out,
    w_gate,
    w_up,
    w_down,
    expert_ids,
    gates,
):
    peers = lax.axis_size("exp")
    groups = lax.axis_size("fsdp")
    group_rows, steps, _, key = queries.shape
    tokens = group_rows * steps
    model = residual.shape[2]
    width = model // peers
    experts = w_gate.shape[0]
    pairs = tokens * groups * TOP
    rows = pairs // peers

    lo, hi, pos, gate = routing(expert_ids, gates, experts, peers, rows)

    res = residual.reshape(steps, peers, width).transpose(1, 0, 2)
    res = jnp.pad(jnp.tile(res, (1, 16 // steps, 1)), ((0, 0), (0, 0), (0, WIDE - width)))
    own_gain = lax.dynamic_slice(gain, (lax.axis_index("exp") * width,), (width,))
    own_gain = jnp.pad(own_gain, (0, WIDE - width)).reshape(1, WIDE)
    lens = jnp.repeat(lengths, steps).reshape(tokens, 1)
    xall, att = attend(
        queries.reshape(tokens, key),
        new_keys.reshape(tokens, key),
        cache,
        lens,
        w_value[0],
        w_out[0],
        res,
        own_gain,
        peers,
        groups,
    )
    part = gate_up(
        lo, hi, xall.reshape(groups * tokens, WIDE), pos, w_gate, w_up, peers, rows
    )
    hid = hidden(part, peers)
    routed = down(lo, hi, hid, pos, gate, w_down)
    out = finish(routed.reshape(groups, tokens, WIDE), att, peers, groups)
    return out[:, :, :width].transpose(1, 0, 2).reshape(residual.shape)


def solution(mesh):
    return jax.shard_map(
        shards,
        mesh=mesh,
        in_specs=(
            P(("fsdp", "exp"), None, None),
            P(),
            P("fsdp", None, "exp", None),
            P("fsdp", None, None),
            P("fsdp", None, None),
            P("fsdp"),
            P("exp", None, None),
            P("exp", None, None),
            P(None, "exp", "fsdp"),
            P(None, "exp", "fsdp"),
            P(None, "exp", "fsdp"),
            P(("fsdp", "exp"), None, None),
            P(("fsdp", "exp"), None, None),
        ),
        out_specs=P(("fsdp", "exp"), None, None),
        check_vma=False,
    )
```

```python
import functools

import jax
import jax.numpy as jnp
from jax import lax
from jax.experimental import pallas as pl
from jax.experimental.pallas import tpu as pltpu
from jax.sharding import PartitionSpec as P

TOP = 8
STEPS = 4
score_scale = 0.07216878364870322
MESH = pl.DeviceIdType.MESH
BF = jnp.bfloat16
F32 = jnp.float32
WIDE = 256
HIGH = 58 * 1024 * 1024
NX, NZ, NY = 2, 4, 4
NT = (((1,), (1,)), ((), ()))


def matmul(a, b):
    return jnp.dot(a, b, preferred_element_type=F32)


def vmem():
    return pl.BlockSpec(memory_space=pltpu.VMEM)


def anywhere():
    return pl.BlockSpec(memory_space=pl.ANY)


def greet(barrier, axis, me, size):
    def one(d):
        pl.semaphore_signal(
            barrier, inc=1, device_id={axis: lax.rem(me + d, size)}, device_id_type=MESH
        )

    each(1, size, one)


def each(lower, upper, body):
    def step(i, carry):
        body(i)
        return carry

    lax.fori_loop(lower, upper, step, 0)


class Place:
    def __init__(self):
        self.me = lax.axis_index("exp")
        self.x = self.me // (NZ * NY)
        self.z = lax.rem(self.me // NY, NZ)
        self.y = lax.rem(self.me, NY)

    def index(self, x, z, y):
        return (lax.rem(x, NX) * NZ + lax.rem(z, NZ)) * NY + lax.rem(y, NY)

    def plus(self, offset):
        dx, dz, dy = offset
        return self.index(self.x + dx, self.z + dz, self.y + dy)

    def minus(self, offset):
        dx, dz, dy = offset
        return self.index(self.x + NX - dx, self.z + NZ - dz, self.y + NY - dy)


class Route:
    def __init__(self, kind, first, count):
        self.kind = kind
        self.first, self.count = first, count
        self.rows = pl.ds(first, count)
        self.line = NX if kind == "x" else NZ
        self.plane = NX * NZ * NY // self.line

    def offset(self, d, g):
        if self.kind == "z":
            return (g // NY, d, lax.rem(g, NY))
        if self.kind == "y":
            return (g // NZ, lax.rem(g, NZ), d)
        return (d, g // NY, lax.rem(g, NY))

    def split(self, offset):
        dx, dz, dy = offset
        if self.kind == "z":
            return dz, dx * NY + dy
        if self.kind == "y":
            return dy, dx * NZ + dz
        return dx, dz * NY + dy


ROUTES = (Route("z", 0, 48), Route("y", 48, 48), Route("x", 96, 32))


def remote(src, dst, send, recv, peer):
    return pltpu.make_async_remote_copy(
        src_ref=src,
        dst_ref=dst,
        send_sem=send,
        recv_sem=recv,
        device_id={"exp": peer},
        device_id_type=MESH,
    )


class Reduce:
    def __init__(self, place, route, src, bufs):
        self.place, self.route, self.src = place, route, src
        self.got, self.out, self.fin, self.s1, self.r1, self.s2, self.r2 = bufs

    def first(self, d, g):
        route = self.route
        return remote(
            self.src.at[self.place.plus(route.offset(d, g)), route.rows],
            self.got.at[d - 1, g],
            self.s1.at[d - 1, g],
            self.r1.at[d - 1, g],
            self.place.plus(route.offset(d, 0)),
        )

    def second(self, g):
        return remote(
            self.out.at[g],
            self.fin.at[g],
            self.s2.at[g],
            self.r2.at[g],
            self.place.plus(self.route.offset(0, g)),
        )

    def send(self, offset):
        d, g = self.route.split(offset)

        @pl.when(d > 0)
        def _():
            self.first(d, g).start()

    def combined(self, g):
        route = self.route
        total = self.src[self.place.plus(route.offset(0, g)), route.rows].astype(F32)
        for d in range(1, route.line):
            self.first(d, g).wait_recv()
            total = total + self.got[d - 1, g].astype(F32)
        return total

    def relay(self, g):
        self.out[g] = self.combined(g).astype(BF)
        self.second(g).start()

    def add(self, g, acc_ref):
        self.second(g).wait_recv()
        acc_ref[self.route.rows] += self.fin[g].astype(F32)

    def finish(self):
        route = self.route

        def one(g):
            for d in range(1, route.line):
                self.first(d, g).wait_send()

        each(0, route.plane, one)
        each(1, route.plane, lambda g: self.second(g).wait_send())


def reduce_scratch(route, cols):
    lines, plane = route.line - 1, route.plane
    return [
        pltpu.VMEM((lines, plane, route.count, cols), BF),
        pltpu.VMEM((plane, route.count, cols), BF),
        pltpu.VMEM((plane, route.count, cols), BF),
        pltpu.SemaphoreType.DMA((lines, plane)),
        pltpu.SemaphoreType.DMA((lines, plane)),
        pltpu.SemaphoreType.DMA((plane,)),
        pltpu.SemaphoreType.DMA((plane,)),
    ]


class Gather:
    def __init__(self, place, route, whole, bufs):
        self.place, self.route, self.whole = place, route, whole
        self.s1, self.s2, self.r = bufs

    def near(self, g, source):
        block = self.whole.at[source, self.route.rows]
        return remote(
            block, block, self.s1.at[g], self.r.at[0, g], self.place.plus(self.route.offset(0, g))
        )

    def far(self, d, g, source):
        block = self.whole.at[source, self.route.rows]
        return remote(
            block,
            block,
            self.s2.at[d - 1, g],
            self.r.at[d, g],
            self.place.plus(self.route.offset(d, 0)),
        )

    def begin(self):
        each(1, self.route.plane, lambda g: self.near(g, self.place.me).start())
        self.forward(0)

    def forward(self, g):
        source = self.place.minus(self.route.offset(0, g))
        for d in range(1, self.route.line):
            self.far(d, g, source).start()

    def relay(self, g):
        self.near(g, self.place.minus(self.route.offset(0, g))).wait_recv()
        self.forward(g)

    def arrive(self, offset):
        d, g = self.route.split(offset)

        @pl.when(d > 0)
        def _():
            self.far(d, g, self.place.minus(offset)).wait_recv()

    def finish(self):
        route = self.route

        def one(g):
            source = self.place.minus(route.offset(0, g))
            for d in range(1, route.line):
                self.far(d, g, source).wait_send()

        each(0, route.plane, one)
        each(1, route.plane, lambda g: self.near(g, self.place.me).wait_send())


def gather_scratch(route):
    lines, plane = route.line - 1, route.plane
    return [
        pltpu.SemaphoreType.DMA((plane,)),
        pltpu.SemaphoreType.DMA((lines, plane)),
        pltpu.SemaphoreType.DMA((route.line, plane)),
    ]


def offset_of(o):
    return (o // (NZ * NY), lax.rem(o // NY, NZ), lax.rem(o, NY))


def spread(block, lanes):
    wide = jnp.concatenate([block] * (lanes // block.shape[1]), axis=1)
    step = lax.rem(lax.broadcasted_iota(jnp.int32, wide.shape, 1) // TOP, STEPS)
    row = lax.broadcasted_iota(jnp.int32, wide.shape, 0)
    return jnp.sum(jnp.where(step == row, wide, 0.0), 0, keepdims=True)


def attend_kernel(peers, groups, *refs):
    (
        len_ref,
        q_ref,
        nk_ref,
        cache_ref,
        wv_ref,
        wo_ref,
        res_ref,
        gain_ref,
        ids_ref,
        gates_ref,
        xall_ref,
        att_ref,
        meta_ref,
        cache_v,
        wo_s,
        res_s,
        q_s,
        nk_s,
        new_s,
        ctx_s,
        send_v,
        acc,
        ssq_s,
        ssq_r,
        nrm_v,
        meta_v,
        cache_sem,
        ssq_send,
        ssq_recv,
        meta_send,
        meta_recv,
        f_send,
        f_recv,
        m_send,
        m_recv,
        own_sem,
    ) = refs[:36]
    place = Place()
    me = place.me
    fs = lax.axis_index("fsdp")
    tokens = q_s.shape[0]
    latent = wv_ref.shape[0]
    width = wo_ref.shape[1] // peers
    barrier = pltpu.get_barrier_semaphore()
    greet(barrier, "exp", me, peers)
    greet(barrier, "fsdp", fs, groups)
    sums = [Reduce(place, r, send_v, refs[36 + 7 * i : 43 + 7 * i]) for i, r in enumerate(ROUTES)]

    def cache_copy(i):
        rows = pl.ds(ROUTES[i].first // STEPS, ROUTES[i].count // STEPS)
        return pltpu.make_async_copy(cache_ref.at[rows], cache_v.at[rows], cache_sem.at[i])

    for i in range(len(ROUTES)):
        cache_copy(i).start()

    lane = lax.broadcasted_iota(jnp.int32, (1, 128), 1)
    here = lane // (STEPS * TOP) == lax.rem(me, 4)
    own_ids = jnp.where(here, spread(ids_ref[0].astype(F32), 128), 0.0)
    own_gates = jnp.where(here, spread(gates_ref[0], 128), 0.0)
    meta_v[me] = jnp.concatenate([own_ids, own_gates, jnp.zeros((6, 128), F32)], axis=0)

    def meta_copy(d, slot):
        return remote(
            meta_v.at[slot],
            meta_v.at[slot],
            meta_send.at[d],
            meta_recv.at[slot],
            lax.rem(me + d, peers),
        )

    for b in range(tokens // 16):
        rows = slice(b * 16, b * 16 + 16)
        q_s[rows, :] = jnp.concatenate(
            [q_ref[4 * b + i].astype(F32) for i in range(4)], axis=0
        ).astype(BF)
        nk_s[rows, :] = jnp.concatenate(
            [nk_ref[4 * b + i].astype(F32) for i in range(4)], axis=0
        ).astype(BF)

    gain = jnp.zeros((1, width), F32)
    pad = jnp.zeros((wo_ref.shape[0], WIDE - width), BF)
    res_pad = jnp.zeros((16, WIDE - width), F32)
    for j in range(peers):
        part = slice(j * width, (j + 1) * width)
        wo_s[j] = jnp.concatenate([wo_ref[:, part], pad], axis=1)
        res = jnp.concatenate([res_ref[0, :, part].astype(F32)] * 4, axis=0)
        res_s[j] = jnp.concatenate([res, res_pad], axis=1)
        gain = jnp.where(me == j, gain_ref[:, part], gain)
    gain = jnp.concatenate([gain, jnp.zeros((1, WIDE - width), F32)], axis=1)

    token_r = lax.broadcasted_iota(jnp.int32, (tokens, tokens), 0)
    token_c = lax.broadcasted_iota(jnp.int32, (tokens, tokens), 1)
    same = (token_r // STEPS == token_c // STEPS) & (token_c <= token_r)
    fresh = lax.dot_general(q_s[...], nk_s[...], NT, preferred_element_type=F32)
    new_s[...] = jnp.where(same, fresh * score_scale, -1e30)

    pl.semaphore_wait(barrier, peers - 1 + groups - 1)
    each(1, peers, lambda d: meta_copy(d, me).start())

    which = lax.broadcasted_iota(jnp.int32, (16, 1), 0) // STEPS
    position = lax.broadcasted_iota(jnp.int32, (16, cache_ref.shape[2]), 1)

    for i, route in enumerate(ROUTES):
        cache_copy(i).wait()

        def block(b, route=route):
            rows = pl.ds(pl.multiple_of(b * 16, 16), 16)
            first = b * 4
            q16 = q_s[rows, :]
            scores = matmul(q16, cache_v[first])
            length = jnp.full(position.shape, len_ref[first])
            for n in range(1, 4):
                scores = jnp.where(which == n, matmul(q16, cache_v[first + n]), scores)
                length = jnp.where(which == n, len_ref[first + n], length)
            scores = jnp.where(position < length, scores * score_scale, -1e30)
            new = new_s[rows, :]
            highest = jnp.maximum(
                jnp.max(scores, -1, keepdims=True), jnp.max(new, -1, keepdims=True)
            )
            cache_exp = jnp.exp(scores - highest)
            new_exp = jnp.exp(new - highest)
            total = jnp.sum(cache_exp, -1, keepdims=True) + jnp.sum(new_exp, -1, keepdims=True)
            cache_w = (cache_exp / total).astype(BF)
            new_w = (new_exp / total).astype(BF)
            context = lax.dot_general(
                cache_w, cache_v[first, :latent, :], NT, preferred_element_type=F32
            )
            for n in range(1, 4):
                part = lax.dot_general(
                    cache_w, cache_v[first + n, :latent, :], NT, preferred_element_type=F32
                )
                context = jnp.where(which == n, part, context)
            context = context + matmul(new_w, nk_s[:, :latent])
            ctx_s[rows, :] = context.astype(BF)

        each(route.first // 16, (route.first + route.count) // 16, block)
        values = matmul(ctx_s[route.rows, :], wv_ref[...]).astype(BF)
        owner = (route.first + lax.broadcasted_iota(jnp.int32, (route.count, 1), 0)) // STEPS

        def project(o, route=route, values=values, owner=owner, i=i):
            offset = offset_of(o)
            j = place.plus(offset)
            part = matmul(values, wo_s[j])
            res = jnp.concatenate([res_s[j]] * (route.count // 16), axis=0)
            send_v[j, route.rows, :] = (part + jnp.where(owner == me, res, 0.0)).astype(BF)
            sums[i].send(offset)

        each(0, peers, project)

    each(1, peers, lambda d: meta_copy(d, lax.rem(me + d, peers)).wait_recv())
    whole = pltpu.make_async_copy(meta_v, meta_ref.at[fs], own_sem.at[0])
    whole.start()

    def group_copy(d, slot, src, dst, sends, recvs):
        return pltpu.make_async_remote_copy(
            src_ref=src,
            dst_ref=dst.at[slot],
            send_sem=sends.at[d],
            recv_sem=recvs.at[slot],
            device_id={"fsdp": lax.rem(fs + d, groups)},
            device_id_type=MESH,
        )

    meta_group = functools.partial(group_copy, src=meta_v, dst=meta_ref, sends=m_send, recvs=m_recv)
    for d in range(1, groups):
        meta_group(d, fs).start()

    for s in sums:
        each(1, s.route.plane, s.relay)
        acc[s.route.rows] = s.combined(0)
    for s in sums:
        each(1, s.route.plane, lambda g, s=s: s.add(g, acc))

    attended = acc[...]
    att_ref[...] = attended
    diagonal = token_r == token_c
    column = jnp.sum(attended * attended, -1, keepdims=True)
    row = jnp.sum(jnp.where(diagonal, column, 0.0), 0, keepdims=True)
    ssq_s[...] = jnp.broadcast_to(row, ssq_s.shape)

    def ssq_copy(d, slot):
        return remote(
            ssq_s, ssq_r.at[slot], ssq_send.at[d], ssq_recv.at[slot], lax.rem(me + d, peers)
        )

    each(1, peers, lambda d: ssq_copy(d, me).start())

    def add_ssq(d, total):
        slot = lax.rem(me + d, peers)
        ssq_copy(d, slot).wait_recv()
        return total + ssq_r[slot]

    total = lax.fori_loop(1, peers, add_ssq, ssq_s[...])[:1, :]
    column = jnp.sum(jnp.where(diagonal, total, 0.0), 1, keepdims=True)
    scale = lax.rsqrt(column / (width * peers) + 1e-06)
    nrm_v[...] = (attended * scale * gain).astype(BF)

    own = pltpu.make_async_copy(nrm_v, xall_ref.at[fs], own_sem.at[1])
    own.start()
    x_group = functools.partial(group_copy, src=nrm_v, dst=xall_ref, sends=f_send, recvs=f_recv)
    for d in range(1, groups):
        x_group(d, fs).start()
    for s in sums:
        s.finish()

    def close(d):
        ssq_copy(d, me).wait_send()
        meta_copy(d, me).wait_send()

    each(1, peers, close)
    for d in range(1, groups):
        meta_group(d, lax.rem(fs + d, groups)).wait_recv()
        x_group(d, lax.rem(fs + d, groups)).wait_recv()
    for d in range(1, groups):
        meta_group(d, fs).wait_send()
        x_group(d, fs).wait_send()
    whole.wait()
    own.wait()


def attend(lens, q, nk, cache, wv, wo, res, gain, ids, gates, peers, groups):
    tokens = q.shape[0] * q.shape[1]
    key = q.shape[2]
    scratch = [
        pltpu.VMEM(cache.shape, BF),
        pltpu.VMEM((peers, wo.shape[0], WIDE), BF),
        pltpu.VMEM((peers, 16, WIDE), F32),
        pltpu.VMEM((tokens, key), BF),
        pltpu.VMEM((tokens, key), BF),
        pltpu.VMEM((tokens, tokens), F32),
        pltpu.VMEM((tokens, wv.shape[0]), BF),
        pltpu.VMEM((peers, tokens, WIDE), BF),
        pltpu.VMEM((tokens, WIDE), F32),
        pltpu.VMEM((8, tokens), F32),
        pltpu.VMEM((peers, 8, tokens), F32),
        pltpu.VMEM((tokens, WIDE), BF),
        pltpu.VMEM((peers, 8, 128), F32),
        pltpu.SemaphoreType.DMA((len(ROUTES),)),
        pltpu.SemaphoreType.DMA((peers,)),
        pltpu.SemaphoreType.DMA((peers,)),
        pltpu.SemaphoreType.DMA((peers,)),
        pltpu.SemaphoreType.DMA((peers,)),
        pltpu.SemaphoreType.DMA((groups,)),
        pltpu.SemaphoreType.DMA((groups,)),
        pltpu.SemaphoreType.DMA((groups,)),
        pltpu.SemaphoreType.DMA((groups,)),
        pltpu.SemaphoreType.DMA((2,)),
    ]
    for route in ROUTES:
        scratch += reduce_scratch(route, WIDE)
    return pl.pallas_call(
        functools.partial(attend_kernel, peers, groups),
        out_shape=(
            jax.ShapeDtypeStruct((groups, tokens, WIDE), BF),
            jax.ShapeDtypeStruct((tokens, WIDE), F32),
            jax.ShapeDtypeStruct((groups, peers, 8, 128), F32),
        ),
        in_specs=[pl.BlockSpec(memory_space=pltpu.SMEM)] + [vmem()] * 2 + [anywhere()] + [vmem()] * 6,
        out_specs=(anywhere(), vmem(), anywhere()),
        scratch_shapes=scratch,
        compiler_params=pltpu.CompilerParams(
            collective_id=0, has_side_effects=True, vmem_limit_bytes=HIGH
        ),
        name="attend",
    )(lens, q, nk, cache, wv, wo, res, gain, ids, gates)


def experts_kernel(peers, groups, *refs):
    (
        x_ref,
        meta_ref,
        att_ref,
        wg_ref,
        wu_ref,
        wd_ref,
        out_ref,
        wg_v,
        wu_v,
        wd_v,
        dense,
        part_v,
        acc,
        hid_v,
        code_s,
        gate_s,
        routed_v,
        routed_r,
        send_v,
        recv_v,
        w_sem,
        f_send,
        f_recv,
        o_send,
        o_recv,
    ) = refs[:25]
    place = Place()
    me = place.me
    fs = lax.axis_index("fsdp")
    experts, depth, half = wg_ref.shape
    tokens = x_ref.shape[0]
    rows = part_v.shape[1]
    block = tokens // peers
    own_rows = send_v.shape[1]
    barrier = pltpu.get_barrier_semaphore()
    greet(barrier, "exp", me, peers)
    greet(barrier, "fsdp", fs, groups)
    rest = refs[25:]
    sums = [Reduce(place, r, part_v, rest[7 * i : 7 * i + 7]) for i, r in enumerate(ROUTES)]
    rest = rest[7 * len(ROUTES) :]
    gathers = [Gather(place, r, hid_v, rest[3 * i : 3 * i + 3]) for i, r in enumerate(ROUTES)]

    def weight_copy(n, e):
        src = (wg_ref, wu_ref, wd_ref)[n]
        dst = (wg_v, wu_v, wd_v)[n]
        return pltpu.make_async_copy(src.at[e], dst.at[e], w_sem.at[n, e])

    def load(e):
        weight_copy(0, e).start()
        weight_copy(1, e).start()

    each(0, experts, load)
    each(0, experts, lambda e: weight_copy(2, e).start())

    lane = lax.broadcasted_iota(jnp.int32, (1, rows), 1)

    def read_meta(j):
        info = meta_ref[4 * j] + meta_ref[4 * j + 1] + meta_ref[4 * j + 2] + meta_ref[4 * j + 3]
        code_s[j] = info[0:1, :].astype(jnp.int32) * block + lane // TOP
        gate_s[j] = info[1:2, :]

    each(0, peers, read_meta)

    def multiply(e):
        weight_copy(0, e).wait()
        weight_copy(1, e).wait()
        x = x_ref[...][:, :depth]
        spot = pl.ds(pl.multiple_of(e * block, block), block)
        gate = matmul(x, wg_v[e]).astype(BF)
        dense[:, spot, :half] = gate.reshape(peers, block, half)
        up = matmul(x, wu_v[e]).astype(BF)
        dense[:, spot, half:] = up.reshape(peers, block, half)

    each(0, experts, multiply)
    pl.semaphore_wait(barrier, peers - 1 + groups - 1)

    diagonal = lax.broadcasted_iota(jnp.int32, (rows, rows), 0) == lax.broadcasted_iota(
        jnp.int32, (rows, rows), 1
    )
    slot_c = lax.broadcasted_iota(jnp.int32, (rows, experts * block), 1)
    slot_r = lax.broadcasted_iota(jnp.int32, (experts * block, rows), 0)

    def pick(o):
        offset = offset_of(o)
        j = place.plus(offset)
        code = jnp.sum(jnp.where(diagonal, code_s[j], 0), 1, keepdims=True)
        chosen = (code == slot_c).astype(F32).astype(BF)
        part_v[j] = matmul(chosen, dense[j]).astype(BF)
        for s in sums:
            s.send(offset)

    each(0, peers, pick)

    for s in sums:
        each(1, s.route.plane, s.relay)
        acc[s.route.rows] = s.combined(0)
    for s in sums:
        each(1, s.route.plane, lambda g, s=s: s.add(g, acc))

    gate = acc[:, :half]
    weight = jnp.sum(jnp.where(diagonal, gate_s[me], 0.0), 1, keepdims=True)
    hid_v[me] = (gate / (1.0 + jnp.exp(-gate)) * acc[:, half:] * weight).astype(BF)

    for g in gathers:
        g.begin()
    for g in gathers:
        each(1, g.route.plane, g.relay)

    def expand(o):
        offset = offset_of(o)
        j = place.minus(offset)
        for g in gathers:
            g.arrive(offset)
        chosen = (code_s[j] == slot_r).astype(F32).astype(BF)
        full = matmul(chosen, hid_v[j]).astype(BF)
        spot = pl.ds(pl.multiple_of(j * block, block), block)
        dense[:, spot, :half] = full.reshape(experts, block, half)

    each(0, peers, expand)
    each(0, experts, lambda e: weight_copy(2, e).wait())

    def group_copy(d, slot):
        peer = lax.rem(fs + d, groups)
        return pltpu.make_async_remote_copy(
            src_ref=routed_v.at[peer],
            dst_ref=routed_r.at[slot],
            send_sem=f_send.at[d],
            recv_sem=f_recv.at[slot],
            device_id={"fsdp": peer},
            device_id_type=MESH,
        )

    def shares(piece):
        spot = pl.ds(pl.multiple_of(piece * (tokens // groups), 128), tokens // groups)

        def one(e, total):
            return total + lax.dot_general(
                dense[e, spot, :half], wd_v[e], NT, preferred_element_type=F32
            )

        return lax.fori_loop(0, experts, one, jnp.zeros((tokens // groups, depth), F32))

    for d in range(1, groups):
        peer = lax.rem(fs + d, groups)
        routed_v[peer, :, :depth] = shares(peer).astype(BF)
        group_copy(d, fs).start()
    mixed = att_ref[:, :depth] + shares(fs)
    for d in range(1, groups):
        slot = lax.rem(fs + d, groups)
        group_copy(d, slot).wait_recv()
        mixed = mixed + routed_r[slot][:, :depth].astype(F32)
    for j in range(peers):
        send_v[j, :, :depth] = mixed[j * own_rows : (j + 1) * own_rows, :]

    def out_copy(d, slot):
        peer = lax.rem(me + d, peers)
        return remote(send_v.at[peer], recv_v.at[slot], o_send.at[d], o_recv.at[slot], peer)

    each(1, peers, lambda d: out_copy(d, me).start())
    recv_v[me] = send_v[me]
    for s in sums:
        s.finish()
    for g in gathers:
        g.finish()
    for d in range(1, groups):
        group_copy(d, fs).wait_send()
    each(1, peers, lambda d: out_copy(d, lax.rem(me + d, peers)).wait_recv())
    for j in range(peers):
        out_ref[0, :, j * depth : (j + 1) * depth] = recv_v[j][:, :depth]
    each(1, peers, lambda d: out_copy(d, me).wait_send())


def expert_layer(x, meta, att, wg, wu, wd, peers, groups):
    tokens = x.shape[0]
    experts, depth, half = wg.shape
    block = tokens // peers
    rows = block * TOP
    own = att.shape[0] // peers
    scratch = [
        pltpu.VMEM(wg.shape, BF),
        pltpu.VMEM(wg.shape, BF),
        pltpu.VMEM(wg.shape, BF),
        pltpu.VMEM((peers, experts * block, 2 * half), BF),
        pltpu.VMEM((peers, rows, 2 * half), BF),
        pltpu.VMEM((rows, 2 * half), F32),
        pltpu.VMEM((peers, rows, half), BF),
        pltpu.VMEM((peers, 1, rows), jnp.int32),
        pltpu.VMEM((peers, 1, rows), F32),
        pltpu.VMEM((groups, tokens // groups, WIDE), BF),
        pltpu.VMEM((groups, tokens // groups, WIDE), BF),
        pltpu.VMEM((peers, own, WIDE), F32),
        pltpu.VMEM((peers, own, WIDE), F32),
        pltpu.SemaphoreType.DMA((3, experts)),
        pltpu.SemaphoreType.DMA((groups,)),
        pltpu.SemaphoreType.DMA((groups,)),
        pltpu.SemaphoreType.DMA((peers,)),
        pltpu.SemaphoreType.DMA((peers,)),
    ]
    for route in ROUTES:
        scratch += reduce_scratch(route, 2 * half)
    for route in ROUTES:
        scratch += gather_scratch(route)
    return pl.pallas_call(
        functools.partial(experts_kernel, peers, groups),
        out_shape=jax.ShapeDtypeStruct((1, own, depth * peers), F32),
        in_specs=[vmem()] * 3 + [anywhere()] * 3,
        out_specs=vmem(),
        scratch_shapes=scratch,
        compiler_params=pltpu.CompilerParams(
            collective_id=1, has_side_effects=True, vmem_limit_bytes=HIGH
        ),
        name="experts",
    )(x, meta, att, wg, wu, wd)


def shards(
    residual,
    gain,
    queries,
    new_keys,
    cache,
    lengths,
    w_value,
    w_out,
    w_gate,
    w_up,
    w_down,
    expert_ids,
    gates,
):
    peers = lax.axis_size("exp")
    groups = lax.axis_size("fsdp")
    xall, att, meta = attend(
        lengths,
        queries[:, :, 0, :],
        new_keys,
        cache,
        w_value[0],
        w_out[0],
        residual,
        gain.reshape(1, -1),
        expert_ids,
        gates,
        peers,
        groups,
    )
    x = xall.reshape(-1, WIDE)
    meta = meta.reshape(groups * peers, 8, 128)
    return expert_layer(x, meta, att, w_gate, w_up, w_down, peers, groups)


def solution(mesh):
    return jax.shard_map(
        shards,
        mesh=mesh,
        in_specs=(
            P(("fsdp", "exp"), None, None),
            P(),
            P("fsdp", None, "exp", None),
            P("fsdp", None, None),
            P("fsdp", None, None),
            P("fsdp"),
            P("exp", None, None),
            P("exp", None, None),
            P(None, "exp", "fsdp"),
            P(None, "exp", "fsdp"),
            P(None, "exp", "fsdp"),
            P(("fsdp", "exp"), None, None),
            P(("fsdp", "exp"), None, None),
        ),
        out_specs=P(("fsdp", "exp"), None, None),
        check_vma=False,
    )
```

```python
import functools

import jax
import jax.numpy as jnp
from jax import lax
from jax.experimental import pallas as pl
from jax.experimental.pallas import tpu as pltpu
from jax.sharding import PartitionSpec as P

TOP = 8
STEPS = 4
score_scale = 0.07216878364870322
MESH = pl.DeviceIdType.MESH
BF = jnp.bfloat16
F32 = jnp.float32
WIDE = 256
HIGH = 58 * 1024 * 1024
NX, NZ, NY = 2, 4, 4
NT = (((1,), (1,)), ((), ()))


def matmul(a, b):
    return jnp.dot(a, b, preferred_element_type=F32)


def vmem():
    return pl.BlockSpec(memory_space=pltpu.VMEM)


def anywhere():
    return pl.BlockSpec(memory_space=pl.ANY)


def greet(barrier, axis, me, size):
    def one(d):
        pl.semaphore_signal(
            barrier, inc=1, device_id={axis: lax.rem(me + d, size)}, device_id_type=MESH
        )

    each(1, size, one)


def each(lower, upper, body):
    def step(i, carry):
        body(i)
        return carry

    lax.fori_loop(lower, upper, step, 0)


class Place:
    def __init__(self):
        self.me = lax.axis_index("exp")
        self.x = self.me // (NZ * NY)
        self.z = lax.rem(self.me // NY, NZ)
        self.y = lax.rem(self.me, NY)

    def index(self, x, z, y):
        return (lax.rem(x, NX) * NZ + lax.rem(z, NZ)) * NY + lax.rem(y, NY)

    def plus(self, offset):
        dx, dz, dy = offset
        return self.index(self.x + dx, self.z + dz, self.y + dy)

    def minus(self, offset):
        dx, dz, dy = offset
        return self.index(self.x + NX - dx, self.z + NZ - dz, self.y + NY - dy)


class Route:
    def __init__(self, kind, first, count):
        self.kind = kind
        self.first, self.count = first, count
        self.rows = pl.ds(first, count)
        self.line = NX if kind == "x" else NZ
        self.plane = NX * NZ * NY // self.line

    def offset(self, d, g):
        if self.kind == "z":
            return (g // NY, d, lax.rem(g, NY))
        if self.kind == "y":
            return (g // NZ, lax.rem(g, NZ), d)
        return (d, g // NY, lax.rem(g, NY))

    def split(self, offset):
        dx, dz, dy = offset
        if self.kind == "z":
            return dz, dx * NY + dy
        if self.kind == "y":
            return dy, dx * NZ + dz
        return dx, dz * NY + dy


ROUTES = (Route("z", 0, 48), Route("y", 48, 48), Route("x", 96, 32))


def remote(src, dst, send, recv, peer):
    return pltpu.make_async_remote_copy(
        src_ref=src,
        dst_ref=dst,
        send_sem=send,
        recv_sem=recv,
        device_id={"exp": peer},
        device_id_type=MESH,
    )


class Reduce:
    def __init__(self, place, route, src, bufs):
        self.place, self.route, self.src = place, route, src
        self.got, self.out, self.fin, self.s1, self.r1, self.s2, self.r2 = bufs

    def first(self, d, g):
        route = self.route
        return remote(
            self.src.at[self.place.plus(route.offset(d, g)), route.rows],
            self.got.at[d - 1, g],
            self.s1.at[d - 1, g],
            self.r1.at[d - 1, g],
            self.place.plus(route.offset(d, 0)),
        )

    def second(self, g):
        return remote(
            self.out.at[g],
            self.fin.at[g],
            self.s2.at[g],
            self.r2.at[g],
            self.place.plus(self.route.offset(0, g)),
        )

    def send(self, offset):
        d, g = self.route.split(offset)

        @pl.when(d > 0)
        def _():
            self.first(d, g).start()

    def combined(self, g):
        route = self.route
        total = self.src[self.place.plus(route.offset(0, g)), route.rows].astype(F32)
        for d in range(1, route.line):
            self.first(d, g).wait_recv()
            total = total + self.got[d - 1, g].astype(F32)
        return total

    def add(self, g, acc_ref):
        self.second(g).wait_recv()
        acc_ref[self.route.rows] += self.fin[g].astype(F32)

    def step(self, g, acc_ref):
        total = self.combined(g)

        @pl.when(g == 0)
        def _():
            acc_ref[self.route.rows] = total

        @pl.when(g != 0)
        def _():
            self.out[g] = total.astype(BF)
            self.second(g).start()

    def finish(self):
        route = self.route

        def one(g):
            for d in range(1, route.line):
                self.first(d, g).wait_send()

        each(0, route.plane, one)
        each(1, route.plane, lambda g: self.second(g).wait_send())


def reduce_scratch(route, cols):
    lines, plane = route.line - 1, route.plane
    return [
        pltpu.VMEM((lines, plane, route.count, cols), BF),
        pltpu.VMEM((plane, route.count, cols), BF),
        pltpu.VMEM((plane, route.count, cols), BF),
        pltpu.SemaphoreType.DMA((lines, plane)),
        pltpu.SemaphoreType.DMA((lines, plane)),
        pltpu.SemaphoreType.DMA((plane,)),
        pltpu.SemaphoreType.DMA((plane,)),
    ]


class Gather:
    def __init__(self, place, route, whole, bufs):
        self.place, self.route, self.whole = place, route, whole
        self.s1, self.s2, self.r = bufs

    def near(self, g, source):
        block = self.whole.at[source, self.route.rows]
        return remote(
            block, block, self.s1.at[g], self.r.at[0, g], self.place.plus(self.route.offset(0, g))
        )

    def far(self, d, g, source):
        block = self.whole.at[source, self.route.rows]
        return remote(
            block,
            block,
            self.s2.at[d - 1, g],
            self.r.at[d, g],
            self.place.plus(self.route.offset(d, 0)),
        )

    def begin(self):
        each(1, self.route.plane, lambda g: self.near(g, self.place.me).start())
        self.forward(0)

    def forward(self, g):
        source = self.place.minus(self.route.offset(0, g))
        for d in range(1, self.route.line):
            self.far(d, g, source).start()

    def relay(self, g):
        self.near(g, self.place.minus(self.route.offset(0, g))).wait_recv()
        self.forward(g)

    def arrive(self, offset):
        d, g = self.route.split(offset)

        @pl.when(d > 0)
        def _():
            self.far(d, g, self.place.minus(offset)).wait_recv()

    def finish(self):
        route = self.route

        def one(g):
            source = self.place.minus(route.offset(0, g))
            for d in range(1, route.line):
                self.far(d, g, source).wait_send()

        each(0, route.plane, one)
        each(1, route.plane, lambda g: self.near(g, self.place.me).wait_send())


def gather_scratch(route):
    lines, plane = route.line - 1, route.plane
    return [
        pltpu.SemaphoreType.DMA((plane,)),
        pltpu.SemaphoreType.DMA((lines, plane)),
        pltpu.SemaphoreType.DMA((route.line, plane)),
    ]


def offset_of(o):
    return (o // (NZ * NY), lax.rem(o // NY, NZ), lax.rem(o, NY))


def spread(block, lanes):
    wide = jnp.concatenate([block] * (lanes // block.shape[1]), axis=1)
    step = lax.rem(lax.broadcasted_iota(jnp.int32, wide.shape, 1) // TOP, STEPS)
    row = lax.broadcasted_iota(jnp.int32, wide.shape, 0)
    return jnp.sum(jnp.where(step == row, wide, 0.0), 0, keepdims=True)


def layer_kernel(peers, groups, *refs):
    (
        len_ref,
        q_ref,
        nk_ref,
        cache_ref,
        wv_ref,
        wo_ref,
        res_ref,
        gain_ref,
        ids_ref,
        gates_ref,
        wg_ref,
        wu_ref,
        wd_ref,
        out_ref,
        dense,
        wo_v,
        wo_s,
        res_s,
        q_s,
        nk_s,
        new_s,
        ctx_s,
        send_v,
        att,
        ssq_s,
        ssq_r,
        sum_v,
        x_v,
        meta_v,
        wg_v,
        wu_v,
        wd_v,
        part_v,
        acc,
        hid_v,
        code_s,
        gate_s,
        routed_v,
        routed_r,
        home_s,
        home_r,
        cache_sem,
        wo_sem,
        w_sem,
        ssq_send,
        ssq_recv,
        meta_send,
        meta_recv,
        g_send,
        g_recv,
        o_send,
        o_recv,
    ) = refs[:52]
    place = Place()
    me = place.me
    fs = lax.axis_index("fsdp")
    tokens = q_s.shape[0]
    latent = wv_ref.shape[0]
    experts, depth, half = wg_ref.shape
    rows = part_v.shape[1]
    block = rows // TOP
    per = peers // groups
    own_rows = home_s.shape[1]
    barrier = pltpu.get_barrier_semaphore()
    rest = refs[52:]
    heads = [Reduce(place, r, send_v, rest[7 * i : 7 * i + 7]) for i, r in enumerate(ROUTES)]
    rest = rest[7 * len(ROUTES) :]
    sums = [Reduce(place, r, part_v, rest[7 * i : 7 * i + 7]) for i, r in enumerate(ROUTES)]
    rest = rest[7 * len(ROUTES) :]
    gathers = [Gather(place, r, hid_v, rest[3 * i : 3 * i + 3]) for i, r in enumerate(ROUTES)]

    def group_copy(n, d, block_ref):
        return pltpu.make_async_remote_copy(
            src_ref=block_ref,
            dst_ref=block_ref,
            send_sem=g_send.at[n, d],
            recv_sem=g_recv.at[n, d],
            device_id={"fsdp": lax.rem(fs + d, groups)},
            device_id_type=MESH,
        )

    def from_group(d):
        return lax.rem(fs + groups - d, groups)

    def cache_copy(i, n):
        span = pl.ds(ROUTES[i].first // STEPS, ROUTES[i].count // STEPS)
        positions = cache_ref.shape[2]
        if n == 0:
            src = cache_ref.at[span, pl.ds(0, latent)]
            dst = dense.at[span, pl.ds(0, latent), pl.ds(0, positions)]
        else:
            left = cache_ref.shape[1] - latent
            src = cache_ref.at[span, pl.ds(latent, left)]
            dst = dense.at[span, pl.ds(0, left), pl.ds(positions, positions)]
        return pltpu.make_async_copy(src, dst, cache_sem.at[i, n])

    def weight_copy(n, e):
        src = (wg_ref, wu_ref, wd_ref)[n]
        dst = (wg_v, wu_v, wd_v)[n]
        return pltpu.make_async_copy(src.at[e], dst.at[e], w_sem.at[n, e])

    out_copy = pltpu.make_async_copy(wo_ref, wo_v, wo_sem)
    for n in range(2):
        cache_copy(0, n).start()
    out_copy.start()
    for i in range(1, len(ROUTES)):
        for n in range(2):
            cache_copy(i, n).start()
    greet(barrier, "exp", me, peers)
    greet(barrier, "fsdp", fs, groups)

    for b in range(tokens // 16):
        span = slice(b * 16, b * 16 + 16)
        q_s[span, :] = jnp.concatenate(
            [q_ref[4 * b + i].astype(F32) for i in range(4)], axis=0
        ).astype(BF)
        nk_s[span, :] = jnp.concatenate(
            [nk_ref[4 * b + i].astype(F32) for i in range(4)], axis=0
        ).astype(BF)

    token_r = lax.broadcasted_iota(jnp.int32, (tokens, tokens), 0)
    token_c = lax.broadcasted_iota(jnp.int32, (tokens, tokens), 1)
    diagonal = token_r == token_c
    same = (token_r // STEPS == token_c // STEPS) & (token_c <= token_r)
    fresh = lax.dot_general(q_s[...], nk_s[...], NT, preferred_element_type=F32)
    new_s[...] = jnp.where(same, fresh * score_scale, -1e30)

    which = lax.broadcasted_iota(jnp.int32, (16, 1), 0) // STEPS
    position = lax.broadcasted_iota(jnp.int32, (16, cache_ref.shape[2]), 1)
    rope = cache_ref.shape[1] - latent

    def attend(b):
        span = pl.ds(pl.multiple_of(b * 16, 16), 16)
        first = b * 4
        q16 = q_s[span, :]

        def score(row):
            return matmul(q16[:, :latent], dense[row, :, : position.shape[1]]) + matmul(
                q16[:, latent:], dense[row, :rope, position.shape[1] :]
            )

        scores = score(first)
        length = jnp.full(position.shape, len_ref[first])
        for n in range(1, 4):
            scores = jnp.where(which == n, score(first + n), scores)
            length = jnp.where(which == n, len_ref[first + n], length)
        scores = jnp.where(position < length, scores * score_scale, -1e30)
        new = new_s[span, :]
        highest = jnp.maximum(jnp.max(scores, -1, keepdims=True), jnp.max(new, -1, keepdims=True))
        cache_exp = jnp.exp(scores - highest)
        new_exp = jnp.exp(new - highest)
        total = jnp.sum(cache_exp, -1, keepdims=True) + jnp.sum(new_exp, -1, keepdims=True)
        cache_w = (cache_exp / total).astype(BF)
        new_w = (new_exp / total).astype(BF)

        def mix(row):
            return lax.dot_general(
                cache_w, dense[row, :, : position.shape[1]], NT, preferred_element_type=F32
            )

        context = mix(first)
        for n in range(1, 4):
            context = jnp.where(which == n, mix(first + n), context)
        context = context + matmul(new_w, nk_s[:, :latent])
        ctx_s[span, :] = context.astype(BF)

    def meta_copy(d, slot):
        tile = meta_v.at[fs, slot]
        return remote(tile, tile, meta_send.at[d], meta_recv.at[slot], lax.rem(me + d, peers))

    for i, route in enumerate(ROUTES):
        for n in range(2):
            cache_copy(i, n).wait()
        each(route.first // 16, (route.first + route.count) // 16, attend)
        if i == 0:
            out_copy.wait()
            gain = jnp.zeros((1, depth), F32)
            pad = jnp.zeros((wo_v.shape[0], WIDE - depth), BF)
            res_pad = jnp.zeros((16, WIDE - depth), F32)
            for j in range(peers):
                part = slice(j * depth, (j + 1) * depth)
                wo_s[j] = jnp.concatenate([wo_v[:, part], pad], axis=1)
                res = jnp.concatenate([res_ref[0, :, part].astype(F32)] * 4, axis=0)
                res_s[j] = jnp.concatenate([res, res_pad], axis=1)
                gain = jnp.where(me == j, gain_ref[:, part], gain)
            gain = jnp.concatenate([gain, jnp.zeros((1, WIDE - depth), F32)], axis=1)
            lane = lax.broadcasted_iota(jnp.int32, (1, rows), 1)
            here = lane // (STEPS * TOP) == lax.rem(me, 4)
            own_ids = jnp.where(here, spread(ids_ref[0].astype(F32), rows), 0.0)
            own_gates = jnp.where(here, spread(gates_ref[0], rows), 0.0)
            meta_v[fs, me] = jnp.concatenate(
                [own_ids, own_gates, jnp.zeros((6, rows), F32)], axis=0
            )
            pl.semaphore_wait(barrier, peers - 1 + groups - 1)
        values = matmul(ctx_s[route.rows, :], wv_ref[...]).astype(BF)
        owner = (route.first + lax.broadcasted_iota(jnp.int32, (route.count, 1), 0)) // STEPS
        own_token = owner == me
        together = 4 // route.line

        def project(n, route=route, values=values, own_token=own_token, head=heads[i]):
            spots = [(d, n * together + k) for k in range(together) for d in range(route.line)]
            for d, g in spots:
                j = place.plus(route.offset(d, g))
                part = matmul(values, wo_s[j])
                res = jnp.concatenate([res_s[j]] * (route.count // 16), axis=0)
                send_v[j, route.rows, :] = (part + jnp.where(own_token, res, 0.0)).astype(BF)
            for d, g in spots:
                if d > 0:
                    head.first(d, g).start()

        each(0, route.plane // together, project)
        if i == 0:
            each(1, peers, lambda d: meta_copy(d, me).start())

            def load(e):
                for n in range(3):
                    weight_copy(n, e).start()

            each(0, experts, load)

    each(1, peers, lambda d: meta_copy(d, lax.rem(me + d, peers)).wait_recv())
    for d in range(1, groups):
        group_copy(0, d, meta_v.at[fs]).start()

    for h in heads:
        each(1, h.route.plane, lambda g, h=h: h.step(g, att))
        h.step(0, att)
    for h in heads:
        each(1, h.route.plane, lambda g, h=h: h.add(g, att))

    attended = att[...]
    x_v[fs] = (attended * gain).astype(BF)
    for d in range(1, groups):
        group_copy(1, d, x_v.at[fs]).start()
    column = jnp.sum(attended * attended, -1, keepdims=True)
    row = jnp.sum(jnp.where(diagonal, column, 0.0), 0, keepdims=True)
    ssq_s[...] = jnp.broadcast_to(row, ssq_s.shape)

    def ssq_copy(d, slot):
        return remote(
            ssq_s, ssq_r.at[slot], ssq_send.at[d], ssq_recv.at[slot], lax.rem(me + d, peers)
        )

    each(1, peers, lambda d: ssq_copy(d, me).start())

    pair_lane = lax.broadcasted_iota(jnp.int32, (1, rows), 1)
    slot_c = lax.broadcasted_iota(jnp.int32, (rows, experts * block), 1)
    slot_r = lax.broadcasted_iota(jnp.int32, (experts * block, rows), 0)

    for q in range(groups):
        piece = lax.rem(fs + groups - q, groups)
        if q > 0:
            group_copy(0, q, meta_v.at[piece]).wait_recv()
            group_copy(1, q, x_v.at[piece]).wait_recv()

        def read_meta(n, piece=piece):
            info = meta_v[piece, 4 * n]
            for i in range(1, 4):
                info = info + meta_v[piece, 4 * n + i]
            j = piece * per + n
            code_s[j] = info[0:1, :].astype(jnp.int32) * block + pair_lane // TOP
            gate_s[j] = info[1:2, :]

        each(0, per, read_meta)
        x = x_v[piece][:, :depth]
        owners = pl.ds(pl.multiple_of(piece * per, per), per)

        def multiply(n, x=x, owners=owners, q=q):
            for e in (2 * n, 2 * n + 1):
                if q == 0:
                    weight_copy(0, e).wait()
                    weight_copy(1, e).wait()
                spot = pl.ds(pl.multiple_of(e * block, block), block)
                gate = matmul(x, wg_v[e]).astype(BF)
                up = matmul(x, wu_v[e]).astype(BF)
                dense[owners, spot, :half] = gate.reshape(per, block, half)
                dense[owners, spot, half:] = up.reshape(per, block, half)

        each(0, experts // 2, multiply)

        def pick(n, piece=piece):
            j = piece * per + lax.rem(n // NY, 2) * NY + lax.rem(place.y + n, NY)
            code = jnp.sum(jnp.where(diagonal, code_s[j], 0), 1, keepdims=True)
            chosen = (code == slot_c).astype(F32).astype(BF)
            part_v[j] = matmul(chosen, dense[j]).astype(BF)
            offset = (
                lax.rem(j // (NZ * NY) + NX - place.x, NX),
                lax.rem(lax.rem(j // NY, NZ) + NZ - place.z, NZ),
                lax.rem(lax.rem(j, NY) + NY - place.y, NY),
            )
            for s in sums:
                s.send(offset)

        each(0, per, pick)
        if q == 0:
            def add_ssq(d, total):
                slot = lax.rem(me + d, peers)
                ssq_copy(d, slot).wait_recv()
                return total + ssq_r[slot]

            sum_v[fs] = lax.fori_loop(1, peers, add_ssq, ssq_s[...])
            for d in range(1, groups):
                group_copy(2, d, sum_v.at[fs]).start()

    def turn(p):
        return lax.rem(fs + groups - p, groups)

    z_half = place.z // 2
    x_first = jnp.where(turn(z_half) < turn(2 + z_half), 0, 1)
    h_first = jnp.where(turn(2 * place.x) < turn(2 * place.x + 1), 0, 1)

    def z_order(i):
        x = lax.rem(x_first + i // NY, NX)
        return lax.rem(x + NX - place.x, NX) * NY + lax.rem(i, NY)

    def y_order(i):
        p = lax.rem(fs + groups - i // 2, groups)
        z = 2 * lax.rem(p, 2) + lax.rem(i, 2)
        return lax.rem(p // 2 + NX - place.x, NX) * NZ + lax.rem(z + NZ - place.z, NZ)

    def x_order(i):
        z = 2 * lax.rem(h_first + i // 8, 2) + lax.rem(i // NY, 2)
        return lax.rem(z + NZ - place.z, NZ) * NY + lax.rem(i, NY)

    def relay(i):
        sums[0].step(z_order(i), acc)
        sums[1].step(y_order(i), acc)
        sums[2].step(x_order(2 * i), acc)
        sums[2].step(x_order(2 * i + 1), acc)

    each(0, ROUTES[0].plane, relay)
    for s in sums:
        each(1, s.route.plane, lambda g, s=s: s.add(g, acc))

    for d in range(1, groups):
        group_copy(2, d, sum_v.at[from_group(d)]).wait_recv()
    token = block * lax.rem(me, per) + token_r // TOP
    squares = jnp.sum(jnp.where(token == token_c, sum_v[me // per][:1, :], 0.0), 1, keepdims=True)
    scale = lax.rsqrt(squares / (depth * peers) + 1e-06)
    weight = jnp.sum(jnp.where(diagonal, gate_s[me], 0.0), 1, keepdims=True)
    gate = acc[:, :half] * scale
    up = acc[:, half:] * scale
    hid_v[me] = (gate / (1.0 + jnp.exp(-gate)) * up * weight).astype(BF)

    for g in gathers:
        g.begin()
    for g in gathers:
        each(1, g.route.plane, g.relay)

    def expand(o):
        offset = offset_of(o)
        j = place.minus(offset)
        for g in gathers:
            g.arrive(offset)
        chosen = (code_s[j] == slot_r).astype(F32).astype(BF)
        full = matmul(chosen, hid_v[j]).astype(BF)
        spot = pl.ds(pl.multiple_of(j * block, block), block)
        dense[:, spot, :half] = full.reshape(experts, block, half)

    each(0, peers, expand)
    each(0, experts, lambda e: weight_copy(2, e).wait())

    def shares(piece):
        spot = pl.ds(pl.multiple_of(piece * tokens, tokens), tokens)

        def some(n, total):
            for k in range(8):
                e = 8 * n + k
                total = total + lax.dot_general(
                    dense[e, spot, :half], wd_v[e], NT, preferred_element_type=F32
                )
            return total

        return lax.fori_loop(0, experts // 8, some, jnp.zeros((tokens, depth), F32))

    def routed_copy(d):
        peer = lax.rem(fs + d, groups)
        return pltpu.make_async_remote_copy(
            src_ref=routed_v.at[peer],
            dst_ref=routed_r.at[d],
            send_sem=g_send.at[3, d],
            recv_sem=g_recv.at[3, d],
            device_id={"fsdp": peer},
            device_id_type=MESH,
        )

    for d in range(1, groups):
        peer = lax.rem(fs + d, groups)
        routed_v[peer, :, :depth] = shares(peer).astype(BF)
        routed_copy(d).start()
    mixed = att[:, :depth] + shares(fs)
    for d in range(1, groups):
        routed_copy(d).wait_recv()
        mixed = mixed + routed_r[d][:, :depth].astype(F32)
    for j in range(peers):
        home_s[j, :, :depth] = mixed[j * own_rows : (j + 1) * own_rows, :]

    def home_copy(d, slot):
        peer = lax.rem(me + d, peers)
        return remote(home_s.at[peer], home_r.at[slot], o_send.at[d], o_recv.at[slot], peer)

    each(1, peers, lambda d: home_copy(d, me).start())
    home_r[me] = home_s[me]
    for s in heads + sums + gathers:
        s.finish()
    for d in range(1, groups):
        routed_copy(d).wait_send()
        group_copy(0, d, meta_v.at[fs]).wait_send()
        group_copy(1, d, x_v.at[fs]).wait_send()
        group_copy(2, d, sum_v.at[fs]).wait_send()

    def close(d):
        ssq_copy(d, me).wait_send()
        meta_copy(d, me).wait_send()

    each(1, peers, close)
    each(1, peers, lambda d: home_copy(d, lax.rem(me + d, peers)).wait_recv())
    for j in range(peers):
        out_ref[0, :, j * depth : (j + 1) * depth] = home_r[j][:, :depth]
    each(1, peers, lambda d: home_copy(d, me).wait_send())


def shards(
    residual,
    gain,
    queries,
    new_keys,
    cache,
    lengths,
    w_value,
    w_out,
    w_gate,
    w_up,
    w_down,
    expert_ids,
    gates,
):
    peers = lax.axis_size("exp")
    groups = lax.axis_size("fsdp")
    group_rows, steps, _, key = queries.shape
    tokens = group_rows * steps
    experts, depth, half = w_gate.shape
    block = tokens * groups // peers
    rows = block * TOP
    smem, dma = pl.BlockSpec(memory_space=pltpu.SMEM), pltpu.SemaphoreType.DMA
    scratch = [
        pltpu.VMEM((peers, experts * block, 2 * half), BF),
        pltpu.VMEM(w_out.shape[1:], BF),
        pltpu.VMEM((peers, w_out.shape[1], WIDE), BF),
        pltpu.VMEM((peers, 16, WIDE), F32),
        pltpu.VMEM((tokens, key), BF),
        pltpu.VMEM((tokens, key), BF),
        pltpu.VMEM((tokens, tokens), F32),
        pltpu.VMEM((tokens, w_value.shape[1]), BF),
        pltpu.VMEM((peers, tokens, WIDE), BF),
        pltpu.VMEM((tokens, WIDE), F32),
        pltpu.VMEM((8, tokens), F32),
        pltpu.VMEM((peers, 8, tokens), F32),
        pltpu.VMEM((groups, 8, tokens), F32),
        pltpu.VMEM((groups, tokens, WIDE), BF),
        pltpu.VMEM((groups, peers, 8, rows), F32),
        pltpu.VMEM(w_gate.shape, BF),
        pltpu.VMEM(w_gate.shape, BF),
        pltpu.VMEM(w_gate.shape, BF),
        pltpu.VMEM((peers, rows, 2 * half), BF),
        pltpu.VMEM((rows, 2 * half), F32),
        pltpu.VMEM((peers, rows, half), BF),
        pltpu.VMEM((peers, 1, rows), jnp.int32),
        pltpu.VMEM((peers, 1, rows), F32),
        pltpu.VMEM((groups, tokens, WIDE), BF),
        pltpu.VMEM((groups, tokens, WIDE), BF),
        pltpu.VMEM((peers, steps, WIDE), F32),
        pltpu.VMEM((peers, steps, WIDE), F32),
        dma((len(ROUTES), 2)),
        dma,
        dma((3, experts)),
        dma((peers,)),
        dma((peers,)),
        dma((peers,)),
        dma((peers,)),
        dma((4, groups)),
        dma((4, groups)),
        dma((peers,)),
        dma((peers,)),
    ]
    for route in ROUTES:
        scratch += reduce_scratch(route, WIDE)
    for route in ROUTES:
        scratch += reduce_scratch(route, 2 * half)
    for route in ROUTES:
        scratch += gather_scratch(route)
    return pl.pallas_call(
        functools.partial(layer_kernel, peers, groups),
        out_shape=jax.ShapeDtypeStruct(residual.shape, F32),
        in_specs=[smem, vmem(), vmem(), anywhere(), vmem(), anywhere()]
        + [vmem()] * 4
        + [anywhere()] * 3,
        out_specs=vmem(),
        scratch_shapes=scratch,
        compiler_params=pltpu.CompilerParams(
            collective_id=0, has_side_effects=True, vmem_limit_bytes=HIGH
        ),
        name="layer",
    )(
        lengths,
        queries[:, :, 0, :],
        new_keys,
        cache,
        w_value[0],
        w_out[0],
        residual,
        gain.reshape(1, -1),
        expert_ids,
        gates,
        w_gate,
        w_up,
        w_down,
    )


def solution(mesh):
    return jax.shard_map(
        shards,
        mesh=mesh,
        in_specs=(
            P(("fsdp", "exp"), None, None),
            P(),
            P("fsdp", None, "exp", None),
            P("fsdp", None, None),
            P("fsdp", None, None),
            P("fsdp"),
            P("exp", None, None),
            P("exp", None, None),
            P(None, "exp", "fsdp"),
            P(None, "exp", "fsdp"),
            P(None, "exp", "fsdp"),
            P(("fsdp", "exp"), None, None),
            P(("fsdp", "exp"), None, None),
        ),
        out_specs=P(("fsdp", "exp"), None, None),
        check_vma=False,
    )
```

```python
import functools

import jax
import jax.numpy as jnp
from jax import lax
from jax.experimental import pallas as pl
from jax.experimental.pallas import tpu as pltpu
from jax.sharding import PartitionSpec as P

TOP = 8
STEPS = 4
score_scale = 0.07216878364870322
MESH = pl.DeviceIdType.MESH
BF = jnp.bfloat16
F32 = jnp.float32
WIDE = 256
HIGH = 58 * 1024 * 1024
NX, NZ, NY = 2, 4, 4
NT = (((1,), (1,)), ((), ()))


def matmul(a, b):
    return jnp.dot(a, b, preferred_element_type=F32)


def vmem():
    return pl.BlockSpec(memory_space=pltpu.VMEM)


def anywhere():
    return pl.BlockSpec(memory_space=pl.ANY)


def each(lower, upper, body):
    def step(i, carry):
        body(i)
        return carry

    lax.fori_loop(lower, upper, step, 0)


class Place:
    def __init__(self):
        self.me = lax.axis_index("exp")
        self.x = self.me // (NZ * NY)
        self.z = lax.rem(self.me // NY, NZ)
        self.y = lax.rem(self.me, NY)

    def index(self, x, z, y):
        return (lax.rem(x, NX) * NZ + lax.rem(z, NZ)) * NY + lax.rem(y, NY)

    def plus(self, offset):
        dx, dz, dy = offset
        return self.index(self.x + dx, self.z + dz, self.y + dy)

    def minus(self, offset):
        dx, dz, dy = offset
        return self.index(self.x + NX - dx, self.z + NZ - dz, self.y + NY - dy)


class Route:
    def __init__(self, kind, first, count):
        self.kind = kind
        self.first, self.count = first, count
        self.rows = pl.ds(first, count)
        self.line = NX if kind == "x" else NZ
        self.plane = NX * NZ * NY // self.line

    def offset(self, d, g):
        if self.kind == "z":
            return (g // NY, d, lax.rem(g, NY))
        if self.kind == "y":
            return (g // NZ, lax.rem(g, NZ), d)
        return (d, g // NY, lax.rem(g, NY))

    def split(self, offset):
        dx, dz, dy = offset
        if self.kind == "z":
            return dz, dx * NY + dy
        if self.kind == "y":
            return dy, dx * NZ + dz
        return dx, dz * NY + dy


ROUTES = (Route("z", 0, 48), Route("y", 48, 48), Route("x", 96, 32))


def remote(src, dst, send, recv, peer):
    return pltpu.make_async_remote_copy(
        src_ref=src,
        dst_ref=dst,
        send_sem=send,
        recv_sem=recv,
        device_id={"exp": peer},
        device_id_type=MESH,
    )


class Reduce:
    def __init__(self, place, route, src, bufs):
        self.place, self.route, self.src = place, route, src
        self.got, self.out, self.fin, self.s1, self.r1, self.s2, self.r2 = bufs

    def first(self, d, g):
        route = self.route
        return remote(
            self.src.at[self.place.plus(route.offset(d, g)), route.rows],
            self.got.at[g, d - 1],
            self.s1,
            self.r1.at[g],
            self.place.plus(route.offset(d, 0)),
        )

    def second(self, g):
        return remote(
            self.out.at[g],
            self.fin.at[g],
            self.s2,
            self.r2,
            self.place.plus(self.route.offset(0, g)),
        )

    def send(self, offset):
        d, g = self.route.split(offset)

        @pl.when(d > 0)
        def _():
            self.first(d, g).start()

    def step(self, g, acc_ref):
        route = self.route
        got = self.got.at[g]
        remote(got, got, self.s1, self.r1.at[g], self.place.me).wait_recv()
        total = self.src[self.place.plus(route.offset(0, g)), route.rows].astype(F32)
        for d in range(1, route.line):
            total = total + self.got[g, d - 1].astype(F32)

        @pl.when(g == 0)
        def _():
            acc_ref[route.rows] = total

        @pl.when(g != 0)
        def _():
            self.out[g] = total.astype(BF)
            self.second(g).start()

    def add(self, acc_ref):
        route = self.route
        rest = self.fin.at[pl.ds(1, route.plane - 1)]
        remote(rest, rest, self.s2, self.r2, self.place.me).wait_recv()
        total = acc_ref[route.rows]
        for g in range(1, route.plane):
            total = total + self.fin[g].astype(F32)
        acc_ref[route.rows] = total

    def finish(self):
        rest = self.out.at[pl.ds(1, self.route.plane - 1)]
        remote(self.got, self.got, self.s1, self.r1.at[0], self.place.me).wait_send()
        remote(rest, rest, self.s2, self.r2, self.place.me).wait_send()


def reduce_scratch(route, cols):
    lines, plane = route.line - 1, route.plane
    dma = pltpu.SemaphoreType.DMA
    return [
        pltpu.VMEM((plane, lines, route.count, cols), BF),
        pltpu.VMEM((plane, route.count, cols), BF),
        pltpu.VMEM((plane, route.count, cols), BF),
        dma,
        dma((plane,)),
        dma,
        dma,
    ]


class Gather:
    def __init__(self, place, route, whole, bufs):
        self.place, self.route, self.whole = place, route, whole
        self.s1, self.s2, self.r = bufs

    def near(self, g, source):
        block = self.whole.at[source, self.route.rows]
        return remote(
            block, block, self.s1, self.r.at[0, g], self.place.plus(self.route.offset(0, g))
        )

    def far(self, d, g, source):
        block = self.whole.at[source, self.route.rows]
        return remote(
            block, block, self.s2, self.r.at[d, g], self.place.plus(self.route.offset(d, 0))
        )

    def begin(self):
        each(1, self.route.plane, lambda g: self.near(g, self.place.me).start())
        self.forward(0)

    def forward(self, g):
        source = self.place.minus(self.route.offset(0, g))
        for d in range(1, self.route.line):
            self.far(d, g, source).start()

    def relay(self, g):
        self.near(g, self.place.minus(self.route.offset(0, g))).wait_recv()
        self.forward(g)

    def arrive(self, offset):
        d, g = self.route.split(offset)

        @pl.when(d > 0)
        def _():
            self.far(d, g, self.place.minus(offset)).wait_recv()

    def finish(self):
        route = self.route
        for sem, count in ((self.s1, route.plane - 1), (self.s2, (route.line - 1) * route.plane)):
            blocks = self.whole.at[pl.ds(0, count), route.rows]
            remote(blocks, blocks, sem, self.r.at[0, 0], self.place.me).wait_send()


def gather_scratch(route):
    dma = pltpu.SemaphoreType.DMA
    return [dma, dma, dma((route.line, route.plane))]


def offset_of(o):
    return (o // (NZ * NY), lax.rem(o // NY, NZ), lax.rem(o, NY))


def spread(block, lanes):
    wide = jnp.concatenate([block] * (lanes // block.shape[1]), axis=1)
    step = lax.rem(lax.broadcasted_iota(jnp.int32, wide.shape, 1) // TOP, STEPS)
    row = lax.broadcasted_iota(jnp.int32, wide.shape, 0)
    return jnp.sum(jnp.where(step == row, wide, 0.0), 0, keepdims=True)


def layer_kernel(peers, groups, *refs):
    (
        len_ref,
        q_ref,
        nk_ref,
        cache_ref,
        wv_ref,
        wo_ref,
        res_ref,
        gain_ref,
        ids_ref,
        gates_ref,
        wg_ref,
        wu_ref,
        wd_ref,
        out_ref,
        dense,
        wo_v,
        wo_s,
        res_s,
        q_s,
        nk_s,
        new_s,
        ctx_s,
        send_v,
        att,
        ssq_s,
        ssq_r,
        sum_v,
        x_v,
        meta_v,
        wg_v,
        wu_v,
        wd_v,
        part_v,
        acc,
        hid_v,
        code_s,
        gate_s,
        routed_v,
        routed_r,
        home_s,
        home_r,
        cache_sem,
        wo_sem,
        w_sem,
        ssq_sem,
        meta_sem,
        home_sem,
        g_send,
        g_recv,
    ) = refs[:49]
    place = Place()
    me = place.me
    fs = lax.axis_index("fsdp")
    tokens = q_s.shape[0]
    latent = wv_ref.shape[0]
    experts, depth, half = wg_ref.shape
    rows = part_v.shape[1]
    block = rows // TOP
    per = peers // groups
    own_rows = home_s.shape[1]
    barrier = pltpu.get_barrier_semaphore()

    def greet(axis, mine, size):
        def one(d):
            pl.semaphore_signal(
                barrier, inc=1, device_id={axis: lax.rem(mine + d, size)}, device_id_type=MESH
            )

        each(1, size, one)

    greet("exp", me, peers)
    greet("fsdp", fs, groups)
    rest = refs[49:]
    heads = [Reduce(place, r, send_v, rest[7 * i : 7 * i + 7]) for i, r in enumerate(ROUTES)]
    rest = rest[7 * len(ROUTES) :]
    sums = [Reduce(place, r, part_v, rest[7 * i : 7 * i + 7]) for i, r in enumerate(ROUTES)]
    rest = rest[7 * len(ROUTES) :]
    gathers = [Gather(place, r, hid_v, rest[3 * i : 3 * i + 3]) for i, r in enumerate(ROUTES)]

    def group_copy(n, d, block_ref):
        return pltpu.make_async_remote_copy(
            src_ref=block_ref,
            dst_ref=block_ref,
            send_sem=g_send.at[n, d],
            recv_sem=g_recv.at[n, d],
            device_id={"fsdp": lax.rem(fs + d, groups)},
            device_id_type=MESH,
        )

    def from_group(d):
        return lax.rem(fs + groups - d, groups)

    def cache_copy(i, n):
        span = pl.ds(ROUTES[i].first // STEPS, ROUTES[i].count // STEPS)
        positions = cache_ref.shape[2]
        if n == 0:
            src = cache_ref.at[span, pl.ds(0, latent)]
            dst = dense.at[span, pl.ds(0, latent), pl.ds(0, positions)]
        else:
            left = cache_ref.shape[1] - latent
            src = cache_ref.at[span, pl.ds(latent, left)]
            dst = dense.at[span, pl.ds(0, left), pl.ds(positions, positions)]
        return pltpu.make_async_copy(src, dst, cache_sem.at[i, n])

    def weight_copy(n):
        src = (wg_ref, wu_ref, wd_ref)[n]
        dst = (wg_v, wu_v, wd_v)[n]
        return pltpu.make_async_copy(src, dst, w_sem.at[n])

    out_copy = pltpu.make_async_copy(wo_ref, wo_v, wo_sem)
    for n in range(2):
        cache_copy(0, n).start()
    out_copy.start()
    for i in range(1, len(ROUTES)):
        for n in range(2):
            cache_copy(i, n).start()

    for b in range(tokens // 16):
        span = slice(b * 16, b * 16 + 16)
        q_s[span, :] = jnp.concatenate(
            [q_ref[4 * b + i].astype(F32) for i in range(4)], axis=0
        ).astype(BF)
        nk_s[span, :] = jnp.concatenate(
            [nk_ref[4 * b + i].astype(F32) for i in range(4)], axis=0
        ).astype(BF)

    token_r = lax.broadcasted_iota(jnp.int32, (tokens, tokens), 0)
    token_c = lax.broadcasted_iota(jnp.int32, (tokens, tokens), 1)
    diagonal = token_r == token_c
    same = (token_r // STEPS == token_c // STEPS) & (token_c <= token_r)
    fresh = lax.dot_general(q_s[...], nk_s[...], NT, preferred_element_type=F32)
    new_s[...] = jnp.where(same, fresh * score_scale, -1e30)

    which = lax.broadcasted_iota(jnp.int32, (16, 1), 0) // STEPS
    position = lax.broadcasted_iota(jnp.int32, (16, cache_ref.shape[2]), 1)
    rope = cache_ref.shape[1] - latent

    def attend(b):
        span = pl.ds(pl.multiple_of(b * 16, 16), 16)
        first = b * 4
        q16 = q_s[span, :]

        def score(row):
            return matmul(q16[:, :latent], dense[row, :, : position.shape[1]]) + matmul(
                q16[:, latent:], dense[row, :rope, position.shape[1] :]
            )

        scores = score(first)
        length = jnp.full(position.shape, len_ref[first])
        for n in range(1, 4):
            scores = jnp.where(which == n, score(first + n), scores)
            length = jnp.where(which == n, len_ref[first + n], length)
        scores = jnp.where(position < length, scores * score_scale, -1e30)
        new = new_s[span, :]
        highest = jnp.maximum(jnp.max(scores, -1, keepdims=True), jnp.max(new, -1, keepdims=True))
        cache_exp = jnp.exp(scores - highest)
        new_exp = jnp.exp(new - highest)
        total = jnp.sum(cache_exp, -1, keepdims=True) + jnp.sum(new_exp, -1, keepdims=True)
        cache_w = (cache_exp / total).astype(BF)
        new_w = (new_exp / total).astype(BF)

        def mix(row):
            return lax.dot_general(
                cache_w, dense[row, :, : position.shape[1]], NT, preferred_element_type=F32
            )

        context = mix(first)
        for n in range(1, 4):
            context = jnp.where(which == n, mix(first + n), context)
        context = context + matmul(new_w, nk_s[:, :latent])
        ctx_s[span, :] = context.astype(BF)

    def meta_copy(d):
        tile = meta_v.at[fs, me]
        return remote(tile, tile, meta_sem.at[0], meta_sem.at[1], lax.rem(me + d, peers))

    def all_copies(buffer, sem):
        tiles = buffer.at[pl.ds(0, peers - 1)]
        return remote(tiles, tiles, sem.at[0], sem.at[1], me)

    for i, route in enumerate(ROUTES):
        for n in range(2):
            cache_copy(i, n).wait()
        each(route.first // 16, (route.first + route.count) // 16, attend)
        if i == 0:
            out_copy.wait()
            gain = jnp.zeros((1, depth), F32)
            pad = jnp.zeros((wo_v.shape[0], WIDE - depth), BF)
            res_pad = jnp.zeros((16, WIDE - depth), F32)
            for j in range(peers):
                part = slice(j * depth, (j + 1) * depth)
                wo_s[j] = jnp.concatenate([wo_v[:, part], pad], axis=1)
                res = jnp.concatenate([res_ref[0, :, part].astype(F32)] * 4, axis=0)
                res_s[j] = jnp.concatenate([res, res_pad], axis=1)
                gain = jnp.where(me == j, gain_ref[:, part], gain)
            gain = jnp.concatenate([gain, jnp.zeros((1, WIDE - depth), F32)], axis=1)
            lane = lax.broadcasted_iota(jnp.int32, (1, rows), 1)
            here = lane // (STEPS * TOP) == lax.rem(me, 4)
            own_ids = jnp.where(here, spread(ids_ref[0].astype(F32), rows), 0.0)
            own_gates = jnp.where(here, spread(gates_ref[0], rows), 0.0)
            meta_v[fs, me] = jnp.concatenate(
                [own_ids, own_gates, jnp.zeros((6, rows), F32)], axis=0
            )
            pl.semaphore_wait(barrier, peers - 1 + groups - 1)
        values = matmul(ctx_s[route.rows, :], wv_ref[...]).astype(BF)
        owner = (route.first + lax.broadcasted_iota(jnp.int32, (route.count, 1), 0)) // STEPS
        own_token = owner == me
        together = 4 // route.line

        def project(n, route=route, values=values, own_token=own_token, head=heads[i]):
            spots = [(d, n * together + k) for k in range(together) for d in range(route.line)]
            for d, g in spots:
                j = place.plus(route.offset(d, g))
                part = matmul(values, wo_s[j])
                res = jnp.concatenate([res_s[j]] * (route.count // 16), axis=0)
                send_v[j, route.rows, :] = (part + jnp.where(own_token, res, 0.0)).astype(BF)
            for d, g in spots:
                if d > 0:
                    head.first(d, g).start()

        each(0, route.plane // together, project)
        if i == 0:
            each(1, peers, lambda d: meta_copy(d).start())
            for n in range(3):
                weight_copy(n).start()

    all_copies(meta_v.at[fs], meta_sem).wait_recv()
    for d in range(1, groups):
        group_copy(0, d, meta_v.at[fs]).start()

    for h in heads:
        each(1, h.route.plane, lambda g, h=h: h.step(g, att))
        h.step(0, att)
    for h in heads:
        h.add(att)

    attended = att[...]
    x_v[fs] = (attended * gain).astype(BF)
    for d in range(1, groups):
        group_copy(1, d, x_v.at[fs]).start()
    column = jnp.sum(attended * attended, -1, keepdims=True)
    row = jnp.sum(jnp.where(diagonal, column, 0.0), 0, keepdims=True)
    ssq_s[...] = jnp.broadcast_to(row, ssq_s.shape)

    def ssq_copy(d):
        return remote(ssq_s, ssq_r.at[d], ssq_sem.at[0], ssq_sem.at[1], lax.rem(me + d, peers))

    ssq_r[0] = ssq_s[...]
    each(1, peers, lambda d: ssq_copy(d).start())

    pair_lane = lax.broadcasted_iota(jnp.int32, (1, rows), 1)
    slot_c = lax.broadcasted_iota(jnp.int32, (rows, experts * block), 1)
    slot_r = lax.broadcasted_iota(jnp.int32, (experts * block, rows), 0)

    def read_meta(q):
        piece = from_group(q)

        def one(n):
            info = meta_v[piece, 4 * n]
            for i in range(1, 4):
                info = info + meta_v[piece, 4 * n + i]
            j = piece * per + n
            code_s[j] = info[0:1, :].astype(jnp.int32) * block + pair_lane // TOP
            gate_s[j] = info[1:2, :]

        each(0, per, one)

    def multiply(first, count, x):
        def some(n):
            for e in (2 * n, 2 * n + 1):
                spot = pl.ds(pl.multiple_of(e * block, block), block)
                gate = matmul(x, wg_v[e]).astype(BF)
                up = matmul(x, wu_v[e]).astype(BF)
                dense[first : first + count, spot, :half] = gate.reshape(count, block, half)
                dense[first : first + count, spot, half:] = up.reshape(count, block, half)

        each(0, experts // 2, some)

    def pick(i):
        q = i // per
        n = lax.rem(i // NY, 2) * NY + lax.rem(place.y + i, NY)
        j = from_group(q) * per + n
        code = jnp.sum(jnp.where(diagonal, code_s[j], 0), 1, keepdims=True)
        chosen = (code == slot_c).astype(F32).astype(BF)
        part_v[j] = matmul(chosen, dense[q * per + n]).astype(BF)
        offset = (
            lax.rem(j // (NZ * NY) + NX - place.x, NX),
            lax.rem(lax.rem(j // NY, NZ) + NZ - place.z, NZ),
            lax.rem(lax.rem(j, NY) + NY - place.y, NY),
        )
        for s in sums:
            s.send(offset)

    def relay(q):
        p = from_group(q)
        x_off = lax.rem(p // 2 + NX - place.x, NX)
        z_low = 2 * lax.rem(p, 2)

        def z_off(i):
            return lax.rem(z_low + i + NZ - place.z, NZ)

        @pl.when(lax.rem(p, 2) == place.z // 2)
        def _():
            each(0, NY, lambda i: sums[0].step(x_off * NY + i, acc))

        each(0, 2, lambda i: sums[1].step(x_off * NZ + z_off(i), acc))

        @pl.when(x_off == 0)
        def _():
            each(0, 2 * NY, lambda i: sums[2].step(z_off(i // NY) * NY + lax.rem(i, NY), acc))

    read_meta(0)
    weight_copy(0).wait()
    weight_copy(1).wait()
    multiply(0, per, x_v[fs][:, :depth])
    each(0, per, pick)

    all_copies(ssq_r.at[pl.ds(1, peers - 1)], ssq_sem).wait_recv()
    sum_v[fs] = jnp.sum(ssq_r[...], axis=0)
    for d in range(1, groups):
        group_copy(2, d, sum_v.at[fs]).start()
    for q in range(1, groups):
        group_copy(0, q, meta_v.at[from_group(q)]).wait_recv()
        group_copy(1, q, x_v.at[from_group(q)]).wait_recv()
        read_meta(q)
    others = [x_v[from_group(q)][:, :depth] for q in range(1, groups)]
    multiply(per, peers - per, jnp.concatenate(others, axis=0))
    each(per, 2 * per, pick)
    relay(0)
    each(2 * per, 3 * per, pick)
    relay(1)
    each(3 * per, peers, pick)
    relay(2)
    relay(3)

    for s in sums:
        s.add(acc)

    for d in range(1, groups):
        group_copy(2, d, sum_v.at[from_group(d)]).wait_recv()
    token = block * lax.rem(me, per) + token_r // TOP
    squares = jnp.sum(jnp.where(token == token_c, sum_v[me // per][:1, :], 0.0), 1, keepdims=True)
    scale = lax.rsqrt(squares / (depth * peers) + 1e-06)
    weight = jnp.sum(jnp.where(diagonal, gate_s[me], 0.0), 1, keepdims=True)
    gate = acc[:, :half] * scale
    up = acc[:, half:] * scale
    hid_v[me] = (gate / (1.0 + jnp.exp(-gate)) * up * weight).astype(BF)

    for g in gathers:
        g.begin()
    for g in gathers:
        each(1, g.route.plane, g.relay)

    def expand(o):
        offset = offset_of(o)
        j = place.minus(offset)
        for g in gathers:
            g.arrive(offset)
        chosen = (code_s[j] == slot_r).astype(F32).astype(BF)
        full = matmul(chosen, hid_v[j]).astype(BF)
        spot = pl.ds(pl.multiple_of(j * block, block), block)
        dense[:, spot, :half] = full.reshape(experts, block, half)

    each(0, peers, expand)
    weight_copy(2).wait()

    def shares(pieces):
        spots = [pl.ds(pl.multiple_of(p * tokens, tokens), tokens) for p in pieces]

        def some(n, total):
            for k in range(4):
                e = 4 * n + k
                both = jnp.concatenate([dense[e, spot, :half] for spot in spots], axis=0)
                total = total + lax.dot_general(both, wd_v[e], NT, preferred_element_type=F32)
            return total

        start = jnp.zeros((len(pieces) * tokens, depth), F32)
        return lax.fori_loop(0, experts // 4, some, start)

    def routed_copy(d):
        peer = lax.rem(fs + d, groups)
        return pltpu.make_async_remote_copy(
            src_ref=routed_v.at[peer],
            dst_ref=routed_r.at[d],
            send_sem=g_send.at[3, d],
            recv_sem=g_recv.at[3, d],
            device_id={"fsdp": peer},
            device_id_type=MESH,
        )

    mixed = att[:, :depth]
    for pair in ((2, 3), (1, 0)):
        both = shares([lax.rem(fs + d, groups) for d in pair])
        for k, d in enumerate(pair):
            share = both[k * tokens : (k + 1) * tokens]
            if d > 0:
                routed_v[lax.rem(fs + d, groups), :, :depth] = share.astype(BF)
                routed_copy(d).start()
            else:
                mixed = mixed + share
    for d in range(1, groups):
        routed_copy(d).wait_recv()
        mixed = mixed + routed_r[d][:, :depth].astype(F32)
    for j in range(peers):
        home_s[j, :, :depth] = mixed[j * own_rows : (j + 1) * own_rows, :]

    def home_copy(d):
        peer = lax.rem(me + d, peers)
        return remote(home_s.at[peer], home_r.at[me], home_sem.at[0], home_sem.at[1], peer)

    each(1, peers, lambda d: home_copy(d).start())
    home_r[me] = home_s[me]
    for s in heads + sums + gathers:
        s.finish()
    for d in range(1, groups):
        routed_copy(d).wait_send()
        group_copy(0, d, meta_v.at[fs]).wait_send()
        group_copy(1, d, x_v.at[fs]).wait_send()
        group_copy(2, d, sum_v.at[fs]).wait_send()

    all_copies(ssq_r, ssq_sem).wait_send()
    all_copies(meta_v.at[fs], meta_sem).wait_send()
    all_copies(home_s, home_sem).wait_recv()
    for j in range(peers):
        out_ref[0, :, j * depth : (j + 1) * depth] = home_r[j][:, :depth]
    all_copies(home_s, home_sem).wait_send()


def shards(
    residual,
    gain,
    queries,
    new_keys,
    cache,
    lengths,
    w_value,
    w_out,
    w_gate,
    w_up,
    w_down,
    expert_ids,
    gates,
):
    peers = lax.axis_size("exp")
    groups = lax.axis_size("fsdp")
    group_rows, steps, _, key = queries.shape
    tokens = group_rows * steps
    experts, depth, half = w_gate.shape
    block = tokens * groups // peers
    rows = block * TOP
    smem, dma = pl.BlockSpec(memory_space=pltpu.SMEM), pltpu.SemaphoreType.DMA
    scratch = [
        pltpu.VMEM((peers, experts * block, 2 * half), BF),
        pltpu.VMEM(w_out.shape[1:], BF),
        pltpu.VMEM((peers, w_out.shape[1], WIDE), BF),
        pltpu.VMEM((peers, 16, WIDE), F32),
        pltpu.VMEM((tokens, key), BF),
        pltpu.VMEM((tokens, key), BF),
        pltpu.VMEM((tokens, tokens), F32),
        pltpu.VMEM((tokens, w_value.shape[1]), BF),
        pltpu.VMEM((peers, tokens, WIDE), BF),
        pltpu.VMEM((tokens, WIDE), F32),
        pltpu.VMEM((8, tokens), F32),
        pltpu.VMEM((peers, 8, tokens), F32),
        pltpu.VMEM((groups, 8, tokens), F32),
        pltpu.VMEM((groups, tokens, WIDE), BF),
        pltpu.VMEM((groups, peers, 8, rows), F32),
        pltpu.VMEM(w_gate.shape, BF),
        pltpu.VMEM(w_gate.shape, BF),
        pltpu.VMEM(w_gate.shape, BF),
        pltpu.VMEM((peers, rows, 2 * half), BF),
        pltpu.VMEM((rows, 2 * half), F32),
        pltpu.VMEM((peers, rows, half), BF),
        pltpu.VMEM((peers, 1, rows), jnp.int32),
        pltpu.VMEM((peers, 1, rows), F32),
        pltpu.VMEM((groups, tokens, WIDE), BF),
        pltpu.VMEM((groups, tokens, WIDE), BF),
        pltpu.VMEM((peers, steps, WIDE), F32),
        pltpu.VMEM((peers, steps, WIDE), F32),
        dma((len(ROUTES), 2)),
        dma,
        dma((3,)),
        dma((2,)),
        dma((2,)),
        dma((2,)),
        dma((4, groups)),
        dma((4, groups)),
    ]
    for route in ROUTES:
        scratch += reduce_scratch(route, WIDE)
    for route in ROUTES:
        scratch += reduce_scratch(route, 2 * half)
    for route in ROUTES:
        scratch += gather_scratch(route)
    return pl.pallas_call(
        functools.partial(layer_kernel, peers, groups),
        out_shape=jax.ShapeDtypeStruct(residual.shape, F32),
        in_specs=[smem, vmem(), vmem(), anywhere(), vmem(), anywhere()]
        + [vmem()] * 4
        + [anywhere()] * 3,
        out_specs=vmem(),
        scratch_shapes=scratch,
        compiler_params=pltpu.CompilerParams(
            collective_id=0, has_side_effects=True, vmem_limit_bytes=HIGH
        ),
        name="layer",
    )(
        lengths,
        queries[:, :, 0, :],
        new_keys,
        cache,
        w_value[0],
        w_out[0],
        residual,
        gain.reshape(1, -1),
        expert_ids,
        gates,
        w_gate,
        w_up,
        w_down,
    )


def solution(mesh):
    return jax.shard_map(
        shards,
        mesh=mesh,
        in_specs=(
            P(("fsdp", "exp"), None, None),
            P(),
            P("fsdp", None, "exp", None),
            P("fsdp", None, None),
            P("fsdp", None, None),
            P("fsdp"),
            P("exp", None, None),
            P("exp", None, None),
            P(None, "exp", "fsdp"),
            P(None, "exp", "fsdp"),
            P(None, "exp", "fsdp"),
            P(("fsdp", "exp"), None, None),
            P(("fsdp", "exp"), None, None),
        ),
        out_specs=P(("fsdp", "exp"), None, None),
        check_vma=False,
    )
```

```python
import functools

import jax
import jax.numpy as jnp
from jax import lax
from jax.experimental import pallas as pl
from jax.experimental.pallas import tpu as pltpu
from jax.sharding import PartitionSpec as P

TOP = 8
STEPS = 4
score_scale = 0.07216878364870322
MESH = pl.DeviceIdType.MESH
BF = jnp.bfloat16
F32 = jnp.float32
WIDE = 256
HIGH = 60 * 1024 * 1024
NX, NZ, NY = 2, 4, 4
NT = (((1,), (1,)), ((), ()))


def matmul(a, b):
    return jnp.dot(a, b, preferred_element_type=F32)


def vmem():
    return pl.BlockSpec(memory_space=pltpu.VMEM)


def anywhere():
    return pl.BlockSpec(memory_space=pl.ANY)


def each(lower, upper, body):
    def step(i, carry):
        body(i)
        return carry

    lax.fori_loop(lower, upper, step, 0)


class Place:
    def __init__(self):
        self.me = lax.axis_index("exp")
        self.x = self.me // (NZ * NY)
        self.z = lax.rem(self.me // NY, NZ)
        self.y = lax.rem(self.me, NY)

    def index(self, x, z, y):
        return (lax.rem(x, NX) * NZ + lax.rem(z, NZ)) * NY + lax.rem(y, NY)

    def plus(self, offset):
        dx, dz, dy = offset
        return self.index(self.x + dx, self.z + dz, self.y + dy)

    def minus(self, offset):
        dx, dz, dy = offset
        return self.index(self.x + NX - dx, self.z + NZ - dz, self.y + NY - dy)


class Route:
    def __init__(self, kind, first, count):
        self.kind = kind
        self.first, self.count = first, count
        self.rows = pl.ds(first, count)
        self.line = NX if kind == "x" else NZ
        self.plane = NX * NZ * NY // self.line

    def offset(self, d, g):
        if self.kind == "z":
            return (g // NY, d, lax.rem(g, NY))
        if self.kind == "y":
            return (g // NZ, lax.rem(g, NZ), d)
        return (d, g // NY, lax.rem(g, NY))

    def split(self, offset):
        dx, dz, dy = offset
        if self.kind == "z":
            return dz, dx * NY + dy
        if self.kind == "y":
            return dy, dx * NZ + dz
        return dx, dz * NY + dy


ROUTES = (Route("z", 0, 48), Route("y", 48, 48), Route("x", 96, 32))


def remote(src, dst, send, recv, peer):
    return pltpu.make_async_remote_copy(
        src_ref=src,
        dst_ref=dst,
        send_sem=send,
        recv_sem=recv,
        device_id={"exp": peer},
        device_id_type=MESH,
    )


class Reduce:
    def __init__(self, place, route, src, bufs):
        self.place, self.route, self.src = place, route, src
        self.got, self.out, self.fin, self.s1, self.r1, self.s2, self.r2 = bufs

    def first(self, d, g):
        route = self.route
        return remote(
            self.src.at[self.place.plus(route.offset(d, g)), route.rows],
            self.got.at[g, d - 1],
            self.s1,
            self.r1.at[g],
            self.place.plus(route.offset(d, 0)),
        )

    def second(self, g):
        return remote(
            self.out.at[g],
            self.fin.at[g],
            self.s2,
            self.r2,
            self.place.plus(self.route.offset(0, g)),
        )

    def send(self, offset):
        d, g = self.route.split(offset)

        @pl.when(d > 0)
        def _():
            self.first(d, g).start()

    def step(self, g, acc_ref):
        route = self.route
        got = self.got.at[g]
        remote(got, got, self.s1, self.r1.at[g], self.place.me).wait_recv()
        total = self.src[self.place.plus(route.offset(0, g)), route.rows].astype(F32)
        for d in range(1, route.line):
            total = total + self.got[g, d - 1].astype(F32)

        @pl.when(g == 0)
        def _():
            acc_ref[route.rows] = total

        @pl.when(g != 0)
        def _():
            self.out[g] = total.astype(BF)
            self.second(g).start()

    def add(self, acc_ref):
        route = self.route
        rest = self.fin.at[pl.ds(1, route.plane - 1)]
        remote(rest, rest, self.s2, self.r2, self.place.me).wait_recv()
        total = acc_ref[route.rows]
        for g in range(1, route.plane):
            total = total + self.fin[g].astype(F32)
        acc_ref[route.rows] = total

    def finish(self):
        rest = self.out.at[pl.ds(1, self.route.plane - 1)]
        remote(self.got, self.got, self.s1, self.r1.at[0], self.place.me).wait_send()
        remote(rest, rest, self.s2, self.r2, self.place.me).wait_send()


def reduce_scratch(route, cols):
    lines, plane = route.line - 1, route.plane
    dma = pltpu.SemaphoreType.DMA
    return [
        pltpu.VMEM((plane, lines, route.count, cols), BF),
        pltpu.VMEM((plane, route.count, cols), BF),
        pltpu.VMEM((plane, route.count, cols), BF),
        dma,
        dma((plane,)),
        dma,
        dma,
    ]


class Gather:
    def __init__(self, place, route, whole, bufs):
        self.place, self.route, self.whole = place, route, whole
        self.s1, self.s2, self.r = bufs

    def near(self, g, source):
        block = self.whole.at[source, self.route.rows]
        return remote(
            block, block, self.s1, self.r.at[0, g], self.place.plus(self.route.offset(0, g))
        )

    def far(self, d, g, source):
        block = self.whole.at[source, self.route.rows]
        return remote(
            block, block, self.s2, self.r.at[d, g], self.place.plus(self.route.offset(d, 0))
        )

    def begin(self):
        each(1, self.route.plane, lambda g: self.near(g, self.place.me).start())
        self.forward(0)

    def forward(self, g):
        source = self.place.minus(self.route.offset(0, g))
        for d in range(1, self.route.line):
            self.far(d, g, source).start()

    def relay(self, g):
        self.near(g, self.place.minus(self.route.offset(0, g))).wait_recv()
        self.forward(g)

    def arrive(self, offset):
        d, g = self.route.split(offset)

        @pl.when(d > 0)
        def _():
            self.far(d, g, self.place.minus(offset)).wait_recv()

    def finish(self):
        route = self.route
        for sem, count in ((self.s1, route.plane - 1), (self.s2, (route.line - 1) * route.plane)):
            blocks = self.whole.at[pl.ds(0, count), route.rows]
            remote(blocks, blocks, sem, self.r.at[0, 0], self.place.me).wait_send()


def gather_scratch(route):
    dma = pltpu.SemaphoreType.DMA
    return [dma, dma, dma((route.line, route.plane))]


def offset_of(o):
    return (o // (NZ * NY), lax.rem(o // NY, NZ), lax.rem(o, NY))


def spread(block, lanes):
    wide = jnp.concatenate([block] * (lanes // block.shape[1]), axis=1)
    step = lax.rem(lax.broadcasted_iota(jnp.int32, wide.shape, 1) // TOP, STEPS)
    row = lax.broadcasted_iota(jnp.int32, wide.shape, 0)
    return jnp.sum(jnp.where(step == row, wide, 0.0), 0, keepdims=True)


def layer_kernel(peers, groups, *refs):
    (
        len_ref,
        q_ref,
        nk_ref,
        cache_ref,
        wv_ref,
        wo_ref,
        res_ref,
        gain_ref,
        ids_ref,
        gates_ref,
        wg_ref,
        wu_ref,
        wd_ref,
        out_ref,
        dense,
        wo_v,
        wo_s,
        res_s,
        q_s,
        nk_s,
        new_s,
        ctx_s,
        send_v,
        att,
        ssq_s,
        ssq_r,
        sum_v,
        x_v,
        meta_v,
        wg_v,
        wu_v,
        wd_v,
        part_v,
        acc,
        hid_v,
        spread_s,
        gate_s,
        routed_v,
        routed_r,
        home_s,
        home_r,
        cache_sem,
        wo_sem,
        w_sem,
        ssq_sem,
        meta_sem,
        home_sem,
        g_send,
        g_recv,
    ) = refs[:49]
    place = Place()
    me = place.me
    fs = lax.axis_index("fsdp")
    tokens = q_s.shape[0]
    latent = wv_ref.shape[0]
    experts, depth, half = wg_ref.shape
    rows = part_v.shape[1]
    block = rows // TOP
    per = peers // groups
    own_rows = home_s.shape[1]
    barrier = pltpu.get_barrier_semaphore()

    def greet(axis, mine, size):
        def one(d):
            pl.semaphore_signal(
                barrier, inc=1, device_id={axis: lax.rem(mine + d, size)}, device_id_type=MESH
            )

        each(1, size, one)

    greet("exp", me, peers)
    greet("fsdp", fs, groups)
    rest = refs[49:]
    heads = [Reduce(place, r, send_v, rest[7 * i : 7 * i + 7]) for i, r in enumerate(ROUTES)]
    rest = rest[7 * len(ROUTES) :]
    sums = [Reduce(place, r, part_v, rest[7 * i : 7 * i + 7]) for i, r in enumerate(ROUTES)]
    rest = rest[7 * len(ROUTES) :]
    gathers = [Gather(place, r, hid_v, rest[3 * i : 3 * i + 3]) for i, r in enumerate(ROUTES)]

    def group_copy(n, d, block_ref):
        return pltpu.make_async_remote_copy(
            src_ref=block_ref,
            dst_ref=block_ref,
            send_sem=g_send.at[n, d],
            recv_sem=g_recv.at[n, d],
            device_id={"fsdp": lax.rem(fs + d, groups)},
            device_id_type=MESH,
        )

    def from_group(d):
        return lax.rem(fs + groups - d, groups)

    def cache_copy(i, n):
        span = pl.ds(ROUTES[i].first // STEPS, ROUTES[i].count // STEPS)
        positions = cache_ref.shape[2]
        if n == 0:
            src = cache_ref.at[span, pl.ds(0, latent)]
            dst = dense.at[span, pl.ds(0, latent), pl.ds(0, positions)]
        else:
            left = cache_ref.shape[1] - latent
            src = cache_ref.at[span, pl.ds(latent, left)]
            dst = dense.at[span, pl.ds(0, left), pl.ds(positions, positions)]
        return pltpu.make_async_copy(src, dst, cache_sem.at[i, n])

    def weight_copy(n):
        src = (wg_ref, wu_ref, wd_ref)[n]
        dst = (wg_v, wu_v, wd_v)[n]
        return pltpu.make_async_copy(src, dst, w_sem.at[n])

    out_copy = pltpu.make_async_copy(wo_ref, wo_v, wo_sem)
    for n in range(2):
        cache_copy(0, n).start()
    out_copy.start()
    for i in range(1, len(ROUTES)):
        for n in range(2):
            cache_copy(i, n).start()

    for b in range(tokens // 16):
        span = slice(b * 16, b * 16 + 16)
        q_s[span, :] = jnp.concatenate(
            [q_ref[4 * b + i].astype(F32) for i in range(4)], axis=0
        ).astype(BF)
        nk_s[span, :] = jnp.concatenate(
            [nk_ref[4 * b + i].astype(F32) for i in range(4)], axis=0
        ).astype(BF)

    token_r = lax.broadcasted_iota(jnp.int32, (tokens, tokens), 0)
    token_c = lax.broadcasted_iota(jnp.int32, (tokens, tokens), 1)
    diagonal = token_r == token_c
    same = (token_r // STEPS == token_c // STEPS) & (token_c <= token_r)
    fresh = lax.dot_general(q_s[...], nk_s[...], NT, preferred_element_type=F32)
    new_s[...] = jnp.where(same, fresh * score_scale, -1e30)

    which = lax.broadcasted_iota(jnp.int32, (16, 1), 0) // STEPS
    position = lax.broadcasted_iota(jnp.int32, (16, cache_ref.shape[2]), 1)
    rope = cache_ref.shape[1] - latent

    def attend(b):
        span = pl.ds(pl.multiple_of(b * 16, 16), 16)
        first = b * 4
        q16 = q_s[span, :]

        def score(row):
            return matmul(q16[:, :latent], dense[row, :, : position.shape[1]]) + matmul(
                q16[:, latent:], dense[row, :rope, position.shape[1] :]
            )

        scores = score(first)
        length = jnp.full(position.shape, len_ref[first])
        for n in range(1, 4):
            scores = jnp.where(which == n, score(first + n), scores)
            length = jnp.where(which == n, len_ref[first + n], length)
        scores = jnp.where(position < length, scores * score_scale, -1e30)
        new = new_s[span, :]
        highest = jnp.maximum(jnp.max(scores, -1, keepdims=True), jnp.max(new, -1, keepdims=True))
        cache_exp = jnp.exp(scores - highest)
        new_exp = jnp.exp(new - highest)
        total = jnp.sum(cache_exp, -1, keepdims=True) + jnp.sum(new_exp, -1, keepdims=True)
        cache_w = (cache_exp / total).astype(BF)
        new_w = (new_exp / total).astype(BF)

        def mix(row):
            return lax.dot_general(
                cache_w, dense[row, :, : position.shape[1]], NT, preferred_element_type=F32
            )

        context = mix(first)
        for n in range(1, 4):
            context = jnp.where(which == n, mix(first + n), context)
        context = context + matmul(new_w, nk_s[:, :latent])
        ctx_s[span, :] = context.astype(BF)

    def meta_copy(d):
        tile = meta_v.at[fs, me]
        return remote(tile, tile, meta_sem.at[0], meta_sem.at[1], lax.rem(me + d, peers))

    def all_copies(buffer, sem):
        tiles = buffer.at[pl.ds(0, peers - 1)]
        return remote(tiles, tiles, sem.at[0], sem.at[1], me)

    for i, route in enumerate(ROUTES):
        for n in range(2):
            cache_copy(i, n).wait()
        each(route.first // 16, (route.first + route.count) // 16, attend)
    for n in range(3):
        weight_copy(n).start()

    for i, route in enumerate(ROUTES):
        if i == 0:
            out_copy.wait()
            gain = jnp.zeros((1, depth), F32)
            pad = jnp.zeros((wo_v.shape[0], WIDE - depth), BF)
            res_pad = jnp.zeros((16, WIDE - depth), F32)
            for j in range(peers):
                part = slice(j * depth, (j + 1) * depth)
                wo_s[j] = jnp.concatenate([wo_v[:, part], pad], axis=1)
                res = jnp.concatenate([res_ref[0, :, part].astype(F32)] * 4, axis=0)
                res_s[j] = jnp.concatenate([res, res_pad], axis=1)
                gain = jnp.where(me == j, gain_ref[:, part], gain)
            gain = jnp.concatenate([gain, jnp.zeros((1, WIDE - depth), F32)], axis=1)
            lane = lax.broadcasted_iota(jnp.int32, (1, rows), 1)
            here = lane // (STEPS * TOP) == lax.rem(me, 4)
            own_ids = jnp.where(here, spread(ids_ref[0].astype(F32), rows), 0.0)
            own_gates = jnp.where(here, spread(gates_ref[0], rows), 0.0)
            meta_v[fs, me] = jnp.concatenate(
                [own_ids, own_gates, jnp.zeros((6, rows), F32)], axis=0
            )
            pl.semaphore_wait(barrier, peers - 1 + groups - 1)
        values = matmul(ctx_s[route.rows, :], wv_ref[...]).astype(BF)
        owner = (route.first + lax.broadcasted_iota(jnp.int32, (route.count, 1), 0)) // STEPS
        own_token = owner == me
        together = 4 // route.line

        def project(n, route=route, values=values, own_token=own_token, head=heads[i]):
            spots = [(d, n * together + k) for k in range(together) for d in range(route.line)]
            for d, g in spots:
                j = place.plus(route.offset(d, g))
                part = matmul(values, wo_s[j])
                res = jnp.concatenate([res_s[j]] * (route.count // 16), axis=0)
                send_v[j, route.rows, :] = (part + jnp.where(own_token, res, 0.0)).astype(BF)
            for d, g in spots:
                if d > 0:
                    head.first(d, g).start()

        each(0, route.plane // together, project)
        if i == 0:
            each(1, peers, lambda d: meta_copy(d).start())

    all_copies(meta_v.at[fs], meta_sem).wait_recv()
    for d in range(1, groups):
        group_copy(0, d, meta_v.at[fs]).start()

    for h in heads:
        each(1, h.route.plane, lambda g, h=h: h.step(g, att))
        h.step(0, att)
    pair_lane = lax.broadcasted_iota(jnp.int32, (1, rows), 1)
    slot_c = lax.broadcasted_iota(jnp.int32, (rows, experts * block), 1)
    slot_r = lax.broadcasted_iota(jnp.int32, (experts * block, rows), 0)

    def read_meta(q):
        piece = from_group(q)

        def one(n):
            info = meta_v[piece, 4 * n]
            for i in range(1, 4):
                info = info + meta_v[piece, 4 * n + i]
            j = piece * per + n
            code = info[0:1, :].astype(jnp.int32) * block + pair_lane // TOP
            spread_s[j] = (code == slot_r).astype(F32).astype(BF)
            code = jnp.sum(jnp.where(diagonal, code, 0), 1, keepdims=True)
            part_v[j] = (code == slot_c).astype(F32).astype(BF)
            gate_s[j] = info[1:2, :]

        each(0, per, one)

    read_meta(0)
    for q in range(1, groups):
        group_copy(0, q, meta_v.at[from_group(q)]).wait_recv()
        read_meta(q)
    for h in heads:
        h.add(att)

    attended = att[...]
    x_v[fs] = (attended * gain).astype(BF)
    for d in range(1, groups):
        group_copy(1, d, x_v.at[fs]).start()
    column = jnp.sum(attended * attended, -1, keepdims=True)
    row = jnp.sum(jnp.where(diagonal, column, 0.0), 0, keepdims=True)
    ssq_s[...] = jnp.broadcast_to(row, ssq_s.shape)

    def ssq_copy(d):
        return remote(ssq_s, ssq_r.at[d], ssq_sem.at[0], ssq_sem.at[1], lax.rem(me + d, peers))

    ssq_r[0] = ssq_s[...]
    each(1, peers, lambda d: ssq_copy(d).start())

    def multiply(first, count, x):
        def some(n):
            for e in [4 * n + k for k in range(4)]:
                spot = pl.ds(pl.multiple_of(e * block, block), block)
                gate = matmul(x, wg_v[e]).astype(BF)
                up = matmul(x, wu_v[e]).astype(BF)
                dense[first : first + count, spot, :half] = gate.reshape(count, block, half)
                dense[first : first + count, spot, half:] = up.reshape(count, block, half)

        each(0, experts // 4, some)

    def pick(i):
        found = []
        for k in range(2):
            q = (2 * i + k) // per
            n = lax.rem((2 * i + k) // NY, 2) * NY + lax.rem(place.y + 2 * i + k, NY)
            j = from_group(q) * per + n
            found.append((j, matmul(part_v[j], dense[q * per + n]).astype(BF)))
        for j, part in found:
            part_v[j] = part
        for j, _ in found:
            offset = (
                lax.rem(j // (NZ * NY) + NX - place.x, NX),
                lax.rem(lax.rem(j // NY, NZ) + NZ - place.z, NZ),
                lax.rem(lax.rem(j, NY) + NY - place.y, NY),
            )
            for s in sums:
                s.send(offset)

    def pick_group(q):
        each(q * per // 2, (q + 1) * per // 2, pick)

    def relay(q):
        p = from_group(q)
        x_off = lax.rem(p // 2 + NX - place.x, NX)
        z_low = 2 * lax.rem(p, 2)

        def z_off(i):
            return lax.rem(z_low + i + NZ - place.z, NZ)

        @pl.when(lax.rem(p, 2) == place.z // 2)
        def _():
            each(0, NY, lambda i: sums[0].step(x_off * NY + i, acc))

        each(0, 2, lambda i: sums[1].step(x_off * NZ + z_off(i), acc))

        @pl.when(x_off == 0)
        def _():
            each(0, 2 * NY, lambda i: sums[2].step(z_off(i // NY) * NY + lax.rem(i, NY), acc))

    weight_copy(0).wait()
    weight_copy(1).wait()
    multiply(0, per, x_v[fs][:, :depth])
    pick_group(0)

    all_copies(ssq_r.at[pl.ds(1, peers - 1)], ssq_sem).wait_recv()
    sum_v[fs] = jnp.sum(ssq_r[...], axis=0)
    for d in range(1, groups):
        group_copy(2, d, sum_v.at[fs]).start()
    for q in range(1, groups):
        group_copy(1, q, x_v.at[from_group(q)]).wait_recv()
    others = [x_v[from_group(q)][:, :depth] for q in range(1, groups)]
    multiply(per, peers - per, jnp.concatenate(others, axis=0))
    pick_group(1)
    relay(0)
    pick_group(2)
    relay(1)
    pick_group(3)
    relay(2)
    relay(3)

    for s in sums:
        s.add(acc)

    for d in range(1, groups):
        group_copy(2, d, sum_v.at[from_group(d)]).wait_recv()
    token = block * lax.rem(me, per) + token_r // TOP
    squares = jnp.sum(jnp.where(token == token_c, sum_v[me // per][:1, :], 0.0), 1, keepdims=True)
    scale = lax.rsqrt(squares / (depth * peers) + 1e-06)
    weight = jnp.sum(jnp.where(diagonal, gate_s[me], 0.0), 1, keepdims=True)
    gate = acc[:, :half] * scale
    up = acc[:, half:] * scale
    hid_v[me] = (gate / (1.0 + jnp.exp(-gate)) * up * weight).astype(BF)

    for g in gathers:
        g.begin()
    for g in gathers:
        each(1, g.route.plane, g.relay)

    def expand(n):
        offsets = [offset_of(2 * n), offset_of(2 * n + 1)]
        for offset in offsets:
            for g in gathers:
                g.arrive(offset)
        blocks = [place.minus(offset) for offset in offsets]
        full = [matmul(spread_s[j], hid_v[j]).astype(BF) for j in blocks]
        for j, rows_of in zip(blocks, full):
            spot = pl.ds(pl.multiple_of(j * block, block), block)
            dense[:, spot, :half] = rows_of.reshape(experts, block, half)

    each(0, peers // 2, expand)
    weight_copy(2).wait()

    def shares(pieces):
        spots = [pl.ds(pl.multiple_of(p * tokens, tokens), tokens) for p in pieces]

        def some(n, total):
            for k in range(4):
                e = 4 * n + k
                both = jnp.concatenate([dense[e, spot, :half] for spot in spots], axis=0)
                total = total + lax.dot_general(both, wd_v[e], NT, preferred_element_type=F32)
            return total

        start = jnp.zeros((len(pieces) * tokens, depth), F32)
        return lax.fori_loop(0, experts // 4, some, start)

    def routed_copy(d):
        peer = lax.rem(fs + d, groups)
        return pltpu.make_async_remote_copy(
            src_ref=routed_v.at[peer],
            dst_ref=routed_r.at[d],
            send_sem=g_send.at[3, d],
            recv_sem=g_recv.at[3, d],
            device_id={"fsdp": peer},
            device_id_type=MESH,
        )

    mixed = att[:, :depth]
    for pair in ((2, 3), (1, 0)):
        both = shares([lax.rem(fs + d, groups) for d in pair])
        for k, d in enumerate(pair):
            share = both[k * tokens : (k + 1) * tokens]
            if d > 0:
                routed_v[lax.rem(fs + d, groups), :, :depth] = share.astype(BF)
                routed_copy(d).start()
            else:
                mixed = mixed + share
    for d in range(1, groups):
        routed_copy(d).wait_recv()
        mixed = mixed + routed_r[d][:, :depth].astype(F32)
    for j in range(peers):
        home_s[j, :, :depth] = mixed[j * own_rows : (j + 1) * own_rows, :]

    def home_copy(d):
        peer = lax.rem(me + d, peers)
        return remote(home_s.at[peer], home_r.at[me], home_sem.at[0], home_sem.at[1], peer)

    each(1, peers, lambda d: home_copy(d).start())
    home_r[me] = home_s[me]
    for s in heads + sums + gathers:
        s.finish()
    for d in range(1, groups):
        routed_copy(d).wait_send()
        group_copy(0, d, meta_v.at[fs]).wait_send()
        group_copy(1, d, x_v.at[fs]).wait_send()
        group_copy(2, d, sum_v.at[fs]).wait_send()

    all_copies(ssq_r, ssq_sem).wait_send()
    all_copies(meta_v.at[fs], meta_sem).wait_send()
    all_copies(home_s, home_sem).wait_recv()
    for j in range(peers):
        out_ref[0, :, j * depth : (j + 1) * depth] = home_r[j][:, :depth]
    all_copies(home_s, home_sem).wait_send()


def shards(
    residual,
    gain,
    queries,
    new_keys,
    cache,
    lengths,
    w_value,
    w_out,
    w_gate,
    w_up,
    w_down,
    expert_ids,
    gates,
):
    peers = lax.axis_size("exp")
    groups = lax.axis_size("fsdp")
    group_rows, steps, _, key = queries.shape
    tokens = group_rows * steps
    experts, depth, half = w_gate.shape
    block = tokens * groups // peers
    rows = block * TOP
    smem, dma = pl.BlockSpec(memory_space=pltpu.SMEM), pltpu.SemaphoreType.DMA
    scratch = [
        pltpu.VMEM((peers, experts * block, 2 * half), BF),
        pltpu.VMEM(w_out.shape[1:], BF),
        pltpu.VMEM((peers, w_out.shape[1], WIDE), BF),
        pltpu.VMEM((peers, 16, WIDE), F32),
        pltpu.VMEM((tokens, key), BF),
        pltpu.VMEM((tokens, key), BF),
        pltpu.VMEM((tokens, tokens), F32),
        pltpu.VMEM((tokens, w_value.shape[1]), BF),
        pltpu.VMEM((peers, tokens, WIDE), BF),
        pltpu.VMEM((tokens, WIDE), F32),
        pltpu.VMEM((8, tokens), F32),
        pltpu.VMEM((peers, 8, tokens), F32),
        pltpu.VMEM((groups, 8, tokens), F32),
        pltpu.VMEM((groups, tokens, WIDE), BF),
        pltpu.VMEM((groups, peers, 8, rows), F32),
        pltpu.VMEM(w_gate.shape, BF),
        pltpu.VMEM(w_gate.shape, BF),
        pltpu.VMEM(w_gate.shape, BF),
        pltpu.VMEM((peers, rows, 2 * half), BF),
        pltpu.VMEM((rows, 2 * half), F32),
        pltpu.VMEM((peers, rows, half), BF),
        pltpu.VMEM((peers, experts * block, rows), BF),
        pltpu.VMEM((peers, 1, rows), F32),
        pltpu.VMEM((groups, tokens, WIDE), BF),
        pltpu.VMEM((groups, tokens, WIDE), BF),
        pltpu.VMEM((peers, steps, WIDE), F32),
        pltpu.VMEM((peers, steps, WIDE), F32),
        dma((len(ROUTES), 2)),
        dma,
        dma((3,)),
        dma((2,)),
        dma((2,)),
        dma((2,)),
        dma((4, groups)),
        dma((4, groups)),
    ]
    for route in ROUTES:
        scratch += reduce_scratch(route, WIDE)
    for route in ROUTES:
        scratch += reduce_scratch(route, 2 * half)
    for route in ROUTES:
        scratch += gather_scratch(route)
    return pl.pallas_call(
        functools.partial(layer_kernel, peers, groups),
        out_shape=jax.ShapeDtypeStruct(residual.shape, F32),
        in_specs=[smem, vmem(), vmem(), anywhere(), vmem(), anywhere()]
        + [vmem()] * 4
        + [anywhere()] * 3,
        out_specs=vmem(),
        scratch_shapes=scratch,
        compiler_params=pltpu.CompilerParams(
            collective_id=0, has_side_effects=True, vmem_limit_bytes=HIGH
        ),
        name="layer",
    )(
        lengths,
        queries[:, :, 0, :],
        new_keys,
        cache,
        w_value[0],
        w_out[0],
        residual,
        gain.reshape(1, -1),
        expert_ids,
        gates,
        w_gate,
        w_up,
        w_down,
    )


def solution(mesh):
    return jax.shard_map(
        shards,
        mesh=mesh,
        in_specs=(
            P(("fsdp", "exp"), None, None),
            P(),
            P("fsdp", None, "exp", None),
            P("fsdp", None, None),
            P("fsdp", None, None),
            P("fsdp"),
            P("exp", None, None),
            P("exp", None, None),
            P(None, "exp", "fsdp"),
            P(None, "exp", "fsdp"),
            P(None, "exp", "fsdp"),
            P(("fsdp", "exp"), None, None),
            P(("fsdp", "exp"), None, None),
        ),
        out_specs=P(("fsdp", "exp"), None, None),
        check_vma=False,
    )
```

```python
import functools

import jax
import jax.numpy as jnp
from jax import lax
from jax.experimental import pallas as pl
from jax.experimental.pallas import tpu as pltpu
from jax.sharding import PartitionSpec as P

TOP = 8
STEPS = 4
score_scale = 0.07216878364870322
MESH = pl.DeviceIdType.MESH
BF = jnp.bfloat16
F32 = jnp.float32
WIDE = 256
HIGH = 60 * 1024 * 1024
NX, NZ, NY = 2, 4, 4
NT = (((1,), (1,)), ((), ()))


def matmul(a, b):
    return jnp.dot(a, b, preferred_element_type=F32)


def vmem():
    return pl.BlockSpec(memory_space=pltpu.VMEM)


def anywhere():
    return pl.BlockSpec(memory_space=pl.ANY)


def each(lower, upper, body):
    def step(i, carry):
        body(i)
        return carry

    lax.fori_loop(lower, upper, step, 0)


class Place:
    def __init__(self):
        self.me = lax.axis_index("exp")
        self.x = self.me // (NZ * NY)
        self.z = lax.rem(self.me // NY, NZ)
        self.y = lax.rem(self.me, NY)

    def index(self, x, z, y):
        return (lax.rem(x, NX) * NZ + lax.rem(z, NZ)) * NY + lax.rem(y, NY)

    def plus(self, offset):
        dx, dz, dy = offset
        return self.index(self.x + dx, self.z + dz, self.y + dy)

    def minus(self, offset):
        dx, dz, dy = offset
        return self.index(self.x + NX - dx, self.z + NZ - dz, self.y + NY - dy)


class Route:
    def __init__(self, kind, first, count):
        self.kind = kind
        self.first, self.count = first, count
        self.rows = pl.ds(first, count)
        self.line = NX if kind == "x" else NZ
        self.plane = NX * NZ * NY // self.line

    def offset(self, d, g):
        if self.kind == "z":
            return (g // NY, d, lax.rem(g, NY))
        if self.kind == "y":
            return (g // NZ, lax.rem(g, NZ), d)
        return (d, g // NY, lax.rem(g, NY))

    def split(self, offset):
        dx, dz, dy = offset
        if self.kind == "z":
            return dz, dx * NY + dy
        if self.kind == "y":
            return dy, dx * NZ + dz
        return dx, dz * NY + dy


ROUTES = (Route("z", 0, 48), Route("y", 48, 48), Route("x", 96, 32))
HEAD_ROUTES = (Route("z", 0, 80), Route("y", 80, 80), Route("x", 160, 64))


def remote(src, dst, send, recv, peer):
    return pltpu.make_async_remote_copy(
        src_ref=src,
        dst_ref=dst,
        send_sem=send,
        recv_sem=recv,
        device_id={"exp": peer},
        device_id_type=MESH,
    )


class Reduce:
    def __init__(self, place, route, src, bufs):
        self.place, self.route, self.src = place, route, src
        self.got, self.out, self.fin, self.s1, self.r1, self.s2, self.r2 = bufs

    def first(self, d, g):
        route = self.route
        return remote(
            self.src.at[self.place.plus(route.offset(d, g)), route.rows],
            self.got.at[g, d - 1],
            self.s1,
            self.r1.at[g],
            self.place.plus(route.offset(d, 0)),
        )

    def second(self, g):
        return remote(
            self.out.at[g],
            self.fin.at[g],
            self.s2,
            self.r2,
            self.place.plus(self.route.offset(0, g)),
        )

    def send(self, offset):
        d, g = self.route.split(offset)

        @pl.when(d > 0)
        def _():
            self.first(d, g).start()

    def step(self, g, acc_ref):
        route = self.route
        got = self.got.at[g]
        remote(got, got, self.s1, self.r1.at[g], self.place.me).wait_recv()
        total = self.src[self.place.plus(route.offset(0, g)), route.rows].astype(F32)
        for d in range(1, route.line):
            total = total + self.got[g, d - 1].astype(F32)

        @pl.when(g == 0)
        def _():
            acc_ref[route.rows] = total

        @pl.when(g != 0)
        def _():
            self.out[g] = total.astype(BF)
            self.second(g).start()

    def add(self, acc_ref):
        route = self.route
        rest = self.fin.at[pl.ds(1, route.plane - 1)]
        remote(rest, rest, self.s2, self.r2, self.place.me).wait_recv()
        total = acc_ref[route.rows]
        for g in range(1, route.plane):
            total = total + self.fin[g].astype(F32)
        acc_ref[route.rows] = total

    def finish(self):
        rest = self.out.at[pl.ds(1, self.route.plane - 1)]
        remote(self.got, self.got, self.s1, self.r1.at[0], self.place.me).wait_send()
        remote(rest, rest, self.s2, self.r2, self.place.me).wait_send()


def reduce_scratch(route, cols):
    lines, plane = route.line - 1, route.plane
    dma = pltpu.SemaphoreType.DMA
    return [
        pltpu.VMEM((plane, lines, route.count, cols), BF),
        pltpu.VMEM((plane, route.count, cols), BF),
        pltpu.VMEM((plane, route.count, cols), BF),
        dma,
        dma((plane,)),
        dma,
        dma,
    ]


class Gather:
    def __init__(self, place, route, whole, bufs):
        self.place, self.route, self.whole = place, route, whole
        self.s1, self.s2, self.r = bufs

    def near(self, g, source):
        block = self.whole.at[source, self.route.rows]
        return remote(
            block, block, self.s1, self.r.at[0, g], self.place.plus(self.route.offset(0, g))
        )

    def far(self, d, g, source):
        block = self.whole.at[source, self.route.rows]
        return remote(
            block, block, self.s2, self.r.at[d, g], self.place.plus(self.route.offset(d, 0))
        )

    def begin(self):
        each(1, self.route.plane, lambda g: self.near(g, self.place.me).start())
        self.forward(0)

    def forward(self, g):
        source = self.place.minus(self.route.offset(0, g))
        for d in range(1, self.route.line):
            self.far(d, g, source).start()

    def relay(self, g):
        self.near(g, self.place.minus(self.route.offset(0, g))).wait_recv()
        self.forward(g)

    def arrive(self, offset):
        d, g = self.route.split(offset)

        @pl.when(d > 0)
        def _():
            self.far(d, g, self.place.minus(offset)).wait_recv()

    def finish(self):
        route = self.route
        for sem, count in ((self.s1, route.plane - 1), (self.s2, (route.line - 1) * route.plane)):
            blocks = self.whole.at[pl.ds(0, count), route.rows]
            remote(blocks, blocks, sem, self.r.at[0, 0], self.place.me).wait_send()


def gather_scratch(route):
    dma = pltpu.SemaphoreType.DMA
    return [dma, dma, dma((route.line, route.plane))]


def offset_of(o):
    return (o // (NZ * NY), lax.rem(o // NY, NZ), lax.rem(o, NY))


def spread(block, lanes):
    wide = jnp.concatenate([block] * (lanes // block.shape[1]), axis=1)
    step = lax.rem(lax.broadcasted_iota(jnp.int32, wide.shape, 1) // TOP, STEPS)
    row = lax.broadcasted_iota(jnp.int32, wide.shape, 0)
    return jnp.sum(jnp.where(step == row, wide, 0.0), 0, keepdims=True)


def layer_kernel(peers, groups, *refs):
    (
        len_ref,
        q_ref,
        nk_ref,
        cache_ref,
        wv_ref,
        wo_ref,
        res_ref,
        gain_ref,
        ids_ref,
        gates_ref,
        wg_ref,
        wu_ref,
        wd_ref,
        out_ref,
        dense,
        wo_v,
        wo_t,
        res_s,
        res_r,
        q_s,
        nk_s,
        new_s,
        ctx_s,
        send_v,
        att_t,
        att,
        ssq_s,
        ssq_r,
        sum_v,
        x_v,
        meta_v,
        wg_v,
        wu_v,
        wd_v,
        part_v,
        acc,
        hid_v,
        spread_s,
        gate_s,
        routed_v,
        routed_r,
        home_s,
        home_r,
        cache_sem,
        wo_sem,
        w_sem,
        ssq_sem,
        meta_sem,
        res_sem,
        home_sem,
        g_send,
        g_recv,
    ) = refs[:52]
    place = Place()
    me = place.me
    fs = lax.axis_index("fsdp")
    tokens = q_s.shape[0]
    latent = wv_ref.shape[0]
    experts, depth, half = wg_ref.shape
    rows = part_v.shape[1]
    block = rows // TOP
    per = peers // groups
    own_rows = home_s.shape[1]
    barrier = pltpu.get_barrier_semaphore()

    def greet(axis, mine, size):
        def one(d):
            pl.semaphore_signal(
                barrier, inc=1, device_id={axis: lax.rem(mine + d, size)}, device_id_type=MESH
            )

        each(1, size, one)

    greet("exp", me, peers)
    greet("fsdp", fs, groups)
    rest = refs[52:]
    heads = [
        Reduce(place, r, send_v, rest[7 * i : 7 * i + 7]) for i, r in enumerate(HEAD_ROUTES)
    ]
    rest = rest[7 * len(ROUTES) :]
    sums = [Reduce(place, r, part_v, rest[7 * i : 7 * i + 7]) for i, r in enumerate(ROUTES)]
    rest = rest[7 * len(ROUTES) :]
    gathers = [Gather(place, r, hid_v, rest[3 * i : 3 * i + 3]) for i, r in enumerate(ROUTES)]

    def group_copy(n, d, block_ref):
        return pltpu.make_async_remote_copy(
            src_ref=block_ref,
            dst_ref=block_ref,
            send_sem=g_send.at[n, d],
            recv_sem=g_recv.at[n, d],
            device_id={"fsdp": lax.rem(fs + d, groups)},
            device_id_type=MESH,
        )

    def from_group(d):
        return lax.rem(fs + groups - d, groups)

    def cache_copy(i, n):
        span = pl.ds(ROUTES[i].first // STEPS, ROUTES[i].count // STEPS)
        positions = cache_ref.shape[2]
        if n == 0:
            src = cache_ref.at[span, pl.ds(0, latent)]
            dst = dense.at[span, pl.ds(0, latent), pl.ds(0, positions)]
        else:
            left = cache_ref.shape[1] - latent
            src = cache_ref.at[span, pl.ds(latent, left)]
            dst = dense.at[span, pl.ds(0, left), pl.ds(positions, positions)]
        return pltpu.make_async_copy(src, dst, cache_sem.at[i, n])

    def weight_copy(n):
        src = (wg_ref, wu_ref, wd_ref)[n]
        dst = (wg_v, wu_v, wd_v)[n]
        return pltpu.make_async_copy(src, dst, w_sem.at[n])

    out_copy = pltpu.make_async_copy(wo_ref, wo_v, wo_sem)
    for n in range(2):
        cache_copy(0, n).start()
    out_copy.start()
    for i in range(1, len(ROUTES)):
        for n in range(2):
            cache_copy(i, n).start()

    for b in range(tokens // 16):
        span = slice(b * 16, b * 16 + 16)
        q_s[span, :] = jnp.concatenate(
            [q_ref[4 * b + i].astype(F32) for i in range(4)], axis=0
        ).astype(BF)
        nk_s[span, :] = jnp.concatenate(
            [nk_ref[4 * b + i].astype(F32) for i in range(4)], axis=0
        ).astype(BF)

    token_r = lax.broadcasted_iota(jnp.int32, (tokens, tokens), 0)
    token_c = lax.broadcasted_iota(jnp.int32, (tokens, tokens), 1)
    diagonal = token_r == token_c
    same = (token_r // STEPS == token_c // STEPS) & (token_c <= token_r)
    fresh = lax.dot_general(q_s[...], nk_s[...], NT, preferred_element_type=F32)
    new_s[...] = jnp.where(same, fresh * score_scale, -1e30)

    which = lax.broadcasted_iota(jnp.int32, (16, 1), 0) // STEPS
    position = lax.broadcasted_iota(jnp.int32, (16, cache_ref.shape[2]), 1)
    rope = cache_ref.shape[1] - latent

    def attend(b):
        span = pl.ds(pl.multiple_of(b * 16, 16), 16)
        first = b * 4
        q16 = q_s[span, :]

        def score(row):
            return matmul(q16[:, :latent], dense[row, :, : position.shape[1]]) + matmul(
                q16[:, latent:], dense[row, :rope, position.shape[1] :]
            )

        scores = score(first)
        length = jnp.full(position.shape, len_ref[first])
        for n in range(1, 4):
            scores = jnp.where(which == n, score(first + n), scores)
            length = jnp.where(which == n, len_ref[first + n], length)
        scores = jnp.where(position < length, scores * score_scale, -1e30)
        new = new_s[span, :]
        highest = jnp.maximum(jnp.max(scores, -1, keepdims=True), jnp.max(new, -1, keepdims=True))
        cache_exp = jnp.exp(scores - highest)
        new_exp = jnp.exp(new - highest)
        total = jnp.sum(cache_exp, -1, keepdims=True) + jnp.sum(new_exp, -1, keepdims=True)
        cache_w = (cache_exp / total).astype(BF)
        new_w = (new_exp / total).astype(BF)

        def mix(row):
            return lax.dot_general(
                cache_w, dense[row, :, : position.shape[1]], NT, preferred_element_type=F32
            )

        context = mix(first)
        for n in range(1, 4):
            context = jnp.where(which == n, mix(first + n), context)
        context = context + matmul(new_w, nk_s[:, :latent])
        ctx_s[span, :] = context.astype(BF)

    def meta_copy(d):
        tile = meta_v.at[fs, me]
        return remote(tile, tile, meta_sem.at[0], meta_sem.at[1], lax.rem(me + d, peers))

    def all_copies(buffer, sem):
        tiles = buffer.at[pl.ds(0, peers - 1)]
        return remote(tiles, tiles, sem.at[0], sem.at[1], me)

    for i, route in enumerate(ROUTES):
        for n in range(2):
            cache_copy(i, n).wait()
        each(route.first // 16, (route.first + route.count) // 16, attend)
        if i == 0:
            for n in range(3):
                weight_copy(n).start()

    out_copy.wait()
    for c in range(wo_v.shape[1] // 128):
        span = slice(c * 128, c * 128 + 128)
        wo_t[span, :] = wo_v[:, span].T
    gain = jnp.zeros((1, depth), F32)
    for j in range(peers):
        part = slice(j * depth, (j + 1) * depth)
        res_s[j, :, :depth] = res_ref[0, :, part].astype(F32)
        gain = jnp.where(me == j, gain_ref[:, part], gain)
    gain = jnp.concatenate([gain, jnp.zeros((1, WIDE - depth), F32)], axis=1)
    lane = lax.broadcasted_iota(jnp.int32, (1, rows), 1)
    here = lane // (STEPS * TOP) == lax.rem(me, 4)
    own_ids = jnp.where(here, spread(ids_ref[0].astype(F32), rows), 0.0)
    own_gates = jnp.where(here, spread(gates_ref[0], rows), 0.0)
    meta_v[fs, me] = jnp.concatenate([own_ids, own_gates, jnp.zeros((6, rows), F32)], axis=0)
    values = matmul(ctx_s[...], wv_ref[...]).astype(BF)
    pl.semaphore_wait(barrier, peers - 1 + groups - 1)

    def project(n):
        offsets = [offset_of(4 * n + k) for k in range(4)]
        for offset in offsets:
            j = place.plus(offset)
            span = pl.ds(pl.multiple_of(j * depth, 16), depth)
            part = lax.dot_general(wo_t[span, :], values, NT, preferred_element_type=F32)
            send_v[j] = part.astype(BF)
        for offset in offsets:
            for h in heads:
                h.send(offset)

    each(0, peers // 4, project)

    def res_copy(d):
        peer = lax.rem(me + d, peers)
        return remote(res_s.at[peer], res_r.at[me], res_sem.at[0], res_sem.at[1], peer)

    each(1, peers, lambda d: meta_copy(d).start())
    each(1, peers, lambda d: res_copy(d).start())
    res_r[me] = res_s[me]

    all_copies(meta_v.at[fs], meta_sem).wait_recv()
    for d in range(1, groups):
        group_copy(0, d, meta_v.at[fs]).start()

    for h in heads:
        each(1, h.route.plane, lambda g, h=h: h.step(g, att_t))
        h.step(0, att_t)
    pair_lane = lax.broadcasted_iota(jnp.int32, (1, rows), 1)
    slot_c = lax.broadcasted_iota(jnp.int32, (rows, experts * block), 1)
    slot_r = lax.broadcasted_iota(jnp.int32, (experts * block, rows), 0)

    def read_meta(q):
        piece = from_group(q)

        def one(n):
            info = meta_v[piece, 4 * n]
            for i in range(1, 4):
                info = info + meta_v[piece, 4 * n + i]
            j = piece * per + n
            code = info[0:1, :].astype(jnp.int32) * block + pair_lane // TOP
            spread_s[j] = (code == slot_r).astype(F32).astype(BF)
            code = jnp.sum(jnp.where(diagonal, code, 0), 1, keepdims=True)
            part_v[j] = (code == slot_c).astype(F32).astype(BF)
            gate_s[j] = info[1:2, :]

        each(0, per, one)

    read_meta(0)
    for q in range(1, groups):
        group_copy(0, q, meta_v.at[from_group(q)]).wait_recv()
        read_meta(q)
    for h in heads:
        h.add(att_t)
    all_copies(res_s, res_sem).wait_recv()

    attended = jnp.concatenate([att_t[...], jnp.zeros((WIDE - depth, tokens), F32)], axis=0).T
    own_res = jnp.concatenate([res_r[n][:, :depth] for n in range(peers)], axis=0)
    own_res = jnp.concatenate([own_res, jnp.zeros((tokens, WIDE - depth), F32)], axis=1)
    attended = attended + own_res
    att[...] = attended
    x_v[fs] = (attended * gain).astype(BF)
    for d in range(1, groups):
        group_copy(1, d, x_v.at[fs]).start()
    column = jnp.sum(attended * attended, -1, keepdims=True)
    row = jnp.sum(jnp.where(diagonal, column, 0.0), 0, keepdims=True)
    ssq_s[...] = jnp.broadcast_to(row, ssq_s.shape)

    def ssq_copy(d):
        return remote(ssq_s, ssq_r.at[d], ssq_sem.at[0], ssq_sem.at[1], lax.rem(me + d, peers))

    ssq_r[0] = ssq_s[...]
    each(1, peers, lambda d: ssq_copy(d).start())

    def multiply(first, count, x):
        def some(n):
            for e in [4 * n + k for k in range(4)]:
                spot = pl.ds(pl.multiple_of(e * block, block), block)
                gate = matmul(x, wg_v[e]).astype(BF)
                up = matmul(x, wu_v[e]).astype(BF)
                dense[first : first + count, spot, :half] = gate.reshape(count, block, half)
                dense[first : first + count, spot, half:] = up.reshape(count, block, half)

        each(0, experts // 4, some)

    def pick(i):
        found = []
        for k in range(2):
            q = (2 * i + k) // per
            n = lax.rem((2 * i + k) // NY, 2) * NY + lax.rem(place.y + 2 * i + k, NY)
            j = from_group(q) * per + n
            found.append((j, matmul(part_v[j], dense[q * per + n]).astype(BF)))
        for j, part in found:
            part_v[j] = part
        for j, _ in found:
            offset = (
                lax.rem(j // (NZ * NY) + NX - place.x, NX),
                lax.rem(lax.rem(j // NY, NZ) + NZ - place.z, NZ),
                lax.rem(lax.rem(j, NY) + NY - place.y, NY),
            )
            for s in sums:
                s.send(offset)

    def pick_group(q):
        each(q * per // 2, (q + 1) * per // 2, pick)

    def relay(q):
        p = from_group(q)
        x_off = lax.rem(p // 2 + NX - place.x, NX)
        z_low = 2 * lax.rem(p, 2)

        def z_off(i):
            return lax.rem(z_low + i + NZ - place.z, NZ)

        @pl.when(lax.rem(p, 2) == place.z // 2)
        def _():
            each(0, NY, lambda i: sums[0].step(x_off * NY + i, acc))

        each(0, 2, lambda i: sums[1].step(x_off * NZ + z_off(i), acc))

        @pl.when(x_off == 0)
        def _():
            each(0, 2 * NY, lambda i: sums[2].step(z_off(i // NY) * NY + lax.rem(i, NY), acc))

    weight_copy(0).wait()
    weight_copy(1).wait()
    multiply(0, per, x_v[fs][:, :depth])
    pick_group(0)

    all_copies(ssq_r.at[pl.ds(1, peers - 1)], ssq_sem).wait_recv()
    sum_v[fs] = jnp.sum(ssq_r[...], axis=0)
    for d in range(1, groups):
        group_copy(2, d, sum_v.at[fs]).start()
    for q in range(1, groups):
        group_copy(1, q, x_v.at[from_group(q)]).wait_recv()
    others = [x_v[from_group(q)][:, :depth] for q in range(1, groups)]
    multiply(per, peers - per, jnp.concatenate(others, axis=0))
    pick_group(1)
    relay(0)
    pick_group(2)
    relay(1)
    pick_group(3)
    relay(2)
    relay(3)

    for s in sums:
        s.add(acc)

    for d in range(1, groups):
        group_copy(2, d, sum_v.at[from_group(d)]).wait_recv()
    token = block * lax.rem(me, per) + token_r // TOP
    squares = jnp.sum(jnp.where(token == token_c, sum_v[me // per][:1, :], 0.0), 1, keepdims=True)
    scale = lax.rsqrt(squares / (depth * peers) + 1e-06)
    weight = jnp.sum(jnp.where(diagonal, gate_s[me], 0.0), 1, keepdims=True)
    gate = acc[:, :half] * scale
    up = acc[:, half:] * scale
    hid_v[me] = (gate / (1.0 + jnp.exp(-gate)) * up * weight).astype(BF)

    for g in gathers:
        g.begin()
    for g in gathers:
        each(1, g.route.plane, g.relay)

    def expand(n):
        offsets = [offset_of(2 * n), offset_of(2 * n + 1)]
        for offset in offsets:
            for g in gathers:
                g.arrive(offset)
        blocks = [place.minus(offset) for offset in offsets]
        full = [matmul(spread_s[j], hid_v[j]).astype(BF) for j in blocks]
        for j, rows_of in zip(blocks, full):
            spot = pl.ds(pl.multiple_of(j * block, block), block)
            dense[:, spot, :half] = rows_of.reshape(experts, block, half)

    each(0, peers // 2, expand)
    weight_copy(2).wait()

    def shares(pieces):
        spots = [pl.ds(pl.multiple_of(p * tokens, tokens), tokens) for p in pieces]

        def some(n, total):
            for k in range(4):
                e = 4 * n + k
                both = jnp.concatenate([dense[e, spot, :half] for spot in spots], axis=0)
                total = total + lax.dot_general(both, wd_v[e], NT, preferred_element_type=F32)
            return total

        start = jnp.zeros((len(pieces) * tokens, depth), F32)
        return lax.fori_loop(0, experts // 4, some, start)

    def routed_copy(d):
        peer = lax.rem(fs + d, groups)
        return pltpu.make_async_remote_copy(
            src_ref=routed_v.at[peer],
            dst_ref=routed_r.at[d],
            send_sem=g_send.at[3, d],
            recv_sem=g_recv.at[3, d],
            device_id={"fsdp": peer},
            device_id_type=MESH,
        )

    mixed = att[:, :depth]
    for pair in ((2, 3), (1, 0)):
        both = shares([lax.rem(fs + d, groups) for d in pair])
        for k, d in enumerate(pair):
            share = both[k * tokens : (k + 1) * tokens]
            if d > 0:
                routed_v[lax.rem(fs + d, groups), :, :depth] = share.astype(BF)
                routed_copy(d).start()
            else:
                mixed = mixed + share
    for d in range(1, groups):
        routed_copy(d).wait_recv()
        mixed = mixed + routed_r[d][:, :depth].astype(F32)
    for j in range(peers):
        home_s[j, :, :depth] = mixed[j * own_rows : (j + 1) * own_rows, :]

    def home_copy(d):
        peer = lax.rem(me + d, peers)
        return remote(home_s.at[peer], home_r.at[me], home_sem.at[0], home_sem.at[1], peer)

    each(1, peers, lambda d: home_copy(d).start())
    home_r[me] = home_s[me]
    for s in heads + sums + gathers:
        s.finish()
    for d in range(1, groups):
        routed_copy(d).wait_send()
        group_copy(0, d, meta_v.at[fs]).wait_send()
        group_copy(1, d, x_v.at[fs]).wait_send()
        group_copy(2, d, sum_v.at[fs]).wait_send()

    all_copies(ssq_r, ssq_sem).wait_send()
    all_copies(meta_v.at[fs], meta_sem).wait_send()
    all_copies(res_s, res_sem).wait_send()
    all_copies(home_s, home_sem).wait_recv()
    for j in range(peers):
        out_ref[0, :, j * depth : (j + 1) * depth] = home_r[j][:, :depth]
    all_copies(home_s, home_sem).wait_send()


def shards(
    residual,
    gain,
    queries,
    new_keys,
    cache,
    lengths,
    w_value,
    w_out,
    w_gate,
    w_up,
    w_down,
    expert_ids,
    gates,
):
    peers = lax.axis_size("exp")
    groups = lax.axis_size("fsdp")
    group_rows, steps, _, key = queries.shape
    tokens = group_rows * steps
    experts, depth, half = w_gate.shape
    block = tokens * groups // peers
    rows = block * TOP
    smem, dma = pl.BlockSpec(memory_space=pltpu.SMEM), pltpu.SemaphoreType.DMA
    scratch = [
        pltpu.VMEM((peers, experts * block, 2 * half), BF),
        pltpu.VMEM(w_out.shape[1:], BF),
        pltpu.VMEM((w_out.shape[2], w_out.shape[1]), BF),
        pltpu.VMEM((peers, steps, WIDE), F32),
        pltpu.VMEM((peers, steps, WIDE), F32),
        pltpu.VMEM((tokens, key), BF),
        pltpu.VMEM((tokens, key), BF),
        pltpu.VMEM((tokens, tokens), F32),
        pltpu.VMEM((tokens, w_value.shape[1]), BF),
        pltpu.VMEM((peers, depth, tokens), BF),
        pltpu.VMEM((depth, tokens), F32),
        pltpu.VMEM((tokens, WIDE), F32),
        pltpu.VMEM((8, tokens), F32),
        pltpu.VMEM((peers, 8, tokens), F32),
        pltpu.VMEM((groups, 8, tokens), F32),
        pltpu.VMEM((groups, tokens, WIDE), BF),
        pltpu.VMEM((groups, peers, 8, rows), F32),
        pltpu.VMEM(w_gate.shape, BF),
        pltpu.VMEM(w_gate.shape, BF),
        pltpu.VMEM(w_gate.shape, BF),
        pltpu.VMEM((peers, rows, 2 * half), BF),
        pltpu.VMEM((rows, 2 * half), F32),
        pltpu.VMEM((peers, rows, half), BF),
        pltpu.VMEM((peers, experts * block, rows), BF),
        pltpu.VMEM((peers, 1, rows), F32),
        pltpu.VMEM((groups, tokens, WIDE), BF),
        pltpu.VMEM((groups, tokens, WIDE), BF),
        pltpu.VMEM((peers, steps, WIDE), F32),
        pltpu.VMEM((peers, steps, WIDE), F32),
        dma((len(ROUTES), 2)),
        dma,
        dma((3,)),
        dma((2,)),
        dma((2,)),
        dma((2,)),
        dma((2,)),
        dma((4, groups)),
        dma((4, groups)),
    ]
    for route in HEAD_ROUTES:
        scratch += reduce_scratch(route, tokens)
    for route in ROUTES:
        scratch += reduce_scratch(route, 2 * half)
    for route in ROUTES:
        scratch += gather_scratch(route)
    return pl.pallas_call(
        functools.partial(layer_kernel, peers, groups),
        out_shape=jax.ShapeDtypeStruct(residual.shape, F32),
        in_specs=[smem, vmem(), vmem(), anywhere(), vmem(), anywhere()]
        + [vmem()] * 4
        + [anywhere()] * 3,
        out_specs=vmem(),
        scratch_shapes=scratch,
        compiler_params=pltpu.CompilerParams(
            collective_id=0, has_side_effects=True, vmem_limit_bytes=HIGH
        ),
        name="layer",
    )(
        lengths,
        queries[:, :, 0, :],
        new_keys,
        cache,
        w_value[0],
        w_out[0],
        residual,
        gain.reshape(1, -1),
        expert_ids,
        gates,
        w_gate,
        w_up,
        w_down,
    )


def solution(mesh):
    return jax.shard_map(
        shards,
        mesh=mesh,
        in_specs=(
            P(("fsdp", "exp"), None, None),
            P(),
            P("fsdp", None, "exp", None),
            P("fsdp", None, None),
            P("fsdp", None, None),
            P("fsdp"),
            P("exp", None, None),
            P("exp", None, None),
            P(None, "exp", "fsdp"),
            P(None, "exp", "fsdp"),
            P(None, "exp", "fsdp"),
            P(("fsdp", "exp"), None, None),
            P(("fsdp", "exp"), None, None),
        ),
        out_specs=P(("fsdp", "exp"), None, None),
        check_vma=False,
    )
```

```python
import functools

import jax
import jax.numpy as jnp
from jax import lax
from jax.experimental import pallas as pl
from jax.experimental.pallas import tpu as pltpu
from jax.sharding import PartitionSpec as P

TOP = 8
STEPS = 4
score_scale = 0.07216878364870322
MESH = pl.DeviceIdType.MESH
BF = jnp.bfloat16
F32 = jnp.float32
WIDE = 256
HIGH = 60 * 1024 * 1024
NX, NZ, NY = 2, 4, 4
NT = (((1,), (1,)), ((), ()))


def matmul(a, b):
    return jnp.dot(a, b, preferred_element_type=F32)


def vmem():
    return pl.BlockSpec(memory_space=pltpu.VMEM)


def anywhere():
    return pl.BlockSpec(memory_space=pl.ANY)


def each(lower, upper, body):
    def step(i, carry):
        body(i)
        return carry

    lax.fori_loop(lower, upper, step, 0)


class Place:
    def __init__(self):
        self.me = lax.axis_index("exp")
        self.x = self.me // (NZ * NY)
        self.z = lax.rem(self.me // NY, NZ)
        self.y = lax.rem(self.me, NY)

    def index(self, x, z, y):
        return (lax.rem(x, NX) * NZ + lax.rem(z, NZ)) * NY + lax.rem(y, NY)

    def plus(self, offset):
        dx, dz, dy = offset
        return self.index(self.x + dx, self.z + dz, self.y + dy)

    def minus(self, offset):
        dx, dz, dy = offset
        return self.index(self.x + NX - dx, self.z + NZ - dz, self.y + NY - dy)


class Route:
    def __init__(self, kind, first, count):
        self.axes = {"z": (1, 2, 0), "y": (2, 0, 1), "x": (0, 1, 2)}[kind]
        self.n = tuple((NX, NZ, NY)[a] for a in self.axes)
        self.first, self.count = first, count
        self.rows = pl.ds(first, count)
        self.plane = self.n[1] * self.n[2]

    def offset(self, d1, d2, d3):
        out = [0, 0, 0]
        for a, d in zip(self.axes, (d1, d2, d3)):
            out[a] = d
        return tuple(out)

    def split(self, offset):
        return tuple(offset[a] for a in self.axes)


ROUTES = (Route("z", 0, 32), Route("y", 32, 48), Route("x", 80, 48))
HEAD_ROUTES = (Route("z", 0, 64), Route("y", 64, 80), Route("x", 144, 80))


def remote(src, dst, send, recv, peer):
    return pltpu.make_async_remote_copy(
        src_ref=src,
        dst_ref=dst,
        send_sem=send,
        recv_sem=recv,
        device_id={"exp": peer},
        device_id_type=MESH,
    )


class Reduce:
    def __init__(self, place, route, src, bufs):
        self.place, self.route, self.src = place, route, src
        self.got1, self.out1, self.got2, self.keep, self.out2, self.got3 = bufs[:6]
        self.sent, self.r1, self.r2 = bufs[6:]

    def first(self, d1, d2, d3):
        route = self.route
        g = d2 * route.n[2] + d3
        return remote(
            self.src.at[self.place.plus(route.offset(d1, d2, d3)), route.rows],
            self.got1.at[g, d1 - 1],
            self.sent.at[0],
            self.r1.at[g],
            self.place.plus(route.offset(d1, 0, 0)),
        )

    def second(self, d2, d3):
        return remote(
            self.out1.at[d2 * self.route.n[2] + d3],
            self.got2.at[d3, d2 - 1],
            self.sent.at[1],
            self.r2.at[d3],
            self.place.plus(self.route.offset(0, d2, 0)),
        )

    def third(self, d3):
        return remote(
            self.out2.at[d3],
            self.got3.at[d3 - 1],
            self.sent.at[2],
            self.r2.at[self.route.n[2]],
            self.place.plus(self.route.offset(0, 0, d3)),
        )

    def send(self, offset):
        d1, d2, d3 = self.route.split(offset)

        @pl.when(d1 > 0)
        def _():
            self.first(d1, d2, d3).start()

    def arrived(self, got, sem):
        remote(got, got, self.sent.at[0], sem, self.place.me).wait_recv()

    def step(self, g):
        route = self.route
        d2, d3 = g // route.n[2], lax.rem(g, route.n[2])
        self.arrived(self.got1.at[g], self.r1.at[g])
        total = self.src[self.place.plus(route.offset(0, d2, d3)), route.rows].astype(F32)
        for d in range(1, route.n[0]):
            total = total + self.got1[g, d - 1].astype(F32)

        @pl.when(d2 == 0)
        def _():
            self.keep[d3] = total

        @pl.when(d2 != 0)
        def _():
            self.out1[g] = total.astype(BF)
            self.second(d2, d3).start()

    def turn(self, d3):
        self.arrived(self.got2.at[d3], self.r2.at[d3])
        total = self.keep[d3]
        for d in range(1, self.route.n[1]):
            total = total + self.got2[d3, d - 1].astype(F32)
        return total

    def turns(self):
        for d3 in range(1, self.route.n[2]):
            self.out2[d3] = self.turn(d3).astype(BF)
            self.third(d3).start()
        self.keep[0] = self.turn(0)

    def add(self, acc_ref):
        self.arrived(self.got3, self.r2.at[self.route.n[2]])
        total = self.keep[0]
        for d in range(1, self.route.n[2]):
            total = total + self.got3[d - 1].astype(F32)
        acc_ref[self.route.rows] = total

    def finish(self):
        for n, got in enumerate((self.got1, self.got2, self.got3)):
            remote(got, got, self.sent.at[n], self.r2.at[0], self.place.me).wait_send()


def reduce_scratch(route, cols):
    n1, n2, n3 = route.n
    dma = pltpu.SemaphoreType.DMA
    return [
        pltpu.VMEM((n2 * n3, n1 - 1, route.count, cols), BF),
        pltpu.VMEM((n2 * n3, route.count, cols), BF),
        pltpu.VMEM((n3, n2 - 1, route.count, cols), BF),
        pltpu.VMEM((n3, route.count, cols), F32),
        pltpu.VMEM((n3, route.count, cols), BF),
        pltpu.VMEM((n3 - 1, route.count, cols), BF),
        dma((3,)),
        dma((n2 * n3,)),
        dma((n3 + 1,)),
    ]


class Gather:
    def __init__(self, place, route, whole, bufs):
        self.place, self.route, self.whole = place, route, whole
        self.sent, self.r = bufs

    def copy(self, source, to, offset):
        _, n2, n3 = self.route.n
        d1, d2, d3 = offset
        block = self.whole.at[source, self.route.rows]
        peer = self.place.plus(self.route.offset(*to))
        return remote(block, block, self.sent, self.r.at[(d1 * n2 + d2) * n3 + d3], peer)

    def source(self, *offset):
        return self.place.minus(self.route.offset(*offset))

    def push1(self, d2, d3):
        for d in range(1, self.route.n[0]):
            self.copy(self.source(0, d2, d3), (d, 0, 0), (d, d2, d3)).start()

    def push2(self, d3):
        for d in range(1, self.route.n[1]):
            self.copy(self.source(0, 0, d3), (0, d, 0), (0, d, d3)).start()

    def begin(self):
        for d in range(1, self.route.n[2]):
            self.copy(self.place.me, (0, 0, d), (0, 0, d)).start()
        self.push2(0)
        self.push1(0, 0)

    def wait(self, offset):
        self.copy(self.source(*offset), (0, 0, 0), offset).wait_recv()

    def relay_last(self, d3):
        self.wait((0, 0, d3))
        self.push2(d3)
        self.push1(0, d3)

    def relay_middle(self, g):
        d2, d3 = g // self.route.n[2], lax.rem(g, self.route.n[2])
        self.wait((0, d2, d3))
        self.push1(d2, d3)

    def arrive(self, offset):
        split = self.route.split(offset)

        @pl.when(split[0] > 0)
        def _():
            self.wait(split)

    def finish(self):
        n1, n2, n3 = self.route.n
        blocks = self.whole.at[pl.ds(0, n1 * n2 * n3 - 1), self.route.rows]
        remote(blocks, blocks, self.sent, self.r.at[0], self.place.me).wait_send()


def gather_scratch(route):
    dma = pltpu.SemaphoreType.DMA
    return [dma, dma((route.n[0] * route.n[1] * route.n[2],))]


def offset_of(o):
    return (o // (NZ * NY), lax.rem(o // NY, NZ), lax.rem(o, NY))


def spread(block, lanes):
    wide = jnp.concatenate([block] * (lanes // block.shape[1]), axis=1)
    step = lax.rem(lax.broadcasted_iota(jnp.int32, wide.shape, 1) // TOP, STEPS)
    row = lax.broadcasted_iota(jnp.int32, wide.shape, 0)
    return jnp.sum(jnp.where(step == row, wide, 0.0), 0, keepdims=True)


def layer_kernel(peers, groups, *refs):
    (
        len_ref,
        q_ref,
        nk_ref,
        cache_ref,
        wv_ref,
        wo_ref,
        res_ref,
        gain_ref,
        ids_ref,
        gates_ref,
        wg_ref,
        wu_ref,
        wd_ref,
        out_ref,
        dense,
        wo_v,
        wo_t,
        res_s,
        res_r,
        q_s,
        nk_s,
        new_s,
        ctx_s,
        send_v,
        att_t,
        att,
        ssq_s,
        ssq_r,
        sum_v,
        x_v,
        meta_v,
        wg_v,
        wu_v,
        wd_v,
        part_v,
        acc,
        hid_v,
        spread_s,
        gate_s,
        routed_v,
        routed_r,
        home_s,
        home_r,
        cache_sem,
        wo_sem,
        w_sem,
        ssq_sem,
        meta_sem,
        res_sem,
        home_sem,
        g_send,
        g_recv,
    ) = refs[:52]
    place = Place()
    me = place.me
    fs = lax.axis_index("fsdp")
    tokens = q_s.shape[0]
    latent = wv_ref.shape[0]
    experts, depth, half = wg_ref.shape
    rows = part_v.shape[1]
    block = rows // TOP
    per = peers // groups
    own_rows = home_s.shape[1]
    barrier = pltpu.get_barrier_semaphore()

    def greet(axis, mine, size):
        def one(d):
            pl.semaphore_signal(
                barrier, inc=1, device_id={axis: lax.rem(mine + d, size)}, device_id_type=MESH
            )

        each(1, size, one)

    greet("exp", me, peers)
    greet("fsdp", fs, groups)
    rest = refs[52:]
    heads = [
        Reduce(place, r, send_v, rest[9 * i : 9 * i + 9]) for i, r in enumerate(HEAD_ROUTES)
    ]
    rest = rest[9 * len(ROUTES) :]
    sums = [Reduce(place, r, part_v, rest[9 * i : 9 * i + 9]) for i, r in enumerate(ROUTES)]
    rest = rest[9 * len(ROUTES) :]
    gathers = [Gather(place, r, hid_v, rest[2 * i : 2 * i + 2]) for i, r in enumerate(ROUTES)]

    def group_copy(n, d, block_ref):
        return pltpu.make_async_remote_copy(
            src_ref=block_ref,
            dst_ref=block_ref,
            send_sem=g_send.at[n, d],
            recv_sem=g_recv.at[n, d],
            device_id={"fsdp": lax.rem(fs + d, groups)},
            device_id_type=MESH,
        )

    def from_group(d):
        return lax.rem(fs + groups - d, groups)

    def cache_copy(i, n):
        span = pl.ds(ROUTES[i].first // STEPS, ROUTES[i].count // STEPS)
        positions = cache_ref.shape[2]
        if n == 0:
            src = cache_ref.at[span, pl.ds(0, latent)]
            dst = dense.at[span, pl.ds(0, latent), pl.ds(0, positions)]
        else:
            left = cache_ref.shape[1] - latent
            src = cache_ref.at[span, pl.ds(latent, left)]
            dst = dense.at[span, pl.ds(0, left), pl.ds(positions, positions)]
        return pltpu.make_async_copy(src, dst, cache_sem.at[i, n])

    def weight_copy(n):
        src = (wg_ref, wu_ref, wd_ref)[n]
        dst = (wg_v, wu_v, wd_v)[n]
        return pltpu.make_async_copy(src, dst, w_sem.at[n])

    out_copy = pltpu.make_async_copy(wo_ref, wo_v, wo_sem)
    for n in range(2):
        cache_copy(0, n).start()
    out_copy.start()
    for i in range(1, len(ROUTES)):
        for n in range(2):
            cache_copy(i, n).start()

    for b in range(tokens // 16):
        span = slice(b * 16, b * 16 + 16)
        q_s[span, :] = jnp.concatenate(
            [q_ref[4 * b + i].astype(F32) for i in range(4)], axis=0
        ).astype(BF)
        nk_s[span, :] = jnp.concatenate(
            [nk_ref[4 * b + i].astype(F32) for i in range(4)], axis=0
        ).astype(BF)

    token_r = lax.broadcasted_iota(jnp.int32, (tokens, tokens), 0)
    token_c = lax.broadcasted_iota(jnp.int32, (tokens, tokens), 1)
    diagonal = token_r == token_c
    same = (token_r // STEPS == token_c // STEPS) & (token_c <= token_r)
    fresh = lax.dot_general(q_s[...], nk_s[...], NT, preferred_element_type=F32)
    new_s[...] = jnp.where(same, fresh * score_scale, -1e30)

    which = lax.broadcasted_iota(jnp.int32, (16, 1), 0) // STEPS
    position = lax.broadcasted_iota(jnp.int32, (16, cache_ref.shape[2]), 1)
    rope = cache_ref.shape[1] - latent

    def attend(b):
        span = pl.ds(pl.multiple_of(b * 16, 16), 16)
        first = b * 4
        q16 = q_s[span, :]

        def score(row):
            return matmul(q16[:, :latent], dense[row, :, : position.shape[1]]) + matmul(
                q16[:, latent:], dense[row, :rope, position.shape[1] :]
            )

        scores = score(first)
        length = jnp.full(position.shape, len_ref[first])
        for n in range(1, 4):
            scores = jnp.where(which == n, score(first + n), scores)
            length = jnp.where(which == n, len_ref[first + n], length)
        scores = jnp.where(position < length, scores * score_scale, -1e30)
        new = new_s[span, :]
        highest = jnp.maximum(jnp.max(scores, -1, keepdims=True), jnp.max(new, -1, keepdims=True))
        cache_exp = jnp.exp(scores - highest)
        new_exp = jnp.exp(new - highest)
        total = jnp.sum(cache_exp, -1, keepdims=True) + jnp.sum(new_exp, -1, keepdims=True)
        cache_w = (cache_exp / total).astype(BF)
        new_w = (new_exp / total).astype(BF)

        def mix(row):
            return lax.dot_general(
                cache_w, dense[row, :, : position.shape[1]], NT, preferred_element_type=F32
            )

        context = mix(first)
        for n in range(1, 4):
            context = jnp.where(which == n, mix(first + n), context)
        context = context + matmul(new_w, nk_s[:, :latent])
        ctx_s[span, :] = context.astype(BF)

    def meta_copy(d):
        tile = meta_v.at[fs, me]
        return remote(tile, tile, meta_sem.at[0], meta_sem.at[1], lax.rem(me + d, peers))

    def all_copies(buffer, sem):
        tiles = buffer.at[pl.ds(0, peers - 1)]
        return remote(tiles, tiles, sem.at[0], sem.at[1], me)

    for i, route in enumerate(ROUTES):
        for n in range(2):
            cache_copy(i, n).wait()
        each(route.first // 16, (route.first + route.count) // 16, attend)
        if i == 0:
            for n in range(3):
                weight_copy(n).start()

    out_copy.wait()
    for c in range(wo_v.shape[1] // 128):
        span = slice(c * 128, c * 128 + 128)
        wo_t[span, :] = wo_v[:, span].T
    gain = jnp.zeros((1, depth), F32)
    for j in range(peers):
        part = slice(j * depth, (j + 1) * depth)
        res_s[j, :, :depth] = res_ref[0, :, part].astype(F32)
        gain = jnp.where(me == j, gain_ref[:, part], gain)
    gain = jnp.concatenate([gain, jnp.zeros((1, WIDE - depth), F32)], axis=1)
    lane = lax.broadcasted_iota(jnp.int32, (1, rows), 1)
    here = lane // (STEPS * TOP) == lax.rem(me, 4)
    own_ids = jnp.where(here, spread(ids_ref[0].astype(F32), rows), 0.0)
    own_gates = jnp.where(here, spread(gates_ref[0], rows), 0.0)
    meta_v[fs, me] = jnp.concatenate([own_ids, own_gates, jnp.zeros((6, rows), F32)], axis=0)
    values = matmul(ctx_s[...], wv_ref[...]).astype(BF)
    pl.semaphore_wait(barrier, peers - 1 + groups - 1)

    def project(n):
        offsets = [offset_of(4 * n + k) for k in range(4)]
        for offset in offsets:
            j = place.plus(offset)
            span = pl.ds(pl.multiple_of(j * depth, 16), depth)
            part = lax.dot_general(wo_t[span, :], values, NT, preferred_element_type=F32)
            send_v[j] = part.astype(BF)
        for offset in offsets:
            for h in heads:
                h.send(offset)

    each(0, peers // 4, project)

    def res_copy(d):
        peer = lax.rem(me + d, peers)
        return remote(res_s.at[peer], res_r.at[me], res_sem.at[0], res_sem.at[1], peer)

    each(1, peers, lambda d: meta_copy(d).start())
    each(1, peers, lambda d: res_copy(d).start())
    res_r[me] = res_s[me]

    all_copies(meta_v.at[fs], meta_sem).wait_recv()
    for d in range(1, groups):
        group_copy(0, d, meta_v.at[fs]).start()

    for h in heads:
        each(h.route.n[2], h.route.plane, h.step)
    for h in heads:
        each(0, h.route.n[2], h.step)
    pair_lane = lax.broadcasted_iota(jnp.int32, (1, rows), 1)
    slot_c = lax.broadcasted_iota(jnp.int32, (rows, experts * block), 1)
    slot_r = lax.broadcasted_iota(jnp.int32, (experts * block, rows), 0)

    def read_meta(q):
        piece = from_group(q)

        def one(n):
            info = meta_v[piece, 4 * n]
            for i in range(1, 4):
                info = info + meta_v[piece, 4 * n + i]
            j = piece * per + n
            code = info[0:1, :].astype(jnp.int32) * block + pair_lane // TOP
            spread_s[j] = (code == slot_r).astype(F32).astype(BF)
            code = jnp.sum(jnp.where(diagonal, code, 0), 1, keepdims=True)
            part_v[j] = (code == slot_c).astype(F32).astype(BF)
            gate_s[j] = info[1:2, :]

        each(0, per, one)

    read_meta(0)
    for h in heads:
        h.turns()
    for q in range(1, groups):
        group_copy(0, q, meta_v.at[from_group(q)]).wait_recv()
        read_meta(q)
    for h in heads:
        h.add(att_t)
    all_copies(res_s, res_sem).wait_recv()

    attended = jnp.concatenate([att_t[...], jnp.zeros((WIDE - depth, tokens), F32)], axis=0).T
    own_res = jnp.concatenate([res_r[n][:, :depth] for n in range(peers)], axis=0)
    own_res = jnp.concatenate([own_res, jnp.zeros((tokens, WIDE - depth), F32)], axis=1)
    attended = attended + own_res
    att[...] = attended
    x_v[fs] = (attended * gain).astype(BF)
    for d in range(1, groups):
        group_copy(1, d, x_v.at[fs]).start()
    column = jnp.sum(attended * attended, -1, keepdims=True)
    row = jnp.sum(jnp.where(diagonal, column, 0.0), 0, keepdims=True)
    ssq_s[...] = jnp.broadcast_to(row, ssq_s.shape)

    def ssq_copy(d):
        return remote(ssq_s, ssq_r.at[d], ssq_sem.at[0], ssq_sem.at[1], lax.rem(me + d, peers))

    ssq_r[0] = ssq_s[...]
    each(1, peers, lambda d: ssq_copy(d).start())

    def multiply(first, count, x):
        def some(n):
            for e in [4 * n + k for k in range(4)]:
                spot = pl.ds(pl.multiple_of(e * block, block), block)
                gate = matmul(x, wg_v[e]).astype(BF)
                up = matmul(x, wu_v[e]).astype(BF)
                dense[first : first + count, spot, :half] = gate.reshape(count, block, half)
                dense[first : first + count, spot, half:] = up.reshape(count, block, half)

        each(0, experts // 4, some)

    def pick(i):
        found = []
        for k in range(2):
            q = (2 * i + k) // per
            n = lax.rem((2 * i + k) // NY, 2) * NY + lax.rem(place.y + 2 * i + k, NY)
            j = from_group(q) * per + n
            found.append((j, matmul(part_v[j], dense[q * per + n]).astype(BF)))
        for j, part in found:
            part_v[j] = part
        for j, _ in found:
            offset = (
                lax.rem(j // (NZ * NY) + NX - place.x, NX),
                lax.rem(lax.rem(j // NY, NZ) + NZ - place.z, NZ),
                lax.rem(lax.rem(j, NY) + NY - place.y, NY),
            )
            for s in sums:
                s.send(offset)

    def pick_group(q):
        each(q * per // 2, (q + 1) * per // 2, pick)

    def relay(q):
        p = from_group(q)
        x_off = lax.rem(p // 2 + NX - place.x, NX)
        z_low = 2 * lax.rem(p, 2)

        def z_off(i):
            return lax.rem(z_low + i + NZ - place.z, NZ)

        @pl.when(lax.rem(p, 2) == place.z // 2)
        def _():
            each(0, NY, lambda i: sums[0].step(i * NX + x_off))

        each(0, 2, lambda i: sums[1].step(x_off * NZ + z_off(i)))

        @pl.when(x_off == 0)
        def _():
            each(0, 2 * NY, lambda i: sums[2].step(z_off(i // NY) * NY + lax.rem(i, NY)))

    weight_copy(0).wait()
    weight_copy(1).wait()
    multiply(0, per, x_v[fs][:, :depth])
    pick_group(0)

    all_copies(ssq_r.at[pl.ds(1, peers - 1)], ssq_sem).wait_recv()
    sum_v[fs] = jnp.sum(ssq_r[...], axis=0)
    for d in range(1, groups):
        group_copy(2, d, sum_v.at[fs]).start()
    for q in range(1, groups):
        group_copy(1, q, x_v.at[from_group(q)]).wait_recv()
    others = [x_v[from_group(q)][:, :depth] for q in range(1, groups)]
    multiply(per, peers - per, jnp.concatenate(others, axis=0))
    pick_group(1)
    relay(0)
    pick_group(2)
    relay(1)
    pick_group(3)
    relay(2)
    relay(3)

    for s in sums:
        s.turns()
    for s in sums:
        s.add(acc)

    for d in range(1, groups):
        group_copy(2, d, sum_v.at[from_group(d)]).wait_recv()
    token = block * lax.rem(me, per) + token_r // TOP
    squares = jnp.sum(jnp.where(token == token_c, sum_v[me // per][:1, :], 0.0), 1, keepdims=True)
    scale = lax.rsqrt(squares / (depth * peers) + 1e-06)
    weight = jnp.sum(jnp.where(diagonal, gate_s[me], 0.0), 1, keepdims=True)
    gate = acc[:, :half] * scale
    up = acc[:, half:] * scale
    hid_v[me] = (gate / (1.0 + jnp.exp(-gate)) * up * weight).astype(BF)

    for g in gathers:
        g.begin()
    for g in gathers:
        for d3 in range(1, g.route.n[2]):
            g.relay_last(d3)
    for g in gathers:
        each(g.route.n[2], g.route.plane, g.relay_middle)

    def expand(n):
        offsets = [offset_of(2 * n), offset_of(2 * n + 1)]
        for offset in offsets:
            for g in gathers:
                g.arrive(offset)
        blocks = [place.minus(offset) for offset in offsets]
        full = [matmul(spread_s[j], hid_v[j]).astype(BF) for j in blocks]
        for j, rows_of in zip(blocks, full):
            spot = pl.ds(pl.multiple_of(j * block, block), block)
            dense[:, spot, :half] = rows_of.reshape(experts, block, half)

    each(0, peers // 2, expand)
    weight_copy(2).wait()

    def shares(pieces):
        spots = [pl.ds(pl.multiple_of(p * tokens, tokens), tokens) for p in pieces]

        def some(n, total):
            for k in range(4):
                e = 4 * n + k
                both = jnp.concatenate([dense[e, spot, :half] for spot in spots], axis=0)
                total = total + lax.dot_general(both, wd_v[e], NT, preferred_element_type=F32)
            return total

        start = jnp.zeros((len(pieces) * tokens, depth), F32)
        return lax.fori_loop(0, experts // 4, some, start)

    def routed_copy(d):
        peer = lax.rem(fs + d, groups)
        return pltpu.make_async_remote_copy(
            src_ref=routed_v.at[peer],
            dst_ref=routed_r.at[d],
            send_sem=g_send.at[3, d],
            recv_sem=g_recv.at[3, d],
            device_id={"fsdp": peer},
            device_id_type=MESH,
        )

    mixed = att[:, :depth]
    for pair in ((2, 3), (1, 0)):
        both = shares([lax.rem(fs + d, groups) for d in pair])
        for k, d in enumerate(pair):
            share = both[k * tokens : (k + 1) * tokens]
            if d > 0:
                routed_v[lax.rem(fs + d, groups), :, :depth] = share.astype(BF)
                routed_copy(d).start()
            else:
                mixed = mixed + share
    for d in range(1, groups):
        routed_copy(d).wait_recv()
        mixed = mixed + routed_r[d][:, :depth].astype(F32)
    for j in range(peers):
        home_s[j, :, :depth] = mixed[j * own_rows : (j + 1) * own_rows, :]

    def home_copy(d):
        peer = lax.rem(me + d, peers)
        return remote(home_s.at[peer], home_r.at[me], home_sem.at[0], home_sem.at[1], peer)

    each(1, peers, lambda d: home_copy(d).start())
    home_r[me] = home_s[me]
    for s in heads + sums + gathers:
        s.finish()
    for d in range(1, groups):
        routed_copy(d).wait_send()
        group_copy(0, d, meta_v.at[fs]).wait_send()
        group_copy(1, d, x_v.at[fs]).wait_send()
        group_copy(2, d, sum_v.at[fs]).wait_send()

    all_copies(ssq_r, ssq_sem).wait_send()
    all_copies(meta_v.at[fs], meta_sem).wait_send()
    all_copies(res_s, res_sem).wait_send()
    all_copies(home_s, home_sem).wait_recv()
    for j in range(peers):
        out_ref[0, :, j * depth : (j + 1) * depth] = home_r[j][:, :depth]
    all_copies(home_s, home_sem).wait_send()


def shards(
    residual,
    gain,
    queries,
    new_keys,
    cache,
    lengths,
    w_value,
    w_out,
    w_gate,
    w_up,
    w_down,
    expert_ids,
    gates,
):
    peers = lax.axis_size("exp")
    groups = lax.axis_size("fsdp")
    group_rows, steps, _, key = queries.shape
    tokens = group_rows * steps
    experts, depth, half = w_gate.shape
    block = tokens * groups // peers
    rows = block * TOP
    smem, dma = pl.BlockSpec(memory_space=pltpu.SMEM), pltpu.SemaphoreType.DMA
    scratch = [
        pltpu.VMEM((peers, experts * block, 2 * half), BF),
        pltpu.VMEM(w_out.shape[1:], BF),
        pltpu.VMEM((w_out.shape[2], w_out.shape[1]), BF),
        pltpu.VMEM((peers, steps, WIDE), F32),
        pltpu.VMEM((peers, steps, WIDE), F32),
        pltpu.VMEM((tokens, key), BF),
        pltpu.VMEM((tokens, key), BF),
        pltpu.VMEM((tokens, tokens), F32),
        pltpu.VMEM((tokens, w_value.shape[1]), BF),
        pltpu.VMEM((peers, depth, tokens), BF),
        pltpu.VMEM((depth, tokens), F32),
        pltpu.VMEM((tokens, WIDE), F32),
        pltpu.VMEM((8, tokens), F32),
        pltpu.VMEM((peers, 8, tokens), F32),
        pltpu.VMEM((groups, 8, tokens), F32),
        pltpu.VMEM((groups, tokens, WIDE), BF),
        pltpu.VMEM((groups, peers, 8, rows), F32),
        pltpu.VMEM(w_gate.shape, BF),
        pltpu.VMEM(w_gate.shape, BF),
        pltpu.VMEM(w_gate.shape, BF),
        pltpu.VMEM((peers, rows, 2 * half), BF),
        pltpu.VMEM((rows, 2 * half), F32),
        pltpu.VMEM((peers, rows, half), BF),
        pltpu.VMEM((peers, experts * block, rows), BF),
        pltpu.VMEM((peers, 1, rows), F32),
        pltpu.VMEM((groups, tokens, WIDE), BF),
        pltpu.VMEM((groups, tokens, WIDE), BF),
        pltpu.VMEM((peers, steps, WIDE), F32),
        pltpu.VMEM((peers, steps, WIDE), F32),
        dma((len(ROUTES), 2)),
        dma,
        dma((3,)),
        dma((2,)),
        dma((2,)),
        dma((2,)),
        dma((2,)),
        dma((4, groups)),
        dma((4, groups)),
    ]
    for route in HEAD_ROUTES:
        scratch += reduce_scratch(route, tokens)
    for route in ROUTES:
        scratch += reduce_scratch(route, 2 * half)
    for route in ROUTES:
        scratch += gather_scratch(route)
    return pl.pallas_call(
        functools.partial(layer_kernel, peers, groups),
        out_shape=jax.ShapeDtypeStruct(residual.shape, F32),
        in_specs=[smem, vmem(), vmem(), anywhere(), vmem(), anywhere()]
        + [vmem()] * 4
        + [anywhere()] * 3,
        out_specs=vmem(),
        scratch_shapes=scratch,
        compiler_params=pltpu.CompilerParams(
            collective_id=0, has_side_effects=True, vmem_limit_bytes=HIGH
        ),
        name="layer",
    )(
        lengths,
        queries[:, :, 0, :],
        new_keys,
        cache,
        w_value[0],
        w_out[0],
        residual,
        gain.reshape(1, -1),
        expert_ids,
        gates,
        w_gate,
        w_up,
        w_down,
    )


def solution(mesh):
    return jax.shard_map(
        shards,
        mesh=mesh,
        in_specs=(
            P(("fsdp", "exp"), None, None),
            P(),
            P("fsdp", None, "exp", None),
            P("fsdp", None, None),
            P("fsdp", None, None),
            P("fsdp"),
            P("exp", None, None),
            P("exp", None, None),
            P(None, "exp", "fsdp"),
            P(None, "exp", "fsdp"),
            P(None, "exp", "fsdp"),
            P(("fsdp", "exp"), None, None),
            P(("fsdp", "exp"), None, None),
        ),
        out_specs=P(("fsdp", "exp"), None, None),
        check_vma=False,
    )
```

```python
import functools

import jax
import jax.numpy as jnp
from jax import lax
from jax.experimental import pallas as pl
from jax.experimental.pallas import tpu as pltpu
from jax.sharding import PartitionSpec as P

TOP = 8
STEPS = 4
score_scale = 0.07216878364870322
MESH = pl.DeviceIdType.MESH
BF = jnp.bfloat16
F32 = jnp.float32
WIDE = 256
HIGH = 60 * 1024 * 1024
NX, NZ, NY = 2, 4, 4
NT = (((1,), (1,)), ((), ()))


def matmul(a, b):
    return jnp.dot(a, b, preferred_element_type=F32)


def vmem():
    return pl.BlockSpec(memory_space=pltpu.VMEM)


def anywhere():
    return pl.BlockSpec(memory_space=pl.ANY)


def each(lower, upper, body):
    def step(i, carry):
        body(i)
        return carry

    lax.fori_loop(lower, upper, step, 0)


class Place:
    def __init__(self):
        self.me = lax.axis_index("exp")
        self.x = self.me // (NZ * NY)
        self.z = lax.rem(self.me // NY, NZ)
        self.y = lax.rem(self.me, NY)

    def index(self, x, z, y):
        return (lax.rem(x, NX) * NZ + lax.rem(z, NZ)) * NY + lax.rem(y, NY)

    def plus(self, offset):
        dx, dz, dy = offset
        return self.index(self.x + dx, self.z + dz, self.y + dy)

    def minus(self, offset):
        dx, dz, dy = offset
        return self.index(self.x + NX - dx, self.z + NZ - dz, self.y + NY - dy)


class Route:
    def __init__(self, kind, first, count):
        self.axes = {"z": (1, 2, 0), "y": (2, 0, 1), "x": (0, 1, 2)}[kind]
        self.n = tuple((NX, NZ, NY)[a] for a in self.axes)
        self.first, self.count = first, count
        self.rows = pl.ds(first, count)
        self.plane = self.n[1] * self.n[2]

    def offset(self, d1, d2, d3):
        out = [0, 0, 0]
        for a, d in zip(self.axes, (d1, d2, d3)):
            out[a] = d
        return tuple(out)

    def split(self, offset):
        return tuple(offset[a] for a in self.axes)


ROUTES = (Route("z", 0, 32), Route("y", 32, 48), Route("x", 80, 48))
HEAD_ROUTES = (Route("z", 0, 64), Route("y", 64, 80), Route("x", 144, 80))


def remote(src, dst, send, recv, peer):
    return pltpu.make_async_remote_copy(
        src_ref=src,
        dst_ref=dst,
        send_sem=send,
        recv_sem=recv,
        device_id={"exp": peer},
        device_id_type=MESH,
    )


class Reduce:
    def __init__(self, place, route, src, bufs):
        self.place, self.route, self.src = place, route, src
        self.got1, self.out1, self.got2, self.keep, self.out2, self.got3 = bufs[:6]
        self.sent, self.r1, self.r2 = bufs[6:]

    def first(self, d1, d2, d3):
        route = self.route
        g = d2 * route.n[2] + d3
        return remote(
            self.src.at[self.place.plus(route.offset(d1, d2, d3)), route.rows],
            self.got1.at[g, d1 - 1],
            self.sent.at[0],
            self.r1.at[g],
            self.place.plus(route.offset(d1, 0, 0)),
        )

    def second(self, d2, d3):
        return remote(
            self.out1.at[d2 * self.route.n[2] + d3],
            self.got2.at[d3, d2 - 1],
            self.sent.at[1],
            self.r2.at[d3],
            self.place.plus(self.route.offset(0, d2, 0)),
        )

    def third(self, d3):
        return remote(
            self.out2.at[d3],
            self.got3.at[d3 - 1],
            self.sent.at[2],
            self.r2.at[self.route.n[2]],
            self.place.plus(self.route.offset(0, 0, d3)),
        )

    def send(self, offset):
        d1, d2, d3 = self.route.split(offset)

        @pl.when(d1 > 0)
        def _():
            self.first(d1, d2, d3).start()

    def arrived(self, got, sem):
        remote(got, got, self.sent.at[0], sem, self.place.me).wait_recv()

    def step(self, g):
        route = self.route
        d2, d3 = g // route.n[2], lax.rem(g, route.n[2])
        self.arrived(self.got1.at[g], self.r1.at[g])
        total = self.src[self.place.plus(route.offset(0, d2, d3)), route.rows].astype(F32)
        for d in range(1, route.n[0]):
            total = total + self.got1[g, d - 1].astype(F32)

        @pl.when(d2 == 0)
        def _():
            self.keep[d3] = total

        @pl.when(d2 != 0)
        def _():
            self.out1[g] = total.astype(BF)
            self.second(d2, d3).start()

    def turn(self, d3):
        self.arrived(self.got2.at[d3], self.r2.at[d3])
        total = self.keep[d3]
        for d in range(1, self.route.n[1]):
            total = total + self.got2[d3, d - 1].astype(F32)
        return total

    def turns(self):
        for d3 in range(1, self.route.n[2]):
            self.out2[d3] = self.turn(d3).astype(BF)
            self.third(d3).start()
        self.keep[0] = self.turn(0)

    def add(self, acc_ref):
        self.arrived(self.got3, self.r2.at[self.route.n[2]])
        total = self.keep[0]
        for d in range(1, self.route.n[2]):
            total = total + self.got3[d - 1].astype(F32)
        acc_ref[self.route.rows] = total

    def finish(self):
        for n, got in enumerate((self.got1, self.got2, self.got3)):
            remote(got, got, self.sent.at[n], self.r2.at[0], self.place.me).wait_send()


def reduce_scratch(route, cols):
    n1, n2, n3 = route.n
    dma = pltpu.SemaphoreType.DMA
    return [
        pltpu.VMEM((n2 * n3, n1 - 1, route.count, cols), BF),
        pltpu.VMEM((n2 * n3, route.count, cols), BF),
        pltpu.VMEM((n3, n2 - 1, route.count, cols), BF),
        pltpu.VMEM((n3, route.count, cols), F32),
        pltpu.VMEM((n3, route.count, cols), BF),
        pltpu.VMEM((n3 - 1, route.count, cols), BF),
        dma((3,)),
        dma((n2 * n3,)),
        dma((n3 + 1,)),
    ]


class Gather:
    def __init__(self, place, route, whole, bufs):
        self.place, self.route, self.whole = place, route, whole
        self.sent, self.r = bufs

    def copy(self, source, to, offset):
        _, n2, n3 = self.route.n
        d1, d2, d3 = offset
        block = self.whole.at[source, self.route.rows]
        peer = self.place.plus(self.route.offset(*to))
        return remote(block, block, self.sent, self.r.at[(d1 * n2 + d2) * n3 + d3], peer)

    def source(self, *offset):
        return self.place.minus(self.route.offset(*offset))

    def push1(self, d2, d3):
        for d in range(1, self.route.n[0]):
            self.copy(self.source(0, d2, d3), (d, 0, 0), (d, d2, d3)).start()

    def push2(self, d3):
        for d in range(1, self.route.n[1]):
            self.copy(self.source(0, 0, d3), (0, d, 0), (0, d, d3)).start()

    def begin(self):
        for d in range(1, self.route.n[2]):
            self.copy(self.place.me, (0, 0, d), (0, 0, d)).start()
        self.push2(0)
        self.push1(0, 0)

    def wait(self, offset):
        self.copy(self.source(*offset), (0, 0, 0), offset).wait_recv()

    def relay_last(self, d3):
        self.wait((0, 0, d3))
        self.push2(d3)
        self.push1(0, d3)

    def relay_middle(self, g):
        d2, d3 = g // self.route.n[2], lax.rem(g, self.route.n[2])
        self.wait((0, d2, d3))
        self.push1(d2, d3)

    def arrive(self, offset):
        split = self.route.split(offset)

        @pl.when(split[0] > 0)
        def _():
            self.wait(split)

    def finish(self):
        n1, n2, n3 = self.route.n
        blocks = self.whole.at[pl.ds(0, n1 * n2 * n3 - 1), self.route.rows]
        remote(blocks, blocks, self.sent, self.r.at[0], self.place.me).wait_send()


def gather_scratch(route):
    dma = pltpu.SemaphoreType.DMA
    return [dma, dma((route.n[0] * route.n[1] * route.n[2],))]


def offset_of(o):
    return (o // (NZ * NY), lax.rem(o // NY, NZ), lax.rem(o, NY))


def spread(block, lanes):
    wide = jnp.concatenate([block] * (lanes // block.shape[1]), axis=1)
    step = lax.rem(lax.broadcasted_iota(jnp.int32, wide.shape, 1) // TOP, STEPS)
    row = lax.broadcasted_iota(jnp.int32, wide.shape, 0)
    return jnp.sum(jnp.where(step == row, wide, 0.0), 0, keepdims=True)


def layer_kernel(peers, groups, *refs):
    (
        len_ref,
        q_ref,
        nk_ref,
        cache_ref,
        wv_ref,
        wo_ref,
        res_ref,
        gain_ref,
        ids_ref,
        gates_ref,
        wg_ref,
        wu_ref,
        wd_ref,
        out_ref,
        dense,
        wo_v,
        wo_t,
        res_s,
        res_r,
        q_s,
        nk_s,
        new_s,
        ctx_s,
        send_v,
        att_t,
        att,
        ssq_s,
        ssq_r,
        sum_v,
        x_v,
        meta_v,
        wg_v,
        wu_v,
        wd_v,
        part_v,
        acc,
        hid_v,
        spread_s,
        gate_s,
        routed_v,
        routed_r,
        home_s,
        home_r,
        cache_sem,
        wo_sem,
        w_sem,
        ssq_sem,
        meta_sem,
        res_sem,
        home_sem,
        g_send,
        g_recv,
    ) = refs[:52]
    place = Place()
    me = place.me
    fs = lax.axis_index("fsdp")
    tokens = q_s.shape[0]
    latent = wv_ref.shape[0]
    experts, depth, half = wg_ref.shape
    rows = part_v.shape[1]
    block = rows // TOP
    per = peers // groups
    own_rows = home_s.shape[1]
    barrier = pltpu.get_barrier_semaphore()

    def greet(axis, mine, size):
        def one(d):
            pl.semaphore_signal(
                barrier, inc=1, device_id={axis: lax.rem(mine + d, size)}, device_id_type=MESH
            )

        each(1, size, one)

    greet("exp", me, peers)
    greet("fsdp", fs, groups)
    rest = refs[52:]
    heads = [
        Reduce(place, r, send_v, rest[9 * i : 9 * i + 9]) for i, r in enumerate(HEAD_ROUTES)
    ]
    rest = rest[9 * len(ROUTES) :]
    sums = [Reduce(place, r, part_v, rest[9 * i : 9 * i + 9]) for i, r in enumerate(ROUTES)]
    rest = rest[9 * len(ROUTES) :]
    gathers = [Gather(place, r, hid_v, rest[2 * i : 2 * i + 2]) for i, r in enumerate(ROUTES)]

    def group_copy(n, d, block_ref):
        return pltpu.make_async_remote_copy(
            src_ref=block_ref,
            dst_ref=block_ref,
            send_sem=g_send.at[n, d],
            recv_sem=g_recv.at[n, d],
            device_id={"fsdp": lax.rem(fs + d, groups)},
            device_id_type=MESH,
        )

    def from_group(d):
        return lax.rem(fs + groups - d, groups)

    def cache_copy(i, n):
        span = pl.ds(ROUTES[i].first // STEPS, ROUTES[i].count // STEPS)
        positions = cache_ref.shape[2]
        if n == 0:
            src = cache_ref.at[span, pl.ds(0, latent)]
            dst = dense.at[span, pl.ds(0, latent), pl.ds(0, positions)]
        else:
            left = cache_ref.shape[1] - latent
            src = cache_ref.at[span, pl.ds(latent, left)]
            dst = dense.at[span, pl.ds(0, left), pl.ds(positions, positions)]
        return pltpu.make_async_copy(src, dst, cache_sem.at[i, n])

    def weight_copy(n):
        src = (wg_ref, wu_ref, wd_ref)[n]
        dst = (wg_v, wu_v, wd_v)[n]
        return pltpu.make_async_copy(src, dst, w_sem.at[n])

    out_copy = pltpu.make_async_copy(wo_ref, wo_v, wo_sem)
    for n in range(2):
        cache_copy(0, n).start()
    out_copy.start()
    for i in range(1, len(ROUTES)):
        for n in range(2):
            cache_copy(i, n).start()

    for b in range(tokens // 16):
        span = slice(b * 16, b * 16 + 16)
        q_s[span, :] = jnp.concatenate(
            [q_ref[4 * b + i].astype(F32) for i in range(4)], axis=0
        ).astype(BF)
        nk_s[span, :] = jnp.concatenate(
            [nk_ref[4 * b + i].astype(F32) for i in range(4)], axis=0
        ).astype(BF)

    token_r = lax.broadcasted_iota(jnp.int32, (tokens, tokens), 0)
    token_c = lax.broadcasted_iota(jnp.int32, (tokens, tokens), 1)
    diagonal = token_r == token_c
    same = (token_r // STEPS == token_c // STEPS) & (token_c <= token_r)
    fresh = lax.dot_general(q_s[...], nk_s[...], NT, preferred_element_type=F32)
    new_s[...] = jnp.where(same, fresh * score_scale, -1e30)

    which = lax.broadcasted_iota(jnp.int32, (16, 1), 0) // STEPS
    position = lax.broadcasted_iota(jnp.int32, (16, cache_ref.shape[2]), 1)
    rope = cache_ref.shape[1] - latent

    def attend(b):
        span = pl.ds(pl.multiple_of(b * 16, 16), 16)
        first = b * 4
        q16 = q_s[span, :]

        def score(row):
            return matmul(q16[:, :latent], dense[row, :, : position.shape[1]]) + matmul(
                q16[:, latent:], dense[row, :rope, position.shape[1] :]
            )

        scores = score(first)
        length = jnp.full(position.shape, len_ref[first])
        for n in range(1, 4):
            scores = jnp.where(which == n, score(first + n), scores)
            length = jnp.where(which == n, len_ref[first + n], length)
        scores = jnp.where(position < length, scores * score_scale, -1e30)
        new = new_s[span, :]
        highest = jnp.maximum(jnp.max(scores, -1, keepdims=True), jnp.max(new, -1, keepdims=True))
        cache_exp = jnp.exp(scores - highest)
        new_exp = jnp.exp(new - highest)
        total = jnp.sum(cache_exp, -1, keepdims=True) + jnp.sum(new_exp, -1, keepdims=True)
        cache_w = (cache_exp / total).astype(BF)
        new_w = (new_exp / total).astype(BF)

        def mix(row):
            return lax.dot_general(
                cache_w, dense[row, :, : position.shape[1]], NT, preferred_element_type=F32
            )

        context = mix(first)
        for n in range(1, 4):
            context = jnp.where(which == n, mix(first + n), context)
        context = context + matmul(new_w, nk_s[:, :latent])
        ctx_s[span, :] = context.astype(BF)

    def meta_copy(d):
        tile = meta_v.at[fs, me]
        return remote(tile, tile, meta_sem.at[0], meta_sem.at[1], lax.rem(me + d, peers))

    def all_copies(buffer, sem):
        tiles = buffer.at[pl.ds(0, peers - 1)]
        return remote(tiles, tiles, sem.at[0], sem.at[1], me)

    for i, route in enumerate(ROUTES):
        for n in range(2):
            cache_copy(i, n).wait()
        each(route.first // 16, (route.first + route.count) // 16, attend)
        if i == 0:
            for n in range(3):
                weight_copy(n).start()

    out_copy.wait()
    for c in range(wo_v.shape[1] // 128):
        span = slice(c * 128, c * 128 + 128)
        wo_t[span, :] = wo_v[:, span].T
    gain = jnp.zeros((1, depth), F32)
    for j in range(peers):
        part = slice(j * depth, (j + 1) * depth)
        res_s[j, :, :depth] = res_ref[0, :, part].astype(F32)
        gain = jnp.where(me == j, gain_ref[:, part], gain)
    gain = jnp.concatenate([gain, jnp.zeros((1, WIDE - depth), F32)], axis=1)
    lane = lax.broadcasted_iota(jnp.int32, (1, rows), 1)
    here = lane // (STEPS * TOP) == lax.rem(me, 4)
    own_ids = jnp.where(here, spread(ids_ref[0].astype(F32), rows), 0.0)
    own_gates = jnp.where(here, spread(gates_ref[0], rows), 0.0)
    meta_v[fs, me] = jnp.concatenate([own_ids, own_gates, jnp.zeros((6, rows), F32)], axis=0)
    values = matmul(ctx_s[...], wv_ref[...]).astype(BF)
    pl.semaphore_wait(barrier, peers - 1 + groups - 1)

    def project(n):
        offsets = [offset_of(4 * n + k) for k in range(4)]
        for offset in offsets:
            j = place.plus(offset)
            span = pl.ds(pl.multiple_of(j * depth, 16), depth)
            part = lax.dot_general(wo_t[span, :], values, NT, preferred_element_type=F32)
            send_v[j] = part.astype(BF)
        for offset in offsets:
            for h in heads:
                h.send(offset)

    each(0, peers // 4, project)

    def res_copy(d):
        peer = lax.rem(me + d, peers)
        return remote(res_s.at[peer], res_r.at[me], res_sem.at[0], res_sem.at[1], peer)

    each(1, peers, lambda d: meta_copy(d).start())
    each(1, peers, lambda d: res_copy(d).start())
    res_r[me] = res_s[me]

    for h in heads:
        each(h.route.n[2], h.route.plane, h.step)
    for h in heads:
        each(0, h.route.n[2], h.step)
    pair_lane = lax.broadcasted_iota(jnp.int32, (1, rows), 1)
    slot_c = lax.broadcasted_iota(jnp.int32, (rows, experts * block), 1)
    slot_r = lax.broadcasted_iota(jnp.int32, (experts * block, rows), 0)

    def read_meta(q):
        piece = from_group(q)

        def one(n):
            info = meta_v[piece, 4 * n]
            for i in range(1, 4):
                info = info + meta_v[piece, 4 * n + i]
            j = piece * per + n
            code = info[0:1, :].astype(jnp.int32) * block + pair_lane // TOP
            spread_s[j] = (code == slot_r).astype(F32).astype(BF)
            code = jnp.sum(jnp.where(diagonal, code, 0), 1, keepdims=True)
            part_v[j] = (code == slot_c).astype(F32).astype(BF)
            gate_s[j] = info[1:2, :]

        each(0, per, one)

    for h in heads:
        h.turns()
    all_copies(meta_v.at[fs], meta_sem).wait_recv()
    for d in range(1, groups):
        group_copy(0, d, meta_v.at[fs]).start()
    read_meta(0)
    for h in heads:
        h.add(att_t)
    all_copies(res_s, res_sem).wait_recv()

    attended = jnp.concatenate([att_t[...], jnp.zeros((WIDE - depth, tokens), F32)], axis=0).T
    own_res = jnp.concatenate([res_r[n][:, :depth] for n in range(peers)], axis=0)
    own_res = jnp.concatenate([own_res, jnp.zeros((tokens, WIDE - depth), F32)], axis=1)
    attended = attended + own_res
    att[...] = attended
    x_v[fs] = (attended * gain).astype(BF)
    for d in range(1, groups):
        group_copy(1, d, x_v.at[fs]).start()
    column = jnp.sum(attended * attended, -1, keepdims=True)
    row = jnp.sum(jnp.where(diagonal, column, 0.0), 0, keepdims=True)
    ssq_s[...] = jnp.broadcast_to(row, ssq_s.shape)

    def ssq_copy(d):
        return remote(ssq_s, ssq_r.at[d], ssq_sem.at[0], ssq_sem.at[1], lax.rem(me + d, peers))

    ssq_r[0] = ssq_s[...]
    each(1, peers, lambda d: ssq_copy(d).start())

    def multiply(first, count, x):
        def some(n):
            for e in [4 * n + k for k in range(4)]:
                spot = pl.ds(pl.multiple_of(e * block, block), block)
                gate = matmul(x, wg_v[e]).astype(BF)
                up = matmul(x, wu_v[e]).astype(BF)
                dense[first : first + count, spot, :half] = gate.reshape(count, block, half)
                dense[first : first + count, spot, half:] = up.reshape(count, block, half)

        each(0, experts // 4, some)

    def pick(i):
        found = []
        for k in range(2):
            q = (2 * i + k) // per
            n = lax.rem((2 * i + k) // NY, 2) * NY + lax.rem(place.y + 2 * i + k, NY)
            j = from_group(q) * per + n
            found.append((j, matmul(part_v[j], dense[q * per + n]).astype(BF)))
        for j, part in found:
            part_v[j] = part
        for j, _ in found:
            offset = (
                lax.rem(j // (NZ * NY) + NX - place.x, NX),
                lax.rem(lax.rem(j // NY, NZ) + NZ - place.z, NZ),
                lax.rem(lax.rem(j, NY) + NY - place.y, NY),
            )
            for s in sums:
                s.send(offset)

    def pick_group(q):
        each(q * per // 2, (q + 1) * per // 2, pick)

    def relay(q):
        p = from_group(q)
        x_off = lax.rem(p // 2 + NX - place.x, NX)
        z_low = 2 * lax.rem(p, 2)

        def z_off(i):
            return lax.rem(z_low + i + NZ - place.z, NZ)

        @pl.when(lax.rem(p, 2) == place.z // 2)
        def _():
            each(0, NY, lambda i: sums[0].step(i * NX + x_off))

        each(0, 2, lambda i: sums[1].step(x_off * NZ + z_off(i)))

        @pl.when(x_off == 0)
        def _():
            each(0, 2 * NY, lambda i: sums[2].step(z_off(i // NY) * NY + lax.rem(i, NY)))

    weight_copy(0).wait()
    weight_copy(1).wait()
    multiply(0, per, x_v[fs][:, :depth])
    pick_group(0)

    for q in range(1, groups):
        group_copy(0, q, meta_v.at[from_group(q)]).wait_recv()
        group_copy(1, q, x_v.at[from_group(q)]).wait_recv()
        read_meta(q)
    others = [x_v[from_group(q)][:, :depth] for q in range(1, groups)]
    multiply(per, peers - per, jnp.concatenate(others, axis=0))
    pick_group(1)
    relay(0)
    pick_group(2)
    relay(1)
    pick_group(3)
    all_copies(ssq_r.at[pl.ds(1, peers - 1)], ssq_sem).wait_recv()
    sum_v[fs] = jnp.sum(ssq_r[...], axis=0)
    for d in range(1, groups):
        group_copy(2, d, sum_v.at[fs]).start()
    relay(2)
    relay(3)

    for s in sums:
        s.turns()
    for s in sums:
        s.add(acc)

    for d in range(1, groups):
        group_copy(2, d, sum_v.at[from_group(d)]).wait_recv()
    token = block * lax.rem(me, per) + token_r // TOP
    squares = jnp.sum(jnp.where(token == token_c, sum_v[me // per][:1, :], 0.0), 1, keepdims=True)
    scale = lax.rsqrt(squares / (depth * peers) + 1e-06)
    weight = jnp.sum(jnp.where(diagonal, gate_s[me], 0.0), 1, keepdims=True)
    gate = acc[:, :half] * scale
    up = acc[:, half:] * scale
    hid_v[me] = (gate / (1.0 + jnp.exp(-gate)) * up * weight).astype(BF)

    for g in gathers:
        g.begin()
    for g in gathers:
        for d3 in range(1, g.route.n[2]):
            g.relay_last(d3)
    for g in gathers:
        each(g.route.n[2], g.route.plane, g.relay_middle)

    def expand(n):
        offsets = [offset_of(2 * n), offset_of(2 * n + 1)]
        for offset in offsets:
            for g in gathers:
                g.arrive(offset)
        blocks = [place.minus(offset) for offset in offsets]
        full = [matmul(spread_s[j], hid_v[j]).astype(BF) for j in blocks]
        for j, rows_of in zip(blocks, full):
            spot = pl.ds(pl.multiple_of(j * block, block), block)
            dense[:, spot, :half] = rows_of.reshape(experts, block, half)

    each(0, peers // 2, expand)
    weight_copy(2).wait()

    def shares(pieces):
        spots = [pl.ds(pl.multiple_of(p * tokens, tokens), tokens) for p in pieces]

        def some(n, total):
            for k in range(4):
                e = 4 * n + k
                both = jnp.concatenate([dense[e, spot, :half] for spot in spots], axis=0)
                total = total + lax.dot_general(both, wd_v[e], NT, preferred_element_type=F32)
            return total

        start = jnp.zeros((len(pieces) * tokens, depth), F32)
        return lax.fori_loop(0, experts // 4, some, start)

    def routed_copy(d):
        peer = lax.rem(fs + d, groups)
        return pltpu.make_async_remote_copy(
            src_ref=routed_v.at[peer],
            dst_ref=routed_r.at[d],
            send_sem=g_send.at[3, d],
            recv_sem=g_recv.at[3, d],
            device_id={"fsdp": peer},
            device_id_type=MESH,
        )

    mixed = att[:, :depth]
    for pair in ((2, 3), (1, 0)):
        both = shares([lax.rem(fs + d, groups) for d in pair])
        for k, d in enumerate(pair):
            share = both[k * tokens : (k + 1) * tokens]
            if d > 0:
                routed_v[lax.rem(fs + d, groups), :, :depth] = share.astype(BF)
                routed_copy(d).start()
            else:
                mixed = mixed + share
    for d in range(1, groups):
        routed_copy(d).wait_recv()
        mixed = mixed + routed_r[d][:, :depth].astype(F32)
    for j in range(peers):
        home_s[j, :, :depth] = mixed[j * own_rows : (j + 1) * own_rows, :]

    def home_copy(d):
        peer = lax.rem(me + d, peers)
        return remote(home_s.at[peer], home_r.at[me], home_sem.at[0], home_sem.at[1], peer)

    each(1, peers, lambda d: home_copy(d).start())
    home_r[me] = home_s[me]
    for s in heads + sums + gathers:
        s.finish()
    for d in range(1, groups):
        routed_copy(d).wait_send()
        group_copy(0, d, meta_v.at[fs]).wait_send()
        group_copy(1, d, x_v.at[fs]).wait_send()
        group_copy(2, d, sum_v.at[fs]).wait_send()

    all_copies(ssq_r, ssq_sem).wait_send()
    all_copies(meta_v.at[fs], meta_sem).wait_send()
    all_copies(res_s, res_sem).wait_send()
    all_copies(home_s, home_sem).wait_recv()
    for j in range(peers):
        out_ref[0, :, j * depth : (j + 1) * depth] = home_r[j][:, :depth]
    all_copies(home_s, home_sem).wait_send()


def shards(
    residual,
    gain,
    queries,
    new_keys,
    cache,
    lengths,
    w_value,
    w_out,
    w_gate,
    w_up,
    w_down,
    expert_ids,
    gates,
):
    peers = lax.axis_size("exp")
    groups = lax.axis_size("fsdp")
    group_rows, steps, _, key = queries.shape
    tokens = group_rows * steps
    experts, depth, half = w_gate.shape
    block = tokens * groups // peers
    rows = block * TOP
    smem, dma = pl.BlockSpec(memory_space=pltpu.SMEM), pltpu.SemaphoreType.DMA
    scratch = [
        pltpu.VMEM((peers, experts * block, 2 * half), BF),
        pltpu.VMEM(w_out.shape[1:], BF),
        pltpu.VMEM((w_out.shape[2], w_out.shape[1]), BF),
        pltpu.VMEM((peers, steps, WIDE), F32),
        pltpu.VMEM((peers, steps, WIDE), F32),
        pltpu.VMEM((tokens, key), BF),
        pltpu.VMEM((tokens, key), BF),
        pltpu.VMEM((tokens, tokens), F32),
        pltpu.VMEM((tokens, w_value.shape[1]), BF),
        pltpu.VMEM((peers, depth, tokens), BF),
        pltpu.VMEM((depth, tokens), F32),
        pltpu.VMEM((tokens, WIDE), F32),
        pltpu.VMEM((8, tokens), F32),
        pltpu.VMEM((peers, 8, tokens), F32),
        pltpu.VMEM((groups, 8, tokens), F32),
        pltpu.VMEM((groups, tokens, WIDE), BF),
        pltpu.VMEM((groups, peers, 8, rows), F32),
        pltpu.VMEM(w_gate.shape, BF),
        pltpu.VMEM(w_gate.shape, BF),
        pltpu.VMEM(w_gate.shape, BF),
        pltpu.VMEM((peers, rows, 2 * half), BF),
        pltpu.VMEM((rows, 2 * half), F32),
        pltpu.VMEM((peers, rows, half), BF),
        pltpu.VMEM((peers, experts * block, rows), BF),
        pltpu.VMEM((peers, 1, rows), F32),
        pltpu.VMEM((groups, tokens, WIDE), BF),
        pltpu.VMEM((groups, tokens, WIDE), BF),
        pltpu.VMEM((peers, steps, WIDE), F32),
        pltpu.VMEM((peers, steps, WIDE), F32),
        dma((len(ROUTES), 2)),
        dma,
        dma((3,)),
        dma((2,)),
        dma((2,)),
        dma((2,)),
        dma((2,)),
        dma((4, groups)),
        dma((4, groups)),
    ]
    for route in HEAD_ROUTES:
        scratch += reduce_scratch(route, tokens)
    for route in ROUTES:
        scratch += reduce_scratch(route, 2 * half)
    for route in ROUTES:
        scratch += gather_scratch(route)
    return pl.pallas_call(
        functools.partial(layer_kernel, peers, groups),
        out_shape=jax.ShapeDtypeStruct(residual.shape, F32),
        in_specs=[smem, vmem(), vmem(), anywhere(), vmem(), anywhere()]
        + [vmem()] * 4
        + [anywhere()] * 3,
        out_specs=vmem(),
        scratch_shapes=scratch,
        compiler_params=pltpu.CompilerParams(
            collective_id=0, has_side_effects=True, vmem_limit_bytes=HIGH
        ),
        name="layer",
    )(
        lengths,
        queries[:, :, 0, :],
        new_keys,
        cache,
        w_value[0],
        w_out[0],
        residual,
        gain.reshape(1, -1),
        expert_ids,
        gates,
        w_gate,
        w_up,
        w_down,
    )


def solution(mesh):
    return jax.shard_map(
        shards,
        mesh=mesh,
        in_specs=(
            P(("fsdp", "exp"), None, None),
            P(),
            P("fsdp", None, "exp", None),
            P("fsdp", None, None),
            P("fsdp", None, None),
            P("fsdp"),
            P("exp", None, None),
            P("exp", None, None),
            P(None, "exp", "fsdp"),
            P(None, "exp", "fsdp"),
            P(None, "exp", "fsdp"),
            P(("fsdp", "exp"), None, None),
            P(("fsdp", "exp"), None, None),
        ),
        out_specs=P(("fsdp", "exp"), None, None),
        check_vma=False,
    )
```

```python
import functools

import jax
import jax.numpy as jnp
from jax import lax
from jax.experimental import pallas as pl
from jax.experimental.pallas import tpu as pltpu
from jax.sharding import PartitionSpec as P

TOP = 8
STEPS = 4
score_scale = 0.07216878364870322
MESH = pl.DeviceIdType.MESH
BF = jnp.bfloat16
F32 = jnp.float32
WIDE = 256
HIGH = 60 * 1024 * 1024
NX, NZ, NY = 2, 4, 4
NT = (((1,), (1,)), ((), ()))


def matmul(a, b):
    return jnp.dot(a, b, preferred_element_type=F32)


def vmem():
    return pl.BlockSpec(memory_space=pltpu.VMEM)


def anywhere():
    return pl.BlockSpec(memory_space=pl.ANY)


def each(lower, upper, body):
    def step(i, carry):
        body(i)
        return carry

    lax.fori_loop(lower, upper, step, 0)


class Place:
    def __init__(self):
        self.me = lax.axis_index("exp")
        self.x = self.me // (NZ * NY)
        self.z = lax.rem(self.me // NY, NZ)
        self.y = lax.rem(self.me, NY)

    def index(self, x, z, y):
        return (lax.rem(x, NX) * NZ + lax.rem(z, NZ)) * NY + lax.rem(y, NY)

    def plus(self, offset):
        dx, dz, dy = offset
        return self.index(self.x + dx, self.z + dz, self.y + dy)

    def minus(self, offset):
        dx, dz, dy = offset
        return self.index(self.x + NX - dx, self.z + NZ - dz, self.y + NY - dy)


class Route:
    def __init__(self, kind, first, count):
        self.axes = {"z": (1, 2, 0), "y": (2, 0, 1), "x": (0, 1, 2)}[kind]
        self.n = tuple((NX, NZ, NY)[a] for a in self.axes)
        self.first, self.count = first, count
        self.rows = pl.ds(first, count)
        self.plane = self.n[1] * self.n[2]

    def offset(self, d1, d2, d3):
        out = [0, 0, 0]
        for a, d in zip(self.axes, (d1, d2, d3)):
            out[a] = d
        return tuple(out)

    def split(self, offset):
        return tuple(offset[a] for a in self.axes)


ROUTES = (Route("z", 0, 32), Route("y", 32, 48), Route("x", 80, 48))
HEAD_ROUTES = (Route("z", 0, 64), Route("y", 64, 80), Route("x", 144, 80))


def remote(src, dst, send, recv, peer):
    return pltpu.make_async_remote_copy(
        src_ref=src,
        dst_ref=dst,
        send_sem=send,
        recv_sem=recv,
        device_id={"exp": peer},
        device_id_type=MESH,
    )


class Reduce:
    def __init__(self, place, route, src, bufs):
        self.place, self.route, self.src = place, route, src
        self.got1, self.out1, self.got2, self.keep, self.out2, self.got3 = bufs[:6]
        self.sent, self.r1, self.r2 = bufs[6:]

    def first(self, d1, d2, d3):
        route = self.route
        g = d2 * route.n[2] + d3
        return remote(
            self.src.at[self.place.plus(route.offset(d1, d2, d3)), route.rows],
            self.got1.at[g, d1 - 1],
            self.sent.at[0],
            self.r1.at[g],
            self.place.plus(route.offset(d1, 0, 0)),
        )

    def second(self, d2, d3):
        return remote(
            self.out1.at[d2 * self.route.n[2] + d3],
            self.got2.at[d3, d2 - 1],
            self.sent.at[1],
            self.r2.at[d3],
            self.place.plus(self.route.offset(0, d2, 0)),
        )

    def third(self, d3):
        return remote(
            self.out2.at[d3],
            self.got3.at[d3 - 1],
            self.sent.at[2],
            self.r2.at[self.route.n[2]],
            self.place.plus(self.route.offset(0, 0, d3)),
        )

    def send(self, offset):
        d1, d2, d3 = self.route.split(offset)

        @pl.when(d1 > 0)
        def _():
            self.first(d1, d2, d3).start()

    def arrived(self, got, sem):
        remote(got, got, self.sent.at[0], sem, self.place.me).wait_recv()

    def step(self, g):
        route = self.route
        d2, d3 = g // route.n[2], lax.rem(g, route.n[2])
        self.arrived(self.got1.at[g], self.r1.at[g])
        total = self.src[self.place.plus(route.offset(0, d2, d3)), route.rows].astype(F32)
        for d in range(1, route.n[0]):
            total = total + self.got1[g, d - 1].astype(F32)

        @pl.when(d2 == 0)
        def _():
            self.keep[d3] = total

        @pl.when(d2 != 0)
        def _():
            self.out1[g] = total.astype(BF)
            self.second(d2, d3).start()

    def turn(self, d3):
        self.arrived(self.got2.at[d3], self.r2.at[d3])
        total = self.keep[d3]
        for d in range(1, self.route.n[1]):
            total = total + self.got2[d3, d - 1].astype(F32)
        return total

    def turns(self):
        for d3 in range(1, self.route.n[2]):
            self.out2[d3] = self.turn(d3).astype(BF)
            self.third(d3).start()
        self.keep[0] = self.turn(0)

    def add(self, acc_ref):
        self.arrived(self.got3, self.r2.at[self.route.n[2]])
        total = self.keep[0]
        for d in range(1, self.route.n[2]):
            total = total + self.got3[d - 1].astype(F32)
        acc_ref[self.route.rows] = total

    def finish(self):
        for n, got in enumerate((self.got1, self.got2, self.got3)):
            remote(got, got, self.sent.at[n], self.r2.at[0], self.place.me).wait_send()


def reduce_scratch(route, cols):
    n1, n2, n3 = route.n
    dma = pltpu.SemaphoreType.DMA
    return [
        pltpu.VMEM((n2 * n3, n1 - 1, route.count, cols), BF),
        pltpu.VMEM((n2 * n3, route.count, cols), BF),
        pltpu.VMEM((n3, n2 - 1, route.count, cols), BF),
        pltpu.VMEM((n3, route.count, cols), F32),
        pltpu.VMEM((n3, route.count, cols), BF),
        pltpu.VMEM((n3 - 1, route.count, cols), BF),
        dma((3,)),
        dma((n2 * n3,)),
        dma((n3 + 1,)),
    ]


class Gather:
    def __init__(self, place, route, whole, bufs):
        self.place, self.route, self.whole = place, route, whole
        self.sent, self.r = bufs

    def copy(self, source, to, offset):
        _, n2, n3 = self.route.n
        d1, d2, d3 = offset
        block = self.whole.at[source, self.route.rows]
        peer = self.place.plus(self.route.offset(*to))
        return remote(block, block, self.sent, self.r.at[(d1 * n2 + d2) * n3 + d3], peer)

    def source(self, *offset):
        return self.place.minus(self.route.offset(*offset))

    def push1(self, d2, d3):
        for d in sorted(range(1, self.route.n[0]), key=lambda d: d != 2):
            self.copy(self.source(0, d2, d3), (d, 0, 0), (d, d2, d3)).start()

    def push2(self, d3):
        for d in range(1, self.route.n[1]):
            self.copy(self.source(0, 0, d3), (0, d, 0), (0, d, d3)).start()

    def begin(self):
        for d in range(1, self.route.n[2]):
            self.copy(self.place.me, (0, 0, d), (0, 0, d)).start()
        self.push2(0)
        self.push1(0, 0)

    def wait(self, offset):
        self.copy(self.source(*offset), (0, 0, 0), offset).wait_recv()

    def relay_last(self, d3):
        self.wait((0, 0, d3))
        self.push2(d3)
        self.push1(0, d3)

    def relay_middle(self, g):
        d2, d3 = g // self.route.n[2], lax.rem(g, self.route.n[2])
        self.wait((0, d2, d3))
        self.push1(d2, d3)

    def arrive(self, offset):
        split = self.route.split(offset)

        @pl.when(split[0] > 0)
        def _():
            self.wait(split)

    def finish(self):
        n1, n2, n3 = self.route.n
        blocks = self.whole.at[pl.ds(0, n1 * n2 * n3 - 1), self.route.rows]
        remote(blocks, blocks, self.sent, self.r.at[0], self.place.me).wait_send()


def gather_scratch(route):
    dma = pltpu.SemaphoreType.DMA
    return [dma, dma((route.n[0] * route.n[1] * route.n[2],))]


def offset_of_int(o):
    return (o // (NZ * NY), o // NY % NZ, o % NY)


def offset_of(o):
    return (o // (NZ * NY), lax.rem(o // NY, NZ), lax.rem(o, NY))


def hops(offset):
    dx, dz, dy = offset
    return 2 * dx + min(dz, NZ - dz) + min(dy, NY - dy)


FAR_FIRST = sorted((offset_of_int(o) for o in range(1, NX * NZ * NY)), key=hops, reverse=True)


def spread(block, lanes):
    wide = jnp.concatenate([block] * (lanes // block.shape[1]), axis=1)
    step = lax.rem(lax.broadcasted_iota(jnp.int32, wide.shape, 1) // TOP, STEPS)
    row = lax.broadcasted_iota(jnp.int32, wide.shape, 0)
    return jnp.sum(jnp.where(step == row, wide, 0.0), 0, keepdims=True)


def layer_kernel(peers, groups, *refs):
    (
        len_ref,
        q_ref,
        nk_ref,
        cache_ref,
        wv_ref,
        wo_ref,
        res_ref,
        gain_ref,
        ids_ref,
        gates_ref,
        wg_ref,
        wu_ref,
        wd_ref,
        out_ref,
        dense,
        wo_v,
        wo_t,
        res_s,
        res_r,
        q_s,
        nk_s,
        new_s,
        ctx_s,
        send_v,
        att_t,
        att,
        ssq_s,
        ssq_r,
        sum_v,
        x_v,
        meta_v,
        wg_v,
        wu_v,
        wd_v,
        part_v,
        acc,
        hid_v,
        spread_s,
        code_s,
        gate_s,
        routed_v,
        routed_r,
        home_s,
        home_r,
        cache_sem,
        wo_sem,
        w_sem,
        ssq_sem,
        meta_sem,
        res_sem,
        home_sem,
        g_send,
        g_recv,
    ) = refs[:53]
    place = Place()
    me = place.me
    fs = lax.axis_index("fsdp")
    tokens = q_s.shape[0]
    latent = wv_ref.shape[0]
    experts, depth, half = wg_ref.shape
    rows = part_v.shape[1]
    block = rows // TOP
    per = peers // groups
    own_rows = home_s.shape[1]
    barrier = pltpu.get_barrier_semaphore()

    def greet(axis, mine, size):
        def one(d):
            pl.semaphore_signal(
                barrier, inc=1, device_id={axis: lax.rem(mine + d, size)}, device_id_type=MESH
            )

        each(1, size, one)

    greet("exp", me, peers)
    greet("fsdp", fs, groups)
    rest = refs[53:]
    heads = [
        Reduce(place, r, send_v, rest[9 * i : 9 * i + 9]) for i, r in enumerate(HEAD_ROUTES)
    ]
    rest = rest[9 * len(ROUTES) :]
    sums = [Reduce(place, r, part_v, rest[9 * i : 9 * i + 9]) for i, r in enumerate(ROUTES)]
    rest = rest[9 * len(ROUTES) :]
    gathers = [Gather(place, r, hid_v, rest[2 * i : 2 * i + 2]) for i, r in enumerate(ROUTES)]

    def group_copy(n, d, block_ref):
        return pltpu.make_async_remote_copy(
            src_ref=block_ref,
            dst_ref=block_ref,
            send_sem=g_send.at[n, d],
            recv_sem=g_recv.at[n, d],
            device_id={"fsdp": lax.rem(fs + d, groups)},
            device_id_type=MESH,
        )

    def from_group(d):
        return lax.rem(fs + groups - d, groups)

    def cache_copy(i, n):
        span = pl.ds(ROUTES[i].first // STEPS, ROUTES[i].count // STEPS)
        positions = cache_ref.shape[2]
        if n == 0:
            src = cache_ref.at[span, pl.ds(0, latent)]
            dst = dense.at[span, pl.ds(0, latent), pl.ds(0, positions)]
        else:
            left = cache_ref.shape[1] - latent
            src = cache_ref.at[span, pl.ds(latent, left)]
            dst = dense.at[span, pl.ds(0, left), pl.ds(positions, positions)]
        return pltpu.make_async_copy(src, dst, cache_sem.at[i, n])

    def weight_copy(n):
        src = (wg_ref, wu_ref, wd_ref)[n]
        dst = (wg_v, wu_v, wd_v)[n]
        return pltpu.make_async_copy(src, dst, w_sem.at[n])

    out_copy = pltpu.make_async_copy(wo_ref, wo_v, wo_sem)
    for n in range(2):
        cache_copy(0, n).start()
    out_copy.start()
    for i in range(1, len(ROUTES)):
        for n in range(2):
            cache_copy(i, n).start()

    for b in range(tokens // 16):
        span = slice(b * 16, b * 16 + 16)
        q_s[span, :] = jnp.concatenate(
            [q_ref[4 * b + i].astype(F32) for i in range(4)], axis=0
        ).astype(BF)
        nk_s[span, :] = jnp.concatenate(
            [nk_ref[4 * b + i].astype(F32) for i in range(4)], axis=0
        ).astype(BF)

    token_r = lax.broadcasted_iota(jnp.int32, (tokens, tokens), 0)
    token_c = lax.broadcasted_iota(jnp.int32, (tokens, tokens), 1)
    diagonal = token_r == token_c
    same = (token_r // STEPS == token_c // STEPS) & (token_c <= token_r)
    fresh = lax.dot_general(q_s[...], nk_s[...], NT, preferred_element_type=F32)
    new_s[...] = jnp.where(same, fresh * score_scale, -1e30)

    which = lax.broadcasted_iota(jnp.int32, (16, 1), 0) // STEPS
    position = lax.broadcasted_iota(jnp.int32, (16, cache_ref.shape[2]), 1)
    rope = cache_ref.shape[1] - latent

    def attend(b):
        span = pl.ds(pl.multiple_of(b * 16, 16), 16)
        first = b * 4
        q16 = q_s[span, :]

        def score(row):
            return matmul(q16[:, :latent], dense[row, :, : position.shape[1]]) + matmul(
                q16[:, latent:], dense[row, :rope, position.shape[1] :]
            )

        scores = score(first)
        length = jnp.full(position.shape, len_ref[first])
        for n in range(1, 4):
            scores = jnp.where(which == n, score(first + n), scores)
            length = jnp.where(which == n, len_ref[first + n], length)
        scores = jnp.where(position < length, scores * score_scale, -1e30)
        new = new_s[span, :]
        highest = jnp.maximum(jnp.max(scores, -1, keepdims=True), jnp.max(new, -1, keepdims=True))
        cache_exp = jnp.exp(scores - highest)
        new_exp = jnp.exp(new - highest)
        total = jnp.sum(cache_exp, -1, keepdims=True) + jnp.sum(new_exp, -1, keepdims=True)
        cache_w = (cache_exp / total).astype(BF)
        new_w = (new_exp / total).astype(BF)

        def mix(row):
            return lax.dot_general(
                cache_w, dense[row, :, : position.shape[1]], NT, preferred_element_type=F32
            )

        context = mix(first)
        for n in range(1, 4):
            context = jnp.where(which == n, mix(first + n), context)
        context = context + matmul(new_w, nk_s[:, :latent])
        ctx_s[span, :] = context.astype(BF)

    def meta_copy(d):
        tile = meta_v.at[fs, me]
        return remote(tile, tile, meta_sem.at[0], meta_sem.at[1], place.plus(d))

    def all_copies(buffer, sem):
        tiles = buffer.at[pl.ds(0, peers - 1)]
        return remote(tiles, tiles, sem.at[0], sem.at[1], me)

    for i, route in enumerate(ROUTES):
        for n in range(2):
            cache_copy(i, n).wait()
        each(route.first // 16, (route.first + route.count) // 16, attend)
        if i == 0:
            for n in range(3):
                weight_copy(n).start()

    out_copy.wait()
    for c in range(wo_v.shape[1] // 128):
        span = slice(c * 128, c * 128 + 128)
        wo_t[span, :] = wo_v[:, span].T
    gain = jnp.zeros((1, depth), F32)
    for j in range(peers):
        part = slice(j * depth, (j + 1) * depth)
        res_s[j, :, :depth] = res_ref[0, :, part].astype(F32)
        gain = jnp.where(me == j, gain_ref[:, part], gain)
    gain = jnp.concatenate([gain, jnp.zeros((1, WIDE - depth), F32)], axis=1)
    lane = lax.broadcasted_iota(jnp.int32, (1, rows), 1)
    here = lane // (STEPS * TOP) == lax.rem(me, 4)
    own_ids = jnp.where(here, spread(ids_ref[0].astype(F32), rows), 0.0)
    own_gates = jnp.where(here, spread(gates_ref[0], rows), 0.0)
    meta_v[fs, me] = jnp.concatenate([own_ids, own_gates, jnp.zeros((6, rows), F32)], axis=0)
    values = matmul(ctx_s[...], wv_ref[...]).astype(BF)
    pl.semaphore_wait(barrier, peers - 1 + groups - 1)

    def project(n):
        offsets = [offset_of(4 * n + k) for k in range(4)]
        for offset in offsets:
            j = place.plus(offset)
            span = pl.ds(pl.multiple_of(j * depth, 16), depth)
            part = lax.dot_general(wo_t[span, :], values, NT, preferred_element_type=F32)
            send_v[j] = part.astype(BF)
        for offset in offsets:
            for h in heads:
                h.send(offset)

    each(0, peers // 4, project)

    def res_copy(d):
        peer = place.plus(d)
        return remote(res_s.at[peer], res_r.at[me], res_sem.at[0], res_sem.at[1], peer)

    for d in FAR_FIRST:
        meta_copy(d).start()
        res_copy(d).start()
    res_r[me] = res_s[me]

    for h in heads:
        each(h.route.n[2], h.route.plane, h.step)
    for h in heads:
        each(0, h.route.n[2], h.step)
    pair_lane = lax.broadcasted_iota(jnp.int32, (1, rows), 1)
    slot_c = lax.broadcasted_iota(jnp.int32, (rows, experts * block), 1)
    slot_r = lax.broadcasted_iota(jnp.int32, (experts * block, rows), 0)

    def read_meta(q):
        piece = from_group(q)

        def one(n):
            info = meta_v[piece, 4 * n]
            for i in range(1, 4):
                info = info + meta_v[piece, 4 * n + i]
            j = piece * per + n
            code = info[0:1, :].astype(jnp.int32) * block + pair_lane // TOP
            code_s[j] = code
            code = jnp.sum(jnp.where(diagonal, code, 0), 1, keepdims=True)
            part_v[j] = (code == slot_c).astype(F32).astype(BF)
            gate_s[j] = info[1:2, :]

        each(0, per, one)

    for h in heads:
        h.turns()
    all_copies(meta_v.at[fs], meta_sem).wait_recv()
    for d in range(1, groups):
        group_copy(0, d, meta_v.at[fs]).start()
    read_meta(0)
    for h in heads:
        h.add(att_t)
    all_copies(res_s, res_sem).wait_recv()

    attended = jnp.concatenate([att_t[...], jnp.zeros((WIDE - depth, tokens), F32)], axis=0).T
    own_res = jnp.concatenate([res_r[n][:, :depth] for n in range(peers)], axis=0)
    own_res = jnp.concatenate([own_res, jnp.zeros((tokens, WIDE - depth), F32)], axis=1)
    attended = attended + own_res
    att[...] = attended
    x_v[fs] = (attended * gain).astype(BF)
    for d in range(1, groups):
        group_copy(1, d, x_v.at[fs]).start()
    column = jnp.sum(attended * attended, -1, keepdims=True)
    row = jnp.sum(jnp.where(diagonal, column, 0.0), 0, keepdims=True)
    ssq_s[...] = jnp.broadcast_to(row, ssq_s.shape)

    def ssq_copy(d):
        return remote(ssq_s, ssq_r.at[d], ssq_sem.at[0], ssq_sem.at[1], lax.rem(me + d, peers))

    ssq_r[0] = ssq_s[...]
    each(1, peers, lambda d: ssq_copy(d).start())

    def multiply(first, count, x):
        def some(n):
            for e in [4 * n + k for k in range(4)]:
                spot = pl.ds(pl.multiple_of(e * block, block), block)
                gate = matmul(x, wg_v[e]).astype(BF)
                up = matmul(x, wu_v[e]).astype(BF)
                dense[first : first + count, spot, :half] = gate.reshape(count, block, half)
                dense[first : first + count, spot, half:] = up.reshape(count, block, half)

        each(0, experts // 4, some)

    def pick(i):
        found = []
        for k in range(2):
            q = (2 * i + k) // per
            n = lax.rem((2 * i + k) // NY, 2) * NY + lax.rem(place.y + 2 * i + k, NY)
            j = from_group(q) * per + n
            found.append((j, matmul(part_v[j], dense[q * per + n]).astype(BF)))
        for j, part in found:
            part_v[j] = part
        for j, _ in found:
            offset = (
                lax.rem(j // (NZ * NY) + NX - place.x, NX),
                lax.rem(lax.rem(j // NY, NZ) + NZ - place.z, NZ),
                lax.rem(lax.rem(j, NY) + NY - place.y, NY),
            )
            for s in sums:
                s.send(offset)

    def pick_group(q):
        each(q * per // 2, (q + 1) * per // 2, pick)

    def relay(q):
        p = from_group(q)
        x_off = lax.rem(p // 2 + NX - place.x, NX)
        z_low = 2 * lax.rem(p, 2)

        def z_off(i):
            return lax.rem(z_low + i + NZ - place.z, NZ)

        @pl.when(lax.rem(p, 2) == place.z // 2)
        def _():
            each(0, NY, lambda i: sums[0].step(i * NX + x_off))

        each(0, 2, lambda i: sums[1].step(x_off * NZ + z_off(i)))

        @pl.when(x_off == 0)
        def _():
            each(0, 2 * NY, lambda i: sums[2].step(z_off(i // NY) * NY + lax.rem(i, NY)))

    weight_copy(0).wait()
    weight_copy(1).wait()
    multiply(0, per, x_v[fs][:, :depth])
    pick_group(0)

    for q in range(1, groups):
        group_copy(0, q, meta_v.at[from_group(q)]).wait_recv()
        group_copy(1, q, x_v.at[from_group(q)]).wait_recv()
        read_meta(q)
    others = [x_v[from_group(q)][:, :depth] for q in range(1, groups)]
    multiply(per, peers - per, jnp.concatenate(others, axis=0))
    pick_group(1)
    relay(0)
    pick_group(2)
    relay(1)
    pick_group(3)
    all_copies(ssq_r.at[pl.ds(1, peers - 1)], ssq_sem).wait_recv()
    sum_v[fs] = jnp.sum(ssq_r[...], axis=0)
    for d in range(1, groups):
        group_copy(2, d, sum_v.at[fs]).start()
    relay(2)
    relay(3)

    for s in sums:
        s.turns()

    def build(n):
        for j in (2 * n, 2 * n + 1):
            spread_s[j] = (code_s[j] == slot_r).astype(F32).astype(BF)

    each(0, peers // 2, build)
    for s in sums:
        s.add(acc)

    for d in range(1, groups):
        group_copy(2, d, sum_v.at[from_group(d)]).wait_recv()
    token = block * lax.rem(me, per) + token_r // TOP
    squares = jnp.sum(jnp.where(token == token_c, sum_v[me // per][:1, :], 0.0), 1, keepdims=True)
    scale = lax.rsqrt(squares / (depth * peers) + 1e-06)
    weight = jnp.sum(jnp.where(diagonal, gate_s[me], 0.0), 1, keepdims=True)
    gate = acc[:, :half] * scale
    up = acc[:, half:] * scale
    hid_v[me] = (gate / (1.0 + jnp.exp(-gate)) * up * weight).astype(BF)

    for g in gathers:
        g.begin()
    for g in gathers:
        for d3 in range(1, g.route.n[2]):
            g.relay_last(d3)
    for g in gathers:
        each(g.route.n[2], g.route.plane, g.relay_middle)

    def expand(n):
        offsets = [offset_of(2 * n), offset_of(2 * n + 1)]
        for offset in offsets:
            for g in gathers:
                g.arrive(offset)
        blocks = [place.minus(offset) for offset in offsets]
        full = [matmul(spread_s[j], hid_v[j]).astype(BF) for j in blocks]
        for j, rows_of in zip(blocks, full):
            spot = pl.ds(pl.multiple_of(j * block, block), block)
            dense[:, spot, :half] = rows_of.reshape(experts, block, half)

    each(0, peers // 2, expand)
    weight_copy(2).wait()

    def shares(pieces):
        spots = [pl.ds(pl.multiple_of(p * tokens, tokens), tokens) for p in pieces]

        def some(n, total):
            for k in range(4):
                e = 4 * n + k
                both = jnp.concatenate([dense[e, spot, :half] for spot in spots], axis=0)
                total = total + lax.dot_general(both, wd_v[e], NT, preferred_element_type=F32)
            return total

        start = jnp.zeros((len(pieces) * tokens, depth), F32)
        return lax.fori_loop(0, experts // 4, some, start)

    def routed_copy(d):
        peer = lax.rem(fs + d, groups)
        return pltpu.make_async_remote_copy(
            src_ref=routed_v.at[peer],
            dst_ref=routed_r.at[d],
            send_sem=g_send.at[3, d],
            recv_sem=g_recv.at[3, d],
            device_id={"fsdp": peer},
            device_id_type=MESH,
        )

    mixed = att[:, :depth]
    for pair in ((2, 3), (1, 0)):
        both = shares([lax.rem(fs + d, groups) for d in pair])
        for k, d in enumerate(pair):
            share = both[k * tokens : (k + 1) * tokens]
            if d > 0:
                routed_v[lax.rem(fs + d, groups), :, :depth] = share.astype(BF)
                routed_copy(d).start()
            else:
                mixed = mixed + share
    for d in range(1, groups):
        routed_copy(d).wait_recv()
        mixed = mixed + routed_r[d][:, :depth].astype(F32)
    for j in range(peers):
        home_s[j, :, :depth] = mixed[j * own_rows : (j + 1) * own_rows, :]

    def home_copy(d):
        peer = place.plus(d)
        return remote(home_s.at[peer], home_r.at[me], home_sem.at[0], home_sem.at[1], peer)

    for d in FAR_FIRST:
        home_copy(d).start()
    home_r[me] = home_s[me]
    for s in heads + sums + gathers:
        s.finish()
    for d in range(1, groups):
        routed_copy(d).wait_send()
        group_copy(0, d, meta_v.at[fs]).wait_send()
        group_copy(1, d, x_v.at[fs]).wait_send()
        group_copy(2, d, sum_v.at[fs]).wait_send()

    all_copies(ssq_r, ssq_sem).wait_send()
    all_copies(meta_v.at[fs], meta_sem).wait_send()
    all_copies(res_s, res_sem).wait_send()
    all_copies(home_s, home_sem).wait_recv()
    for j in range(peers):
        out_ref[0, :, j * depth : (j + 1) * depth] = home_r[j][:, :depth]
    all_copies(home_s, home_sem).wait_send()


def shards(
    residual,
    gain,
    queries,
    new_keys,
    cache,
    lengths,
    w_value,
    w_out,
    w_gate,
    w_up,
    w_down,
    expert_ids,
    gates,
):
    peers = lax.axis_size("exp")
    groups = lax.axis_size("fsdp")
    group_rows, steps, _, key = queries.shape
    tokens = group_rows * steps
    experts, depth, half = w_gate.shape
    block = tokens * groups // peers
    rows = block * TOP
    smem, dma = pl.BlockSpec(memory_space=pltpu.SMEM), pltpu.SemaphoreType.DMA
    scratch = [
        pltpu.VMEM((peers, experts * block, 2 * half), BF),
        pltpu.VMEM(w_out.shape[1:], BF),
        pltpu.VMEM((w_out.shape[2], w_out.shape[1]), BF),
        pltpu.VMEM((peers, steps, WIDE), F32),
        pltpu.VMEM((peers, steps, WIDE), F32),
        pltpu.VMEM((tokens, key), BF),
        pltpu.VMEM((tokens, key), BF),
        pltpu.VMEM((tokens, tokens), F32),
        pltpu.VMEM((tokens, w_value.shape[1]), BF),
        pltpu.VMEM((peers, depth, tokens), BF),
        pltpu.VMEM((depth, tokens), F32),
        pltpu.VMEM((tokens, WIDE), F32),
        pltpu.VMEM((8, tokens), F32),
        pltpu.VMEM((peers, 8, tokens), F32),
        pltpu.VMEM((groups, 8, tokens), F32),
        pltpu.VMEM((groups, tokens, WIDE), BF),
        pltpu.VMEM((groups, peers, 8, rows), F32),
        pltpu.VMEM(w_gate.shape, BF),
        pltpu.VMEM(w_gate.shape, BF),
        pltpu.VMEM(w_gate.shape, BF),
        pltpu.VMEM((peers, rows, 2 * half), BF),
        pltpu.VMEM((rows, 2 * half), F32),
        pltpu.VMEM((peers, rows, half), BF),
        pltpu.VMEM((peers, experts * block, rows), BF),
        pltpu.VMEM((peers, 1, rows), jnp.int32),
        pltpu.VMEM((peers, 1, rows), F32),
        pltpu.VMEM((groups, tokens, WIDE), BF),
        pltpu.VMEM((groups, tokens, WIDE), BF),
        pltpu.VMEM((peers, steps, WIDE), F32),
        pltpu.VMEM((peers, steps, WIDE), F32),
        dma((len(ROUTES), 2)),
        dma,
        dma((3,)),
        dma((2,)),
        dma((2,)),
        dma((2,)),
        dma((2,)),
        dma((4, groups)),
        dma((4, groups)),
    ]
    for route in HEAD_ROUTES:
        scratch += reduce_scratch(route, tokens)
    for route in ROUTES:
        scratch += reduce_scratch(route, 2 * half)
    for route in ROUTES:
        scratch += gather_scratch(route)
    return pl.pallas_call(
        functools.partial(layer_kernel, peers, groups),
        out_shape=jax.ShapeDtypeStruct(residual.shape, F32),
        in_specs=[smem, vmem(), vmem(), anywhere(), vmem(), anywhere()]
        + [vmem()] * 4
        + [anywhere()] * 3,
        out_specs=vmem(),
        scratch_shapes=scratch,
        compiler_params=pltpu.CompilerParams(
            collective_id=0, has_side_effects=True, vmem_limit_bytes=HIGH
        ),
        name="layer",
    )(
        lengths,
        queries[:, :, 0, :],
        new_keys,
        cache,
        w_value[0],
        w_out[0],
        residual,
        gain.reshape(1, -1),
        expert_ids,
        gates,
        w_gate,
        w_up,
        w_down,
    )


def solution(mesh):
    return jax.shard_map(
        shards,
        mesh=mesh,
        in_specs=(
            P(("fsdp", "exp"), None, None),
            P(),
            P("fsdp", None, "exp", None),
            P("fsdp", None, None),
            P("fsdp", None, None),
            P("fsdp"),
            P("exp", None, None),
            P("exp", None, None),
            P(None, "exp", "fsdp"),
            P(None, "exp", "fsdp"),
            P(None, "exp", "fsdp"),
            P(("fsdp", "exp"), None, None),
            P(("fsdp", "exp"), None, None),
        ),
        out_specs=P(("fsdp", "exp"), None, None),
        check_vma=False,
    )
```

```python
import functools

import jax
import jax.numpy as jnp
from jax import lax
from jax.experimental import pallas as pl
from jax.experimental.pallas import tpu as pltpu
from jax.sharding import PartitionSpec as P

TOP = 8
STEPS = 4
score_scale = 0.07216878364870322
MESH = pl.DeviceIdType.MESH
BF = jnp.bfloat16
F32 = jnp.float32
WIDE = 256
HIGH = 60 * 1024 * 1024
NX, NZ, NY = 2, 4, 4
NT = (((1,), (1,)), ((), ()))


def matmul(a, b):
    return jnp.dot(a, b, preferred_element_type=F32)


def vmem():
    return pl.BlockSpec(memory_space=pltpu.VMEM)


def anywhere():
    return pl.BlockSpec(memory_space=pl.ANY)


def each(lower, upper, body):
    def step(i, carry):
        body(i)
        return carry

    lax.fori_loop(lower, upper, step, 0)


class Place:
    def __init__(self):
        self.me = lax.axis_index("exp")
        self.x = self.me // (NZ * NY)
        self.z = lax.rem(self.me // NY, NZ)
        self.y = lax.rem(self.me, NY)

    def index(self, x, z, y):
        return (lax.rem(x, NX) * NZ + lax.rem(z, NZ)) * NY + lax.rem(y, NY)

    def plus(self, offset):
        dx, dz, dy = offset
        return self.index(self.x + dx, self.z + dz, self.y + dy)

    def minus(self, offset):
        dx, dz, dy = offset
        return self.index(self.x + NX - dx, self.z + NZ - dz, self.y + NY - dy)


class Route:
    def __init__(self, kind, first, count):
        self.axes = {"z": (1, 2, 0), "y": (2, 0, 1), "x": (0, 1, 2)}[kind]
        self.n = tuple((NX, NZ, NY)[a] for a in self.axes)
        self.first, self.count = first, count
        self.rows = pl.ds(first, count)
        self.plane = self.n[1] * self.n[2]

    def offset(self, d1, d2, d3):
        out = [0, 0, 0]
        for a, d in zip(self.axes, (d1, d2, d3)):
            out[a] = d
        return tuple(out)

    def split(self, offset):
        return tuple(offset[a] for a in self.axes)


ROUTES = (Route("z", 0, 32), Route("y", 32, 48), Route("x", 80, 48))
HEAD_ROUTES = (Route("z", 0, 64), Route("y", 64, 80), Route("x", 144, 80))


def remote(src, dst, send, recv, peer):
    return pltpu.make_async_remote_copy(
        src_ref=src,
        dst_ref=dst,
        send_sem=send,
        recv_sem=recv,
        device_id={"exp": peer},
        device_id_type=MESH,
    )


class Reduce:
    def __init__(self, place, route, src, bufs):
        self.place, self.route, self.src = place, route, src
        self.got1, self.out1, self.got2, self.keep, self.out2, self.got3 = bufs[:6]
        self.sent, self.r1, self.r2 = bufs[6:]

    def first(self, d1, d2, d3):
        route = self.route
        g = d2 * route.n[2] + d3
        return remote(
            self.src.at[self.place.plus(route.offset(d1, d2, d3)), route.rows],
            self.got1.at[g, d1 - 1],
            self.sent.at[0],
            self.r1.at[g],
            self.place.plus(route.offset(d1, 0, 0)),
        )

    def second(self, d2, d3):
        return remote(
            self.out1.at[d2 * self.route.n[2] + d3],
            self.got2.at[d3, d2 - 1],
            self.sent.at[1],
            self.r2.at[d3],
            self.place.plus(self.route.offset(0, d2, 0)),
        )

    def third(self, d3):
        return remote(
            self.out2.at[d3],
            self.got3.at[d3 - 1],
            self.sent.at[2],
            self.r2.at[self.route.n[2]],
            self.place.plus(self.route.offset(0, 0, d3)),
        )

    def send(self, offset):
        d1, d2, d3 = self.route.split(offset)

        @pl.when(d1 > 0)
        def _():
            self.first(d1, d2, d3).start()

    def arrived(self, got, sem):
        remote(got, got, self.sent.at[0], sem, self.place.me).wait_recv()

    def step(self, g):
        route = self.route
        d2, d3 = g // route.n[2], lax.rem(g, route.n[2])
        self.arrived(self.got1.at[g], self.r1.at[g])
        total = self.src[self.place.plus(route.offset(0, d2, d3)), route.rows].astype(F32)
        for d in range(1, route.n[0]):
            total = total + self.got1[g, d - 1].astype(F32)

        @pl.when(d2 == 0)
        def _():
            self.keep[d3] = total

        @pl.when(d2 != 0)
        def _():
            self.out1[g] = total.astype(BF)
            self.second(d2, d3).start()

    def turn(self, d3):
        self.arrived(self.got2.at[d3], self.r2.at[d3])
        total = self.keep[d3]
        for d in range(1, self.route.n[1]):
            total = total + self.got2[d3, d - 1].astype(F32)
        return total

    def turns(self):
        for d3 in range(1, self.route.n[2]):
            self.out2[d3] = self.turn(d3).astype(BF)
            self.third(d3).start()
        self.keep[0] = self.turn(0)

    def add(self, acc_ref):
        self.arrived(self.got3, self.r2.at[self.route.n[2]])
        total = self.keep[0]
        for d in range(1, self.route.n[2]):
            total = total + self.got3[d - 1].astype(F32)
        acc_ref[self.route.rows] = total

    def finish(self):
        for n, got in enumerate((self.got1, self.got2, self.got3)):
            remote(got, got, self.sent.at[n], self.r2.at[0], self.place.me).wait_send()


def reduce_scratch(route, cols):
    n1, n2, n3 = route.n
    dma = pltpu.SemaphoreType.DMA
    return [
        pltpu.VMEM((n2 * n3, n1 - 1, route.count, cols), BF),
        pltpu.VMEM((n2 * n3, route.count, cols), BF),
        pltpu.VMEM((n3, n2 - 1, route.count, cols), BF),
        pltpu.VMEM((n3, route.count, cols), F32),
        pltpu.VMEM((n3, route.count, cols), BF),
        pltpu.VMEM((n3 - 1, route.count, cols), BF),
        dma((3,)),
        dma((n2 * n3,)),
        dma((n3 + 1,)),
    ]


class Gather:
    def __init__(self, place, route, whole, bufs):
        self.place, self.route, self.whole = place, route, whole
        self.sent, self.r = bufs

    def copy(self, source, to, offset):
        _, n2, n3 = self.route.n
        d1, d2, d3 = offset
        block = self.whole.at[source, self.route.rows]
        peer = self.place.plus(self.route.offset(*to))
        return remote(block, block, self.sent, self.r.at[(d1 * n2 + d2) * n3 + d3], peer)

    def source(self, *offset):
        return self.place.minus(self.route.offset(*offset))

    def push1(self, d2, d3):
        for d in sorted(range(1, self.route.n[0]), key=lambda d: d != 2):
            self.copy(self.source(0, d2, d3), (d, 0, 0), (d, d2, d3)).start()

    def push2(self, d3):
        for d in range(1, self.route.n[1]):
            self.copy(self.source(0, 0, d3), (0, d, 0), (0, d, d3)).start()

    def begin(self):
        for d in range(1, self.route.n[2]):
            self.copy(self.place.me, (0, 0, d), (0, 0, d)).start()
        self.push2(0)
        self.push1(0, 0)

    def wait(self, offset):
        self.copy(self.source(*offset), (0, 0, 0), offset).wait_recv()

    def relay_last(self, d3):
        self.wait((0, 0, d3))
        self.push2(d3)
        self.push1(0, d3)

    def relay_middle(self, g):
        d2, d3 = g // self.route.n[2], lax.rem(g, self.route.n[2])
        self.wait((0, d2, d3))
        self.push1(d2, d3)

    def arrive(self, offset):
        split = self.route.split(offset)

        @pl.when(split[0] > 0)
        def _():
            self.wait(split)

    def finish(self):
        n1, n2, n3 = self.route.n
        blocks = self.whole.at[pl.ds(0, n1 * n2 * n3 - 1), self.route.rows]
        remote(blocks, blocks, self.sent, self.r.at[0], self.place.me).wait_send()


def gather_scratch(route):
    dma = pltpu.SemaphoreType.DMA
    return [dma, dma((route.n[0] * route.n[1] * route.n[2],))]


def offset_of_int(o):
    return (o // (NZ * NY), o // NY % NZ, o % NY)


def offset_of(o):
    return (o // (NZ * NY), lax.rem(o // NY, NZ), lax.rem(o, NY))


def hops(offset):
    dx, dz, dy = offset
    return 2 * dx + min(dz, NZ - dz) + min(dy, NY - dy)


FAR_FIRST = sorted((offset_of_int(o) for o in range(1, NX * NZ * NY)), key=hops, reverse=True)


def spread(block, lanes):
    wide = jnp.concatenate([block] * (lanes // block.shape[1]), axis=1)
    step = lax.rem(lax.broadcasted_iota(jnp.int32, wide.shape, 1) // TOP, STEPS)
    row = lax.broadcasted_iota(jnp.int32, wide.shape, 0)
    return jnp.sum(jnp.where(step == row, wide, 0.0), 0, keepdims=True)


def layer_kernel(peers, groups, *refs):
    (
        len_ref,
        q_ref,
        nk_ref,
        cache_ref,
        wv_ref,
        wo_ref,
        res_ref,
        gain_ref,
        ids_ref,
        gates_ref,
        wg_ref,
        wu_ref,
        wd_ref,
        out_ref,
        dense,
        wo_v,
        wo_t,
        res_s,
        res_r,
        q_s,
        nk_s,
        new_s,
        ctx_s,
        send_v,
        att_t,
        att,
        ssq_s,
        ssq_r,
        sum_v,
        x_v,
        meta_v,
        wg_v,
        wu_v,
        wd_v,
        part_v,
        acc,
        hid_v,
        spread_s,
        code_s,
        gate_s,
        routed_v,
        routed_r,
        home_s,
        home_r,
        cache_sem,
        wo_sem,
        w_sem,
        ssq_sem,
        meta_sem,
        res_sem,
        home_sem,
        g_send,
        g_recv,
    ) = refs[:53]
    place = Place()
    me = place.me
    fs = lax.axis_index("fsdp")
    tokens = q_s.shape[0]
    latent = wv_ref.shape[0]
    experts, depth, half = wg_ref.shape
    rows = part_v.shape[1]
    block = rows // TOP
    per = peers // groups
    own_rows = home_s.shape[1]
    barrier = pltpu.get_barrier_semaphore()

    def greet(axis, mine, size):
        def one(d):
            pl.semaphore_signal(
                barrier, inc=1, device_id={axis: lax.rem(mine + d, size)}, device_id_type=MESH
            )

        each(1, size, one)

    greet("exp", me, peers)
    greet("fsdp", fs, groups)
    rest = refs[53:]
    heads = [
        Reduce(place, r, send_v, rest[9 * i : 9 * i + 9]) for i, r in enumerate(HEAD_ROUTES)
    ]
    rest = rest[9 * len(ROUTES) :]
    sums = [Reduce(place, r, part_v, rest[9 * i : 9 * i + 9]) for i, r in enumerate(ROUTES)]
    rest = rest[9 * len(ROUTES) :]
    gathers = [Gather(place, r, hid_v, rest[2 * i : 2 * i + 2]) for i, r in enumerate(ROUTES)]

    def group_copy(n, d, block_ref):
        return pltpu.make_async_remote_copy(
            src_ref=block_ref,
            dst_ref=block_ref,
            send_sem=g_send.at[n, d],
            recv_sem=g_recv.at[n, d],
            device_id={"fsdp": lax.rem(fs + d, groups)},
            device_id_type=MESH,
        )

    def from_group(d):
        return lax.rem(fs + groups - d, groups)

    def turn_of(q):
        return q + lax.rem(q, 2) * (2 - q) * 2 * (1 - lax.rem(fs, 2))

    def piece_of(q):
        return from_group(turn_of(q))

    def cache_copy(i, n):
        span = pl.ds(ROUTES[i].first // STEPS, ROUTES[i].count // STEPS)
        positions = cache_ref.shape[2]
        if n == 0:
            src = cache_ref.at[span, pl.ds(0, latent)]
            dst = dense.at[span, pl.ds(0, latent), pl.ds(0, positions)]
        else:
            left = cache_ref.shape[1] - latent
            src = cache_ref.at[span, pl.ds(latent, left)]
            dst = dense.at[span, pl.ds(0, left), pl.ds(positions, positions)]
        return pltpu.make_async_copy(src, dst, cache_sem.at[i, n])

    def weight_copy(n):
        src = (wg_ref, wu_ref, wd_ref)[n]
        dst = (wg_v, wu_v, wd_v)[n]
        return pltpu.make_async_copy(src, dst, w_sem.at[n])

    out_copy = pltpu.make_async_copy(wo_ref, wo_v, wo_sem)
    for n in range(2):
        cache_copy(0, n).start()
    out_copy.start()
    for i in range(1, len(ROUTES)):
        for n in range(2):
            cache_copy(i, n).start()

    for b in range(tokens // 16):
        span = slice(b * 16, b * 16 + 16)
        q_s[span, :] = jnp.concatenate(
            [q_ref[4 * b + i].astype(F32) for i in range(4)], axis=0
        ).astype(BF)
        nk_s[span, :] = jnp.concatenate(
            [nk_ref[4 * b + i].astype(F32) for i in range(4)], axis=0
        ).astype(BF)

    token_r = lax.broadcasted_iota(jnp.int32, (tokens, tokens), 0)
    token_c = lax.broadcasted_iota(jnp.int32, (tokens, tokens), 1)
    diagonal = token_r == token_c
    same = (token_r // STEPS == token_c // STEPS) & (token_c <= token_r)
    fresh = lax.dot_general(q_s[...], nk_s[...], NT, preferred_element_type=F32)
    new_s[...] = jnp.where(same, fresh * score_scale, -1e30)

    which = lax.broadcasted_iota(jnp.int32, (16, 1), 0) // STEPS
    position = lax.broadcasted_iota(jnp.int32, (16, cache_ref.shape[2]), 1)
    rope = cache_ref.shape[1] - latent

    def attend(b):
        span = pl.ds(pl.multiple_of(b * 16, 16), 16)
        first = b * 4
        q16 = q_s[span, :]

        def score(row):
            return matmul(q16[:, :latent], dense[row, :, : position.shape[1]]) + matmul(
                q16[:, latent:], dense[row, :rope, position.shape[1] :]
            )

        scores = score(first)
        length = jnp.full(position.shape, len_ref[first])
        for n in range(1, 4):
            scores = jnp.where(which == n, score(first + n), scores)
            length = jnp.where(which == n, len_ref[first + n], length)
        scores = jnp.where(position < length, scores * score_scale, -1e30)
        new = new_s[span, :]
        highest = jnp.maximum(jnp.max(scores, -1, keepdims=True), jnp.max(new, -1, keepdims=True))
        cache_exp = jnp.exp(scores - highest)
        new_exp = jnp.exp(new - highest)
        total = jnp.sum(cache_exp, -1, keepdims=True) + jnp.sum(new_exp, -1, keepdims=True)
        cache_w = (cache_exp / total).astype(BF)
        new_w = (new_exp / total).astype(BF)

        def mix(row):
            return lax.dot_general(
                cache_w, dense[row, :, : position.shape[1]], NT, preferred_element_type=F32
            )

        context = mix(first)
        for n in range(1, 4):
            context = jnp.where(which == n, mix(first + n), context)
        context = context + matmul(new_w, nk_s[:, :latent])
        ctx_s[span, :] = context.astype(BF)

    def meta_copy(d):
        tile = meta_v.at[fs, me]
        return remote(tile, tile, meta_sem.at[0], meta_sem.at[1], place.plus(d))

    def all_copies(buffer, sem):
        tiles = buffer.at[pl.ds(0, peers - 1)]
        return remote(tiles, tiles, sem.at[0], sem.at[1], me)

    for i, route in enumerate(ROUTES):
        for n in range(2):
            cache_copy(i, n).wait()
        each(route.first // 16, (route.first + route.count) // 16, attend)
        if i == 0:
            for n in range(3):
                weight_copy(n).start()

    out_copy.wait()
    for c in range(wo_v.shape[1] // 128):
        span = slice(c * 128, c * 128 + 128)
        wo_t[span, :] = wo_v[:, span].T
    gain = jnp.zeros((1, depth), F32)
    for j in range(peers):
        part = slice(j * depth, (j + 1) * depth)
        res_s[j, :, :depth] = res_ref[0, :, part].astype(F32)
        gain = jnp.where(me == j, gain_ref[:, part], gain)
    gain = jnp.concatenate([gain, jnp.zeros((1, WIDE - depth), F32)], axis=1)
    lane = lax.broadcasted_iota(jnp.int32, (1, rows), 1)
    here = lane // (STEPS * TOP) == lax.rem(me, 4)
    own_ids = jnp.where(here, spread(ids_ref[0].astype(F32), rows), 0.0)
    own_gates = jnp.where(here, spread(gates_ref[0], rows), 0.0)
    meta_v[fs, me] = jnp.concatenate([own_ids, own_gates, jnp.zeros((6, rows), F32)], axis=0)
    values = matmul(ctx_s[...], wv_ref[...]).astype(BF)
    pl.semaphore_wait(barrier, peers - 1 + groups - 1)

    def project(n):
        offsets = [offset_of(4 * n + k) for k in range(4)]
        for offset in offsets:
            j = place.plus(offset)
            span = pl.ds(pl.multiple_of(j * depth, 16), depth)
            part = lax.dot_general(wo_t[span, :], values, NT, preferred_element_type=F32)
            send_v[j] = part.astype(BF)
        for offset in offsets:
            for h in heads:
                h.send(offset)

    each(0, peers // 4, project)

    def res_copy(d):
        peer = place.plus(d)
        return remote(res_s.at[peer], res_r.at[me], res_sem.at[0], res_sem.at[1], peer)

    for d in FAR_FIRST:
        meta_copy(d).start()
        res_copy(d).start()
    res_r[me] = res_s[me]

    for h in heads:
        each(h.route.n[2], h.route.plane, h.step)
    for h in heads:
        each(0, h.route.n[2], h.step)
    pair_lane = lax.broadcasted_iota(jnp.int32, (1, rows), 1)
    slot_c = lax.broadcasted_iota(jnp.int32, (rows, experts * block), 1)
    slot_r = lax.broadcasted_iota(jnp.int32, (experts * block, rows), 0)

    def read_meta(q):
        piece = piece_of(q)

        def one(n):
            info = meta_v[piece, 4 * n]
            for i in range(1, 4):
                info = info + meta_v[piece, 4 * n + i]
            j = piece * per + n
            code = info[0:1, :].astype(jnp.int32) * block + pair_lane // TOP
            code_s[j] = code
            code = jnp.sum(jnp.where(diagonal, code, 0), 1, keepdims=True)
            part_v[j] = (code == slot_c).astype(F32).astype(BF)
            gate_s[j] = info[1:2, :]

        each(0, per, one)

    for h in heads:
        h.turns()
    all_copies(meta_v.at[fs], meta_sem).wait_recv()
    for d in range(1, groups):
        group_copy(0, d, meta_v.at[fs]).start()
    read_meta(0)
    for h in heads:
        h.add(att_t)
    all_copies(res_s, res_sem).wait_recv()

    attended = jnp.concatenate([att_t[...], jnp.zeros((WIDE - depth, tokens), F32)], axis=0).T
    own_res = jnp.concatenate([res_r[n][:, :depth] for n in range(peers)], axis=0)
    own_res = jnp.concatenate([own_res, jnp.zeros((tokens, WIDE - depth), F32)], axis=1)
    attended = attended + own_res
    att[...] = attended
    x_v[fs] = (attended * gain).astype(BF)
    for d in range(1, groups):
        group_copy(1, d, x_v.at[fs]).start()
    column = jnp.sum(attended * attended, -1, keepdims=True)
    row = jnp.sum(jnp.where(diagonal, column, 0.0), 0, keepdims=True)
    ssq_s[...] = jnp.broadcast_to(row, ssq_s.shape)

    def ssq_copy(d):
        return remote(ssq_s, ssq_r.at[d], ssq_sem.at[0], ssq_sem.at[1], lax.rem(me + d, peers))

    ssq_r[0] = ssq_s[...]
    each(1, peers, lambda d: ssq_copy(d).start())

    def multiply(first, count, x):
        def some(n):
            for e in [4 * n + k for k in range(4)]:
                spot = pl.ds(pl.multiple_of(e * block, block), block)
                gate = matmul(x, wg_v[e]).astype(BF)
                up = matmul(x, wu_v[e]).astype(BF)
                dense[first : first + count, spot, :half] = gate.reshape(count, block, half)
                dense[first : first + count, spot, half:] = up.reshape(count, block, half)

        each(0, experts // 4, some)

    def pick(i):
        found = []
        for k in range(2):
            q = (2 * i + k) // per
            n = lax.rem((2 * i + k) // NY, 2) * NY + lax.rem(place.y + 2 * i + k, NY)
            j = piece_of(q) * per + n
            found.append((j, matmul(part_v[j], dense[q * per + n]).astype(BF)))
        for j, part in found:
            part_v[j] = part
        for j, _ in found:
            offset = (
                lax.rem(j // (NZ * NY) + NX - place.x, NX),
                lax.rem(lax.rem(j // NY, NZ) + NZ - place.z, NZ),
                lax.rem(lax.rem(j, NY) + NY - place.y, NY),
            )
            for s in sums:
                s.send(offset)

    def pick_group(q):
        each(q * per // 2, (q + 1) * per // 2, pick)

    def relay(q):
        p = piece_of(q)
        x_off = lax.rem(p // 2 + NX - place.x, NX)
        z_low = 2 * lax.rem(p, 2)

        def z_off(i):
            return lax.rem(z_low + i + NZ - place.z, NZ)

        @pl.when(lax.rem(p, 2) == place.z // 2)
        def _():
            each(0, NY, lambda i: sums[0].step(i * NX + x_off))

        each(0, 2, lambda i: sums[1].step(x_off * NZ + z_off(i)))

        @pl.when(x_off == 0)
        def _():
            each(0, 2 * NY, lambda i: sums[2].step(z_off(i // NY) * NY + lax.rem(i, NY)))

    def receive(q):
        group_copy(0, turn_of(q), meta_v.at[piece_of(q)]).wait_recv()
        group_copy(1, turn_of(q), x_v.at[piece_of(q)]).wait_recv()
        read_meta(q)

    def two(q):
        pair = [x_v[piece_of(n)][:, :depth] for n in (q, q + 1)]
        multiply(q * per, 2 * per, jnp.concatenate(pair, axis=0))

    weight_copy(0).wait()
    weight_copy(1).wait()
    receive(1)
    two(0)
    pick_group(0)
    pick_group(1)
    receive(2)
    receive(3)
    two(2)
    pick_group(2)
    relay(0)
    pick_group(3)
    relay(1)
    all_copies(ssq_r.at[pl.ds(1, peers - 1)], ssq_sem).wait_recv()
    sum_v[fs] = jnp.sum(ssq_r[...], axis=0)
    for d in range(1, groups):
        group_copy(2, d, sum_v.at[fs]).start()
    relay(2)
    relay(3)

    for s in sums:
        s.turns()

    def build(n):
        for j in (2 * n, 2 * n + 1):
            spread_s[j] = (code_s[j] == slot_r).astype(F32).astype(BF)

    each(0, peers // 2, build)
    for s in sums:
        s.add(acc)

    for d in range(1, groups):
        group_copy(2, d, sum_v.at[from_group(d)]).wait_recv()
    token = block * lax.rem(me, per) + token_r // TOP
    squares = jnp.sum(jnp.where(token == token_c, sum_v[me // per][:1, :], 0.0), 1, keepdims=True)
    scale = lax.rsqrt(squares / (depth * peers) + 1e-06)
    weight = jnp.sum(jnp.where(diagonal, gate_s[me], 0.0), 1, keepdims=True)
    gate = acc[:, :half] * scale
    up = acc[:, half:] * scale
    hid_v[me] = (gate / (1.0 + jnp.exp(-gate)) * up * weight).astype(BF)

    for g in gathers:
        g.begin()
    for g in gathers:
        for d3 in range(1, g.route.n[2]):
            g.relay_last(d3)
    for g in gathers:
        each(g.route.n[2], g.route.plane, g.relay_middle)

    def expand(n):
        offsets = [offset_of(2 * n), offset_of(2 * n + 1)]
        for offset in offsets:
            for g in gathers:
                g.arrive(offset)
        blocks = [place.minus(offset) for offset in offsets]
        full = [matmul(spread_s[j], hid_v[j]).astype(BF) for j in blocks]
        for j, rows_of in zip(blocks, full):
            spot = pl.ds(pl.multiple_of(j * block, block), block)
            dense[:, spot, :half] = rows_of.reshape(experts, block, half)

    each(0, peers // 2, expand)
    weight_copy(2).wait()

    def shares(pieces):
        spots = [pl.ds(pl.multiple_of(p * tokens, tokens), tokens) for p in pieces]

        def some(n, total):
            for k in range(4):
                e = 4 * n + k
                both = jnp.concatenate([dense[e, spot, :half] for spot in spots], axis=0)
                total = total + lax.dot_general(both, wd_v[e], NT, preferred_element_type=F32)
            return total

        start = jnp.zeros((len(pieces) * tokens, depth), F32)
        return lax.fori_loop(0, experts // 4, some, start)

    def routed_copy(d):
        peer = lax.rem(fs + d, groups)
        return pltpu.make_async_remote_copy(
            src_ref=routed_v.at[peer],
            dst_ref=routed_r.at[d],
            send_sem=g_send.at[3, d],
            recv_sem=g_recv.at[3, d],
            device_id={"fsdp": peer},
            device_id_type=MESH,
        )

    mixed = att[:, :depth]
    for pair in ((2, 3), (1, 0)):
        both = shares([lax.rem(fs + d, groups) for d in pair])
        for k, d in enumerate(pair):
            share = both[k * tokens : (k + 1) * tokens]
            if d > 0:
                routed_v[lax.rem(fs + d, groups), :, :depth] = share.astype(BF)
                routed_copy(d).start()
            else:
                mixed = mixed + share
    for d in range(1, groups):
        routed_copy(d).wait_recv()
        mixed = mixed + routed_r[d][:, :depth].astype(F32)
    for j in range(peers):
        home_s[j, :, :depth] = mixed[j * own_rows : (j + 1) * own_rows, :]

    def home_copy(d):
        peer = place.plus(d)
        return remote(home_s.at[peer], home_r.at[me], home_sem.at[0], home_sem.at[1], peer)

    for d in FAR_FIRST:
        home_copy(d).start()
    home_r[me] = home_s[me]
    for s in heads + sums + gathers:
        s.finish()
    for d in range(1, groups):
        routed_copy(d).wait_send()
        group_copy(0, d, meta_v.at[fs]).wait_send()
        group_copy(1, d, x_v.at[fs]).wait_send()
        group_copy(2, d, sum_v.at[fs]).wait_send()

    all_copies(ssq_r, ssq_sem).wait_send()
    all_copies(meta_v.at[fs], meta_sem).wait_send()
    all_copies(res_s, res_sem).wait_send()
    all_copies(home_s, home_sem).wait_recv()
    for j in range(peers):
        out_ref[0, :, j * depth : (j + 1) * depth] = home_r[j][:, :depth]
    all_copies(home_s, home_sem).wait_send()


def shards(
    residual,
    gain,
    queries,
    new_keys,
    cache,
    lengths,
    w_value,
    w_out,
    w_gate,
    w_up,
    w_down,
    expert_ids,
    gates,
):
    peers = lax.axis_size("exp")
    groups = lax.axis_size("fsdp")
    group_rows, steps, _, key = queries.shape
    tokens = group_rows * steps
    experts, depth, half = w_gate.shape
    block = tokens * groups // peers
    rows = block * TOP
    smem, dma = pl.BlockSpec(memory_space=pltpu.SMEM), pltpu.SemaphoreType.DMA
    scratch = [
        pltpu.VMEM((peers, experts * block, 2 * half), BF),
        pltpu.VMEM(w_out.shape[1:], BF),
        pltpu.VMEM((w_out.shape[2], w_out.shape[1]), BF),
        pltpu.VMEM((peers, steps, WIDE), F32),
        pltpu.VMEM((peers, steps, WIDE), F32),
        pltpu.VMEM((tokens, key), BF),
        pltpu.VMEM((tokens, key), BF),
        pltpu.VMEM((tokens, tokens), F32),
        pltpu.VMEM((tokens, w_value.shape[1]), BF),
        pltpu.VMEM((peers, depth, tokens), BF),
        pltpu.VMEM((depth, tokens), F32),
        pltpu.VMEM((tokens, WIDE), F32),
        pltpu.VMEM((8, tokens), F32),
        pltpu.VMEM((peers, 8, tokens), F32),
        pltpu.VMEM((groups, 8, tokens), F32),
        pltpu.VMEM((groups, tokens, WIDE), BF),
        pltpu.VMEM((groups, peers, 8, rows), F32),
        pltpu.VMEM(w_gate.shape, BF),
        pltpu.VMEM(w_gate.shape, BF),
        pltpu.VMEM(w_gate.shape, BF),
        pltpu.VMEM((peers, rows, 2 * half), BF),
        pltpu.VMEM((rows, 2 * half), F32),
        pltpu.VMEM((peers, rows, half), BF),
        pltpu.VMEM((peers, experts * block, rows), BF),
        pltpu.VMEM((peers, 1, rows), jnp.int32),
        pltpu.VMEM((peers, 1, rows), F32),
        pltpu.VMEM((groups, tokens, WIDE), BF),
        pltpu.VMEM((groups, tokens, WIDE), BF),
        pltpu.VMEM((peers, steps, WIDE), F32),
        pltpu.VMEM((peers, steps, WIDE), F32),
        dma((len(ROUTES), 2)),
        dma,
        dma((3,)),
        dma((2,)),
        dma((2,)),
        dma((2,)),
        dma((2,)),
        dma((4, groups)),
        dma((4, groups)),
    ]
    for route in HEAD_ROUTES:
        scratch += reduce_scratch(route, tokens)
    for route in ROUTES:
        scratch += reduce_scratch(route, 2 * half)
    for route in ROUTES:
        scratch += gather_scratch(route)
    return pl.pallas_call(
        functools.partial(layer_kernel, peers, groups),
        out_shape=jax.ShapeDtypeStruct(residual.shape, F32),
        in_specs=[smem, vmem(), vmem(), anywhere(), vmem(), anywhere()]
        + [vmem()] * 4
        + [anywhere()] * 3,
        out_specs=vmem(),
        scratch_shapes=scratch,
        compiler_params=pltpu.CompilerParams(
            collective_id=0, has_side_effects=True, vmem_limit_bytes=HIGH
        ),
        name="layer",
    )(
        lengths,
        queries[:, :, 0, :],
        new_keys,
        cache,
        w_value[0],
        w_out[0],
        residual,
        gain.reshape(1, -1),
        expert_ids,
        gates,
        w_gate,
        w_up,
        w_down,
    )


def solution(mesh):
    return jax.shard_map(
        shards,
        mesh=mesh,
        in_specs=(
            P(("fsdp", "exp"), None, None),
            P(),
            P("fsdp", None, "exp", None),
            P("fsdp", None, None),
            P("fsdp", None, None),
            P("fsdp"),
            P("exp", None, None),
            P("exp", None, None),
            P(None, "exp", "fsdp"),
            P(None, "exp", "fsdp"),
            P(None, "exp", "fsdp"),
            P(("fsdp", "exp"), None, None),
            P(("fsdp", "exp"), None, None),
        ),
        out_specs=P(("fsdp", "exp"), None, None),
        check_vma=False,
    )
```

```python
import functools

import jax
import jax.numpy as jnp
from jax import lax
from jax.experimental import pallas as pl
from jax.experimental.pallas import tpu as pltpu
from jax.sharding import PartitionSpec as P

TOP = 8
STEPS = 4
score_scale = 0.07216878364870322
MESH = pl.DeviceIdType.MESH
BF = jnp.bfloat16
F32 = jnp.float32
WIDE = 256
HIGH = 60 * 1024 * 1024
NX, NZ, NY = 2, 4, 4
NT = (((1,), (1,)), ((), ()))


def matmul(a, b):
    return jnp.dot(a, b, preferred_element_type=F32)


def vmem():
    return pl.BlockSpec(memory_space=pltpu.VMEM)


def anywhere():
    return pl.BlockSpec(memory_space=pl.ANY)


def each(lower, upper, body):
    def step(i, carry):
        body(i)
        return carry

    lax.fori_loop(lower, upper, step, 0)


class Place:
    def __init__(self):
        self.me = lax.axis_index("exp")
        self.x = self.me // (NZ * NY)
        self.z = lax.rem(self.me // NY, NZ)
        self.y = lax.rem(self.me, NY)

    def index(self, x, z, y):
        return (lax.rem(x, NX) * NZ + lax.rem(z, NZ)) * NY + lax.rem(y, NY)

    def plus(self, offset):
        dx, dz, dy = offset
        return self.index(self.x + dx, self.z + dz, self.y + dy)

    def minus(self, offset):
        dx, dz, dy = offset
        return self.index(self.x + NX - dx, self.z + NZ - dz, self.y + NY - dy)


class Route:
    def __init__(self, kind, first, count):
        self.axes = {"z": (1, 2, 0), "y": (2, 0, 1), "x": (0, 1, 2)}[kind]
        self.n = tuple((NX, NZ, NY)[a] for a in self.axes)
        self.first, self.count = first, count
        self.rows = pl.ds(first, count)
        self.plane = self.n[1] * self.n[2]

    def offset(self, d1, d2, d3):
        out = [0, 0, 0]
        for a, d in zip(self.axes, (d1, d2, d3)):
            out[a] = d
        return tuple(out)

    def split(self, offset):
        return tuple(offset[a] for a in self.axes)


ROUTES = (Route("z", 0, 32), Route("y", 32, 48), Route("x", 80, 48))
HEAD_ROUTES = (Route("z", 0, 64), Route("y", 64, 80), Route("x", 144, 80))


def remote(src, dst, send, recv, peer):
    return pltpu.make_async_remote_copy(
        src_ref=src,
        dst_ref=dst,
        send_sem=send,
        recv_sem=recv,
        device_id={"exp": peer},
        device_id_type=MESH,
    )


class Reduce:
    def __init__(self, place, route, src, bufs):
        self.place, self.route, self.src = place, route, src
        self.got1, self.out1, self.got2, self.keep, self.out2, self.got3 = bufs[:6]
        self.sent, self.r1, self.r2 = bufs[6:]

    def first(self, d1, d2, d3):
        route = self.route
        g = d2 * route.n[2] + d3
        return remote(
            self.src.at[self.place.plus(route.offset(d1, d2, d3)), route.rows],
            self.got1.at[g, d1 - 1],
            self.sent.at[0],
            self.r1.at[g],
            self.place.plus(route.offset(d1, 0, 0)),
        )

    def second(self, d2, d3):
        return remote(
            self.out1.at[d2 * self.route.n[2] + d3],
            self.got2.at[d3, d2 - 1],
            self.sent.at[1],
            self.r2.at[d3],
            self.place.plus(self.route.offset(0, d2, 0)),
        )

    def third(self, d3):
        return remote(
            self.out2.at[d3],
            self.got3.at[d3 - 1],
            self.sent.at[2],
            self.r2.at[self.route.n[2]],
            self.place.plus(self.route.offset(0, 0, d3)),
        )

    def send(self, offset):
        d1, d2, d3 = self.route.split(offset)

        @pl.when(d1 > 0)
        def _():
            self.first(d1, d2, d3).start()

    def arrived(self, got, sem):
        remote(got, got, self.sent.at[0], sem, self.place.me).wait_recv()

    def step(self, g):
        route = self.route
        d2, d3 = g // route.n[2], lax.rem(g, route.n[2])
        self.arrived(self.got1.at[g], self.r1.at[g])
        total = self.src[self.place.plus(route.offset(0, d2, d3)), route.rows].astype(F32)
        for d in range(1, route.n[0]):
            total = total + self.got1[g, d - 1].astype(F32)

        @pl.when(d2 == 0)
        def _():
            self.keep[d3] = total

        @pl.when(d2 != 0)
        def _():
            self.out1[g] = total.astype(BF)
            self.second(d2, d3).start()

    def turn(self, d3):
        self.arrived(self.got2.at[d3], self.r2.at[d3])
        total = self.keep[d3]
        for d in range(1, self.route.n[1]):
            total = total + self.got2[d3, d - 1].astype(F32)
        return total

    def turns(self):
        for d3 in range(1, self.route.n[2]):
            self.out2[d3] = self.turn(d3).astype(BF)
            self.third(d3).start()
        self.keep[0] = self.turn(0)

    def add(self, acc_ref):
        self.arrived(self.got3, self.r2.at[self.route.n[2]])
        total = self.keep[0]
        for d in range(1, self.route.n[2]):
            total = total + self.got3[d - 1].astype(F32)
        acc_ref[self.route.rows] = total

    def finish(self):
        for n, got in enumerate((self.got1, self.got2, self.got3)):
            remote(got, got, self.sent.at[n], self.r2.at[0], self.place.me).wait_send()


def reduce_scratch(route, cols):
    n1, n2, n3 = route.n
    dma = pltpu.SemaphoreType.DMA
    return [
        pltpu.VMEM((n2 * n3, n1 - 1, route.count, cols), BF),
        pltpu.VMEM((n2 * n3, route.count, cols), BF),
        pltpu.VMEM((n3, n2 - 1, route.count, cols), BF),
        pltpu.VMEM((n3, route.count, cols), F32),
        pltpu.VMEM((n3, route.count, cols), BF),
        pltpu.VMEM((n3 - 1, route.count, cols), BF),
        dma((3,)),
        dma((n2 * n3,)),
        dma((n3 + 1,)),
    ]


class Gather:
    def __init__(self, place, route, whole, bufs):
        self.place, self.route, self.whole = place, route, whole
        self.sent, self.r = bufs

    def copy(self, source, to, offset):
        _, n2, n3 = self.route.n
        d1, d2, d3 = offset
        block = self.whole.at[source, self.route.rows]
        peer = self.place.plus(self.route.offset(*to))
        return remote(block, block, self.sent, self.r.at[(d1 * n2 + d2) * n3 + d3], peer)

    def source(self, *offset):
        return self.place.minus(self.route.offset(*offset))

    def push1(self, d2, d3):
        for d in sorted(range(1, self.route.n[0]), key=lambda d: d != 2):
            self.copy(self.source(0, d2, d3), (d, 0, 0), (d, d2, d3)).start()

    def push2(self, d3):
        for d in range(1, self.route.n[1]):
            self.copy(self.source(0, 0, d3), (0, d, 0), (0, d, d3)).start()

    def begin(self):
        for d in range(1, self.route.n[2]):
            self.copy(self.place.me, (0, 0, d), (0, 0, d)).start()
        self.push2(0)
        self.push1(0, 0)

    def wait(self, offset):
        self.copy(self.source(*offset), (0, 0, 0), offset).wait_recv()

    def relay_last(self, d3):
        self.wait((0, 0, d3))
        self.push2(d3)
        self.push1(0, d3)

    def relay_middle(self, g):
        d2, d3 = g // self.route.n[2], lax.rem(g, self.route.n[2])
        self.wait((0, d2, d3))
        self.push1(d2, d3)

    def arrive(self, offset):
        split = self.route.split(offset)

        @pl.when(split[0] > 0)
        def _():
            self.wait(split)

    def finish(self):
        n1, n2, n3 = self.route.n
        blocks = self.whole.at[pl.ds(0, n1 * n2 * n3 - 1), self.route.rows]
        remote(blocks, blocks, self.sent, self.r.at[0], self.place.me).wait_send()


def gather_scratch(route):
    dma = pltpu.SemaphoreType.DMA
    return [dma, dma((route.n[0] * route.n[1] * route.n[2],))]


def offset_of_int(o):
    return (o // (NZ * NY), o // NY % NZ, o % NY)


def offset_of(o):
    return (o // (NZ * NY), lax.rem(o // NY, NZ), lax.rem(o, NY))


def hops(offset):
    dx, dz, dy = offset
    return 2 * dx + min(dz, NZ - dz) + min(dy, NY - dy)


FAR_FIRST = sorted((offset_of_int(o) for o in range(1, NX * NZ * NY)), key=hops, reverse=True)


def spread(block, lanes):
    wide = jnp.concatenate([block] * (lanes // block.shape[1]), axis=1)
    step = lax.rem(lax.broadcasted_iota(jnp.int32, wide.shape, 1) // TOP, STEPS)
    row = lax.broadcasted_iota(jnp.int32, wide.shape, 0)
    return jnp.sum(jnp.where(step == row, wide, 0.0), 0, keepdims=True)


def layer_kernel(peers, groups, *refs):
    (
        len_ref,
        q_ref,
        nk_ref,
        cache_ref,
        wv_ref,
        wo_ref,
        res_ref,
        gain_ref,
        ids_ref,
        gates_ref,
        wg_ref,
        wu_ref,
        wd_ref,
        out_ref,
        dense,
        wo_v,
        wo_t,
        res_s,
        res_r,
        q_s,
        nk_s,
        new_s,
        ctx_s,
        send_v,
        att_t,
        att,
        ssq_s,
        ssq_r,
        sum_v,
        x_v,
        meta_v,
        wg_v,
        wu_v,
        wd_v,
        part_v,
        acc,
        hid_v,
        spread_s,
        code_s,
        gate_s,
        routed_v,
        routed_r,
        home_s,
        home_r,
        cache_sem,
        wo_sem,
        w_sem,
        ssq_sem,
        meta_sem,
        res_sem,
        home_sem,
        g_send,
        g_recv,
    ) = refs[:53]
    place = Place()
    me = place.me
    fs = lax.axis_index("fsdp")
    tokens = q_s.shape[0]
    latent = wv_ref.shape[0]
    experts, depth, half = wg_ref.shape
    rows = part_v.shape[1]
    block = rows // TOP
    per = peers // groups
    own_rows = home_s.shape[1]
    barrier = pltpu.get_barrier_semaphore()

    def greet(axis, mine, size):
        def one(d):
            pl.semaphore_signal(
                barrier, inc=1, device_id={axis: lax.rem(mine + d, size)}, device_id_type=MESH
            )

        each(1, size, one)

    greet("exp", me, peers)
    greet("fsdp", fs, groups)
    rest = refs[53:]
    heads = [
        Reduce(place, r, send_v, rest[9 * i : 9 * i + 9]) for i, r in enumerate(HEAD_ROUTES)
    ]
    rest = rest[9 * len(ROUTES) :]
    sums = [Reduce(place, r, part_v, rest[9 * i : 9 * i + 9]) for i, r in enumerate(ROUTES)]
    rest = rest[9 * len(ROUTES) :]
    gathers = [Gather(place, r, hid_v, rest[2 * i : 2 * i + 2]) for i, r in enumerate(ROUTES)]

    def group_copy(n, d, block_ref):
        return pltpu.make_async_remote_copy(
            src_ref=block_ref,
            dst_ref=block_ref,
            send_sem=g_send.at[n, d],
            recv_sem=g_recv.at[n, d],
            device_id={"fsdp": lax.rem(fs + d, groups)},
            device_id_type=MESH,
        )

    def from_group(d):
        return lax.rem(fs + groups - d, groups)

    def cache_copy(i, n):
        span = pl.ds(ROUTES[i].first // STEPS, ROUTES[i].count // STEPS)
        positions = cache_ref.shape[2]
        if n == 0:
            src = cache_ref.at[span, pl.ds(0, latent)]
            dst = dense.at[span, pl.ds(0, latent), pl.ds(0, positions)]
        else:
            left = cache_ref.shape[1] - latent
            src = cache_ref.at[span, pl.ds(latent, left)]
            dst = dense.at[span, pl.ds(0, left), pl.ds(positions, positions)]
        return pltpu.make_async_copy(src, dst, cache_sem.at[i, n])

    def weight_copy(n):
        src = (wg_ref, wu_ref, wd_ref)[n]
        dst = (wg_v, wu_v, wd_v)[n]
        return pltpu.make_async_copy(src, dst, w_sem.at[n])

    out_copy = pltpu.make_async_copy(wo_ref, wo_v, wo_sem)
    for n in range(2):
        cache_copy(0, n).start()
    out_copy.start()
    for i in range(1, len(ROUTES)):
        for n in range(2):
            cache_copy(i, n).start()

    for b in range(tokens // 16):
        span = slice(b * 16, b * 16 + 16)
        q_s[span, :] = jnp.concatenate(
            [q_ref[4 * b + i].astype(F32) for i in range(4)], axis=0
        ).astype(BF)
        nk_s[span, :] = jnp.concatenate(
            [nk_ref[4 * b + i].astype(F32) for i in range(4)], axis=0
        ).astype(BF)

    token_r = lax.broadcasted_iota(jnp.int32, (tokens, tokens), 0)
    token_c = lax.broadcasted_iota(jnp.int32, (tokens, tokens), 1)
    diagonal = token_r == token_c
    same = (token_r // STEPS == token_c // STEPS) & (token_c <= token_r)
    fresh = lax.dot_general(q_s[...], nk_s[...], NT, preferred_element_type=F32)
    new_s[...] = jnp.where(same, fresh * score_scale, -1e30)

    which = lax.broadcasted_iota(jnp.int32, (16, 1), 0) // STEPS
    position = lax.broadcasted_iota(jnp.int32, (16, cache_ref.shape[2]), 1)
    rope = cache_ref.shape[1] - latent

    def attend(b):
        span = pl.ds(pl.multiple_of(b * 16, 16), 16)
        first = b * 4
        q16 = q_s[span, :]

        def score(row):
            return matmul(q16[:, :latent], dense[row, :, : position.shape[1]]) + matmul(
                q16[:, latent:], dense[row, :rope, position.shape[1] :]
            )

        scores = score(first)
        length = jnp.full(position.shape, len_ref[first])
        for n in range(1, 4):
            scores = jnp.where(which == n, score(first + n), scores)
            length = jnp.where(which == n, len_ref[first + n], length)
        scores = jnp.where(position < length, scores * score_scale, -1e30)
        new = new_s[span, :]
        highest = jnp.maximum(jnp.max(scores, -1, keepdims=True), jnp.max(new, -1, keepdims=True))
        cache_exp = jnp.exp(scores - highest)
        new_exp = jnp.exp(new - highest)
        total = jnp.sum(cache_exp, -1, keepdims=True) + jnp.sum(new_exp, -1, keepdims=True)
        cache_w = (cache_exp / total).astype(BF)
        new_w = (new_exp / total).astype(BF)

        def mix(row):
            return lax.dot_general(
                cache_w, dense[row, :, : position.shape[1]], NT, preferred_element_type=F32
            )

        context = mix(first)
        for n in range(1, 4):
            context = jnp.where(which == n, mix(first + n), context)
        context = context + matmul(new_w, nk_s[:, :latent])
        ctx_s[span, :] = context.astype(BF)

    def meta_copy(d):
        tile = meta_v.at[fs, me]
        return remote(tile, tile, meta_sem.at[0], meta_sem.at[1], place.plus(d))

    def all_copies(buffer, sem):
        tiles = buffer.at[pl.ds(0, peers - 1)]
        return remote(tiles, tiles, sem.at[0], sem.at[1], me)

    for i, route in enumerate(ROUTES):
        for n in range(2):
            cache_copy(i, n).wait()
        each(route.first // 16, (route.first + route.count) // 16, attend)
        if i == 0:
            for n in range(3):
                weight_copy(n).start()

    out_copy.wait()
    for c in range(wo_v.shape[1] // 128):
        span = slice(c * 128, c * 128 + 128)
        wo_t[span, :] = wo_v[:, span].T
    gain = jnp.zeros((1, depth), F32)
    for j in range(peers):
        part = slice(j * depth, (j + 1) * depth)
        res_s[j, :, :depth] = res_ref[0, :, part].astype(F32)
        gain = jnp.where(me == j, gain_ref[:, part], gain)
    gain = jnp.concatenate([gain, jnp.zeros((1, WIDE - depth), F32)], axis=1)
    lane = lax.broadcasted_iota(jnp.int32, (1, rows), 1)
    here = lane // (STEPS * TOP) == lax.rem(me, 4)
    own_ids = jnp.where(here, spread(ids_ref[0].astype(F32), rows), 0.0)
    own_gates = jnp.where(here, spread(gates_ref[0], rows), 0.0)
    meta_v[fs, me] = jnp.concatenate([own_ids, own_gates, jnp.zeros((6, rows), F32)], axis=0)
    values = matmul(ctx_s[...], wv_ref[...]).astype(BF)
    pl.semaphore_wait(barrier, peers - 1 + groups - 1)

    def project(n):
        offsets = [offset_of(4 * n + k) for k in range(4)]
        for offset in offsets:
            j = place.plus(offset)
            span = pl.ds(pl.multiple_of(j * depth, 16), depth)
            part = lax.dot_general(wo_t[span, :], values, NT, preferred_element_type=F32)
            send_v[j] = part.astype(BF)
        for offset in offsets:
            for h in heads:
                h.send(offset)

    each(0, peers // 4, project)

    def res_copy(d):
        peer = place.plus(d)
        return remote(res_s.at[peer], res_r.at[me], res_sem.at[0], res_sem.at[1], peer)

    for d in FAR_FIRST:
        meta_copy(d).start()
        res_copy(d).start()
    res_r[me] = res_s[me]

    for h in heads:
        each(h.route.n[2], h.route.plane, h.step)
    for h in heads:
        each(0, h.route.n[2], h.step)
    pair_lane = lax.broadcasted_iota(jnp.int32, (1, rows), 1)
    slot_c = lax.broadcasted_iota(jnp.int32, (rows, experts * block), 1)
    slot_r = lax.broadcasted_iota(jnp.int32, (experts * block, rows), 0)

    def read_meta(q):
        piece = from_group(q)

        def one(n):
            info = meta_v[piece, 4 * n]
            for i in range(1, 4):
                info = info + meta_v[piece, 4 * n + i]
            j = piece * per + n
            code = info[0:1, :].astype(jnp.int32) * block + pair_lane // TOP
            code_s[j] = code
            code = jnp.sum(jnp.where(diagonal, code, 0), 1, keepdims=True)
            part_v[j] = (code == slot_c).astype(F32).astype(BF)
            gate_s[j] = info[1:2, :]

        each(0, per, one)

    for h in heads:
        h.turns()
    all_copies(meta_v.at[fs], meta_sem).wait_recv()
    for d in range(1, groups):
        group_copy(0, d, meta_v.at[fs]).start()
    read_meta(0)
    for h in heads:
        h.add(att_t)
    all_copies(res_s, res_sem).wait_recv()

    attended = jnp.concatenate([att_t[...], jnp.zeros((WIDE - depth, tokens), F32)], axis=0).T
    own_res = jnp.concatenate([res_r[n][:, :depth] for n in range(peers)], axis=0)
    own_res = jnp.concatenate([own_res, jnp.zeros((tokens, WIDE - depth), F32)], axis=1)
    attended = attended + own_res
    att[...] = attended
    x_v[fs] = (attended * gain).astype(BF)
    for d in range(1, groups):
        group_copy(1, d, x_v.at[fs]).start()
    column = jnp.sum(attended * attended, -1, keepdims=True)
    row = jnp.sum(jnp.where(diagonal, column, 0.0), 0, keepdims=True)
    ssq_s[...] = jnp.broadcast_to(row, ssq_s.shape)

    def ssq_copy(d):
        return remote(ssq_s, ssq_r.at[d], ssq_sem.at[0], ssq_sem.at[1], lax.rem(me + d, peers))

    ssq_r[0] = ssq_s[...]
    each(1, peers, lambda d: ssq_copy(d).start())

    def multiply(first, count, x):
        def some(n):
            for e in [4 * n + k for k in range(4)]:
                spot = pl.ds(pl.multiple_of(e * block, block), block)
                gate = matmul(x, wg_v[e]).astype(BF)
                up = matmul(x, wu_v[e]).astype(BF)
                dense[first : first + count, spot, :half] = gate.reshape(count, block, half)
                dense[first : first + count, spot, half:] = up.reshape(count, block, half)

        each(0, experts // 4, some)

    def pick(i):
        found = []
        for k in range(2):
            q = (2 * i + k) // per
            n = lax.rem((2 * i + k) // NY, 2) * NY + lax.rem(place.y + 2 * i + k, NY)
            j = from_group(q) * per + n
            found.append((j, matmul(part_v[j], dense[q * per + n]).astype(BF)))
        for j, part in found:
            part_v[j] = part
        for j, _ in found:
            offset = (
                lax.rem(j // (NZ * NY) + NX - place.x, NX),
                lax.rem(lax.rem(j // NY, NZ) + NZ - place.z, NZ),
                lax.rem(lax.rem(j, NY) + NY - place.y, NY),
            )
            for s in sums:
                s.send(offset)

    def pick_group(q):
        each(q * per // 2, (q + 1) * per // 2, pick)

    def relay(q):
        p = from_group(q)
        x_off = lax.rem(p // 2 + NX - place.x, NX)
        z_low = 2 * lax.rem(p, 2)

        def z_off(i):
            return lax.rem(z_low + i + NZ - place.z, NZ)

        @pl.when(lax.rem(p, 2) == place.z // 2)
        def _():
            each(0, NY, lambda i: sums[0].step(i * NX + x_off))

        each(0, 2, lambda i: sums[1].step(x_off * NZ + z_off(i)))

        @pl.when(x_off == 0)
        def _():
            each(0, 2 * NY, lambda i: sums[2].step(z_off(i // NY) * NY + lax.rem(i, NY)))

    weight_copy(0).wait()
    weight_copy(1).wait()
    multiply(0, per, x_v[fs][:, :depth])
    pick_group(0)

    for q in range(1, groups):
        group_copy(0, q, meta_v.at[from_group(q)]).wait_recv()
        group_copy(1, q, x_v.at[from_group(q)]).wait_recv()
        read_meta(q)
    others = [x_v[from_group(q)][:, :depth] for q in range(1, groups)]
    multiply(per, peers - per, jnp.concatenate(others, axis=0))
    pick_group(1)
    relay(0)
    pick_group(2)
    pick_group(3)
    relay(1)
    all_copies(ssq_r.at[pl.ds(1, peers - 1)], ssq_sem).wait_recv()
    sum_v[fs] = jnp.sum(ssq_r[...], axis=0)
    for d in range(1, groups):
        group_copy(2, d, sum_v.at[fs]).start()
    relay(2)
    relay(3)

    for s in sums:
        s.turns()

    def build(n):
        for j in (2 * n, 2 * n + 1):
            spread_s[j] = (code_s[j] == slot_r).astype(F32).astype(BF)

    each(0, peers // 2, build)
    for s in sums:
        s.add(acc)

    for d in range(1, groups):
        group_copy(2, d, sum_v.at[from_group(d)]).wait_recv()
    token = block * lax.rem(me, per) + token_r // TOP
    squares = jnp.sum(jnp.where(token == token_c, sum_v[me // per][:1, :], 0.0), 1, keepdims=True)
    scale = lax.rsqrt(squares / (depth * peers) + 1e-06)
    weight = jnp.sum(jnp.where(diagonal, gate_s[me], 0.0), 1, keepdims=True)
    gate = acc[:, :half] * scale
    up = acc[:, half:] * scale
    hid_v[me] = (gate / (1.0 + jnp.exp(-gate)) * up * weight).astype(BF)

    for g in gathers:
        g.begin()
    for g in gathers:
        for d3 in range(1, g.route.n[2]):
            g.relay_last(d3)
    for g in gathers:
        each(g.route.n[2], g.route.plane, g.relay_middle)

    def expand(n):
        offsets = [offset_of(2 * n), offset_of(2 * n + 1)]
        for offset in offsets:
            for g in gathers:
                g.arrive(offset)
        blocks = [place.minus(offset) for offset in offsets]
        full = [matmul(spread_s[j], hid_v[j]).astype(BF) for j in blocks]
        for j, rows_of in zip(blocks, full):
            spot = pl.ds(pl.multiple_of(j * block, block), block)
            dense[:, spot, :half] = rows_of.reshape(experts, block, half)

    each(0, peers // 2, expand)
    weight_copy(2).wait()

    def shares(pieces):
        spots = [pl.ds(pl.multiple_of(p * tokens, tokens), tokens) for p in pieces]

        def some(n, total):
            for k in range(4):
                e = 4 * n + k
                both = jnp.concatenate([dense[e, spot, :half] for spot in spots], axis=0)
                total = total + lax.dot_general(both, wd_v[e], NT, preferred_element_type=F32)
            return total

        start = jnp.zeros((len(pieces) * tokens, depth), F32)
        return lax.fori_loop(0, experts // 4, some, start)

    def routed_copy(d):
        peer = lax.rem(fs + d, groups)
        return pltpu.make_async_remote_copy(
            src_ref=routed_v.at[peer],
            dst_ref=routed_r.at[d],
            send_sem=g_send.at[3, d],
            recv_sem=g_recv.at[3, d],
            device_id={"fsdp": peer},
            device_id_type=MESH,
        )

    mixed = att[:, :depth]
    odd = lax.rem(fs, 2)
    for pair in ((2, 3 - 2 * odd), (1 + 2 * odd, None)):
        pieces = [fs if d is None else lax.rem(fs + d, groups) for d in pair]
        both = shares(pieces)
        for k, d in enumerate(pair):
            share = both[k * tokens : (k + 1) * tokens]
            if d is None:
                mixed = mixed + share
            else:
                routed_v[pieces[k], :, :depth] = share.astype(BF)
                routed_copy(d).start()
    for d in range(1, groups):
        routed_copy(d).wait_recv()
        mixed = mixed + routed_r[d][:, :depth].astype(F32)
    for j in range(peers):
        home_s[j, :, :depth] = mixed[j * own_rows : (j + 1) * own_rows, :]

    def home_copy(d):
        peer = place.plus(d)
        return remote(home_s.at[peer], home_r.at[me], home_sem.at[0], home_sem.at[1], peer)

    for d in FAR_FIRST:
        home_copy(d).start()
    home_r[me] = home_s[me]
    for s in heads + sums + gathers:
        s.finish()
    for d in range(1, groups):
        routed_copy(d).wait_send()
        group_copy(0, d, meta_v.at[fs]).wait_send()
        group_copy(1, d, x_v.at[fs]).wait_send()
        group_copy(2, d, sum_v.at[fs]).wait_send()

    all_copies(ssq_r, ssq_sem).wait_send()
    all_copies(meta_v.at[fs], meta_sem).wait_send()
    all_copies(res_s, res_sem).wait_send()
    all_copies(home_s, home_sem).wait_recv()
    for j in range(peers):
        out_ref[0, :, j * depth : (j + 1) * depth] = home_r[j][:, :depth]
    all_copies(home_s, home_sem).wait_send()


def shards(
    residual,
    gain,
    queries,
    new_keys,
    cache,
    lengths,
    w_value,
    w_out,
    w_gate,
    w_up,
    w_down,
    expert_ids,
    gates,
):
    peers = lax.axis_size("exp")
    groups = lax.axis_size("fsdp")
    group_rows, steps, _, key = queries.shape
    tokens = group_rows * steps
    experts, depth, half = w_gate.shape
    block = tokens * groups // peers
    rows = block * TOP
    smem, dma = pl.BlockSpec(memory_space=pltpu.SMEM), pltpu.SemaphoreType.DMA
    scratch = [
        pltpu.VMEM((peers, experts * block, 2 * half), BF),
        pltpu.VMEM(w_out.shape[1:], BF),
        pltpu.VMEM((w_out.shape[2], w_out.shape[1]), BF),
        pltpu.VMEM((peers, steps, WIDE), F32),
        pltpu.VMEM((peers, steps, WIDE), F32),
        pltpu.VMEM((tokens, key), BF),
        pltpu.VMEM((tokens, key), BF),
        pltpu.VMEM((tokens, tokens), F32),
        pltpu.VMEM((tokens, w_value.shape[1]), BF),
        pltpu.VMEM((peers, depth, tokens), BF),
        pltpu.VMEM((depth, tokens), F32),
        pltpu.VMEM((tokens, WIDE), F32),
        pltpu.VMEM((8, tokens), F32),
        pltpu.VMEM((peers, 8, tokens), F32),
        pltpu.VMEM((groups, 8, tokens), F32),
        pltpu.VMEM((groups, tokens, WIDE), BF),
        pltpu.VMEM((groups, peers, 8, rows), F32),
        pltpu.VMEM(w_gate.shape, BF),
        pltpu.VMEM(w_gate.shape, BF),
        pltpu.VMEM(w_gate.shape, BF),
        pltpu.VMEM((peers, rows, 2 * half), BF),
        pltpu.VMEM((rows, 2 * half), F32),
        pltpu.VMEM((peers, rows, half), BF),
        pltpu.VMEM((peers, experts * block, rows), BF),
        pltpu.VMEM((peers, 1, rows), jnp.int32),
        pltpu.VMEM((peers, 1, rows), F32),
        pltpu.VMEM((groups, tokens, WIDE), BF),
        pltpu.VMEM((groups, tokens, WIDE), BF),
        pltpu.VMEM((peers, steps, WIDE), F32),
        pltpu.VMEM((peers, steps, WIDE), F32),
        dma((len(ROUTES), 2)),
        dma,
        dma((3,)),
        dma((2,)),
        dma((2,)),
        dma((2,)),
        dma((2,)),
        dma((4, groups)),
        dma((4, groups)),
    ]
    for route in HEAD_ROUTES:
        scratch += reduce_scratch(route, tokens)
    for route in ROUTES:
        scratch += reduce_scratch(route, 2 * half)
    for route in ROUTES:
        scratch += gather_scratch(route)
    return pl.pallas_call(
        functools.partial(layer_kernel, peers, groups),
        out_shape=jax.ShapeDtypeStruct(residual.shape, F32),
        in_specs=[smem, vmem(), vmem(), anywhere(), vmem(), anywhere()]
        + [vmem()] * 4
        + [anywhere()] * 3,
        out_specs=vmem(),
        scratch_shapes=scratch,
        compiler_params=pltpu.CompilerParams(
            collective_id=0, has_side_effects=True, vmem_limit_bytes=HIGH
        ),
        name="layer",
    )(
        lengths,
        queries[:, :, 0, :],
        new_keys,
        cache,
        w_value[0],
        w_out[0],
        residual,
        gain.reshape(1, -1),
        expert_ids,
        gates,
        w_gate,
        w_up,
        w_down,
    )


def solution(mesh):
    return jax.shard_map(
        shards,
        mesh=mesh,
        in_specs=(
            P(("fsdp", "exp"), None, None),
            P(),
            P("fsdp", None, "exp", None),
            P("fsdp", None, None),
            P("fsdp", None, None),
            P("fsdp"),
            P("exp", None, None),
            P("exp", None, None),
            P(None, "exp", "fsdp"),
            P(None, "exp", "fsdp"),
            P(None, "exp", "fsdp"),
            P(("fsdp", "exp"), None, None),
            P(("fsdp", "exp"), None, None),
        ),
        out_specs=P(("fsdp", "exp"), None, None),
        check_vma=False,
    )
```

```python
import functools

import jax
import jax.numpy as jnp
from jax import lax
from jax.experimental import pallas as pl
from jax.experimental.pallas import tpu as pltpu
from jax.sharding import PartitionSpec as P

TOP = 8
STEPS = 4
score_scale = 0.07216878364870322
MESH = pl.DeviceIdType.MESH
BF = jnp.bfloat16
F32 = jnp.float32
WIDE = 256
HIGH = 60 * 1024 * 1024
NX, NZ, NY = 2, 4, 4
NT = (((1,), (1,)), ((), ()))


def matmul(a, b):
    return jnp.dot(a, b, preferred_element_type=F32)


def vmem():
    return pl.BlockSpec(memory_space=pltpu.VMEM)


def anywhere():
    return pl.BlockSpec(memory_space=pl.ANY)


def each(lower, upper, body):
    def step(i, carry):
        body(i)
        return carry

    lax.fori_loop(lower, upper, step, 0)


class Place:
    def __init__(self):
        self.me = lax.axis_index("exp")
        self.x = self.me // (NZ * NY)
        self.z = lax.rem(self.me // NY, NZ)
        self.y = lax.rem(self.me, NY)

    def index(self, x, z, y):
        return (lax.rem(x, NX) * NZ + lax.rem(z, NZ)) * NY + lax.rem(y, NY)

    def plus(self, offset):
        dx, dz, dy = offset
        return self.index(self.x + dx, self.z + dz, self.y + dy)

    def minus(self, offset):
        dx, dz, dy = offset
        return self.index(self.x + NX - dx, self.z + NZ - dz, self.y + NY - dy)


class Route:
    def __init__(self, kind, first, count):
        self.axes = {"z": (1, 2, 0), "y": (2, 0, 1), "x": (0, 1, 2)}[kind]
        self.n = tuple((NX, NZ, NY)[a] for a in self.axes)
        self.first, self.count = first, count
        self.rows = pl.ds(first, count)
        self.plane = self.n[1] * self.n[2]

    def offset(self, d1, d2, d3):
        out = [0, 0, 0]
        for a, d in zip(self.axes, (d1, d2, d3)):
            out[a] = d
        return tuple(out)

    def split(self, offset):
        return tuple(offset[a] for a in self.axes)


ROUTES = (Route("z", 0, 32), Route("y", 32, 48), Route("x", 80, 48))
HEAD_ROUTES = (Route("z", 0, 64), Route("y", 64, 80), Route("x", 144, 80))


def remote(src, dst, send, recv, peer):
    return pltpu.make_async_remote_copy(
        src_ref=src,
        dst_ref=dst,
        send_sem=send,
        recv_sem=recv,
        device_id={"exp": peer},
        device_id_type=MESH,
    )


class Reduce:
    def __init__(self, place, route, src, bufs):
        self.place, self.route, self.src = place, route, src
        self.got1, self.out1, self.got2, self.keep, self.out2, self.got3 = bufs[:6]
        self.sent, self.r1, self.r2 = bufs[6:]

    def first(self, d1, d2, d3):
        route = self.route
        g = d2 * route.n[2] + d3
        return remote(
            self.src.at[self.place.plus(route.offset(d1, d2, d3)), route.rows],
            self.got1.at[g, d1 - 1],
            self.sent.at[0],
            self.r1.at[g],
            self.place.plus(route.offset(d1, 0, 0)),
        )

    def second(self, d2, d3):
        return remote(
            self.out1.at[d2 * self.route.n[2] + d3],
            self.got2.at[d3, d2 - 1],
            self.sent.at[1],
            self.r2.at[d3],
            self.place.plus(self.route.offset(0, d2, 0)),
        )

    def third(self, d3):
        return remote(
            self.out2.at[d3],
            self.got3.at[d3 - 1],
            self.sent.at[2],
            self.r2.at[self.route.n[2]],
            self.place.plus(self.route.offset(0, 0, d3)),
        )

    def send(self, offset):
        d1, d2, d3 = self.route.split(offset)

        @pl.when(d1 > 0)
        def _():
            self.first(d1, d2, d3).start()

    def arrived(self, got, sem):
        remote(got, got, self.sent.at[0], sem, self.place.me).wait_recv()

    def step(self, g):
        route = self.route
        d2, d3 = g // route.n[2], lax.rem(g, route.n[2])
        self.arrived(self.got1.at[g], self.r1.at[g])
        total = self.src[self.place.plus(route.offset(0, d2, d3)), route.rows].astype(F32)
        for d in range(1, route.n[0]):
            total = total + self.got1[g, d - 1].astype(F32)

        @pl.when(d2 == 0)
        def _():
            self.keep[d3] = total

        @pl.when(d2 != 0)
        def _():
            self.out1[g] = total.astype(BF)
            self.second(d2, d3).start()

    def turn(self, d3):
        self.arrived(self.got2.at[d3], self.r2.at[d3])
        total = self.keep[d3]
        for d in range(1, self.route.n[1]):
            total = total + self.got2[d3, d - 1].astype(F32)
        return total

    def turns(self):
        for d3 in range(1, self.route.n[2]):
            self.out2[d3] = self.turn(d3).astype(BF)
            self.third(d3).start()
        self.keep[0] = self.turn(0)

    def add(self, acc_ref):
        self.arrived(self.got3, self.r2.at[self.route.n[2]])
        total = self.keep[0]
        for d in range(1, self.route.n[2]):
            total = total + self.got3[d - 1].astype(F32)
        acc_ref[self.route.rows] = total

    def finish(self):
        for n, got in enumerate((self.got1, self.got2, self.got3)):
            remote(got, got, self.sent.at[n], self.r2.at[0], self.place.me).wait_send()


def reduce_scratch(route, cols):
    n1, n2, n3 = route.n
    dma = pltpu.SemaphoreType.DMA
    return [
        pltpu.VMEM((n2 * n3, n1 - 1, route.count, cols), BF),
        pltpu.VMEM((n2 * n3, route.count, cols), BF),
        pltpu.VMEM((n3, n2 - 1, route.count, cols), BF),
        pltpu.VMEM((n3, route.count, cols), F32),
        pltpu.VMEM((n3, route.count, cols), BF),
        pltpu.VMEM((n3 - 1, route.count, cols), BF),
        dma((3,)),
        dma((n2 * n3,)),
        dma((n3 + 1,)),
    ]


class Gather:
    def __init__(self, place, route, whole, bufs):
        self.place, self.route, self.whole = place, route, whole
        self.sent, self.r = bufs

    def copy(self, source, to, offset):
        _, n2, n3 = self.route.n
        d1, d2, d3 = offset
        block = self.whole.at[source, self.route.rows]
        peer = self.place.plus(self.route.offset(*to))
        return remote(block, block, self.sent, self.r.at[(d1 * n2 + d2) * n3 + d3], peer)

    def source(self, *offset):
        return self.place.minus(self.route.offset(*offset))

    def push1(self, d2, d3):
        for d in sorted(range(1, self.route.n[0]), key=lambda d: d != 2):
            self.copy(self.source(0, d2, d3), (d, 0, 0), (d, d2, d3)).start()

    def push2(self, d3):
        for d in range(1, self.route.n[1]):
            self.copy(self.source(0, 0, d3), (0, d, 0), (0, d, d3)).start()

    def begin(self):
        for d in range(1, self.route.n[2]):
            self.copy(self.place.me, (0, 0, d), (0, 0, d)).start()

    def wait(self, offset):
        self.copy(self.source(*offset), (0, 0, 0), offset).wait_recv()

    def relay_last(self, d3):
        self.wait((0, 0, d3))
        self.push2(d3)
        self.push1(0, d3)

    def relay_middle(self, g):
        d2, d3 = g // self.route.n[2], lax.rem(g, self.route.n[2])
        self.wait((0, d2, d3))
        self.push1(d2, d3)

    def arrive(self, offset):
        split = self.route.split(offset)

        @pl.when(split[0] > 0)
        def _():
            self.wait(split)

    def finish(self):
        n1, n2, n3 = self.route.n
        blocks = self.whole.at[pl.ds(0, n1 * n2 * n3 - 1), self.route.rows]
        remote(blocks, blocks, self.sent, self.r.at[0], self.place.me).wait_send()


def gather_scratch(route):
    dma = pltpu.SemaphoreType.DMA
    return [dma, dma((route.n[0] * route.n[1] * route.n[2],))]


def offset_of_int(o):
    return (o // (NZ * NY), o // NY % NZ, o % NY)


def offset_of(o):
    return (o // (NZ * NY), lax.rem(o // NY, NZ), lax.rem(o, NY))


def hops(offset):
    dx, dz, dy = offset
    return 2 * dx + min(dz, NZ - dz) + min(dy, NY - dy)


FAR_FIRST = sorted((offset_of_int(o) for o in range(1, NX * NZ * NY)), key=hops, reverse=True)


def spread(block, lanes):
    wide = jnp.concatenate([block] * (lanes // block.shape[1]), axis=1)
    step = lax.rem(lax.broadcasted_iota(jnp.int32, wide.shape, 1) // TOP, STEPS)
    row = lax.broadcasted_iota(jnp.int32, wide.shape, 0)
    return jnp.sum(jnp.where(step == row, wide, 0.0), 0, keepdims=True)


def layer_kernel(peers, groups, *refs):
    (
        len_ref,
        q_ref,
        nk_ref,
        cache_ref,
        wv_ref,
        wo_ref,
        res_ref,
        gain_ref,
        ids_ref,
        gates_ref,
        wg_ref,
        wu_ref,
        wd_ref,
        out_ref,
        dense,
        wo_v,
        wo_t,
        res_s,
        res_r,
        q_s,
        nk_s,
        new_s,
        ctx_s,
        send_v,
        att_t,
        att,
        ssq_s,
        ssq_r,
        sum_v,
        x_v,
        meta_v,
        wg_v,
        wu_v,
        wd_v,
        part_v,
        acc,
        hid_v,
        spread_s,
        code_s,
        gate_s,
        routed_v,
        routed_r,
        home_s,
        home_r,
        cache_sem,
        wo_sem,
        w_sem,
        ssq_sem,
        meta_sem,
        res_sem,
        home_sem,
        g_send,
        g_recv,
    ) = refs[:53]
    place = Place()
    me = place.me
    fs = lax.axis_index("fsdp")
    tokens = q_s.shape[0]
    latent = wv_ref.shape[0]
    experts, depth, half = wg_ref.shape
    rows = part_v.shape[1]
    block = rows // TOP
    per = peers // groups
    own_rows = home_s.shape[1]
    barrier = pltpu.get_barrier_semaphore()

    def greet(axis, mine, size):
        def one(d):
            pl.semaphore_signal(
                barrier, inc=1, device_id={axis: lax.rem(mine + d, size)}, device_id_type=MESH
            )

        each(1, size, one)

    greet("exp", me, peers)
    greet("fsdp", fs, groups)
    rest = refs[53:]
    heads = [
        Reduce(place, r, send_v, rest[9 * i : 9 * i + 9]) for i, r in enumerate(HEAD_ROUTES)
    ]
    rest = rest[9 * len(ROUTES) :]
    sums = [Reduce(place, r, part_v, rest[9 * i : 9 * i + 9]) for i, r in enumerate(ROUTES)]
    rest = rest[9 * len(ROUTES) :]
    gathers = [Gather(place, r, hid_v, rest[2 * i : 2 * i + 2]) for i, r in enumerate(ROUTES)]

    def group_copy(n, d, block_ref):
        return pltpu.make_async_remote_copy(
            src_ref=block_ref,
            dst_ref=block_ref,
            send_sem=g_send.at[n, d],
            recv_sem=g_recv.at[n, d],
            device_id={"fsdp": lax.rem(fs + d, groups)},
            device_id_type=MESH,
        )

    def from_group(d):
        return lax.rem(fs + groups - d, groups)

    def cache_copy(i, n):
        span = pl.ds(ROUTES[i].first // STEPS, ROUTES[i].count // STEPS)
        positions = cache_ref.shape[2]
        if n == 0:
            src = cache_ref.at[span, pl.ds(0, latent)]
            dst = dense.at[span, pl.ds(0, latent), pl.ds(0, positions)]
        else:
            left = cache_ref.shape[1] - latent
            src = cache_ref.at[span, pl.ds(latent, left)]
            dst = dense.at[span, pl.ds(0, left), pl.ds(positions, positions)]
        return pltpu.make_async_copy(src, dst, cache_sem.at[i, n])

    def weight_copy(n):
        src = (wg_ref, wu_ref, wd_ref)[n]
        dst = (wg_v, wu_v, wd_v)[n]
        return pltpu.make_async_copy(src, dst, w_sem.at[n])

    out_copy = pltpu.make_async_copy(wo_ref, wo_v, wo_sem)
    for n in range(2):
        cache_copy(0, n).start()
    out_copy.start()
    for i in range(1, len(ROUTES)):
        for n in range(2):
            cache_copy(i, n).start()

    for b in range(tokens // 16):
        span = slice(b * 16, b * 16 + 16)
        q_s[span, :] = jnp.concatenate(
            [q_ref[4 * b + i].astype(F32) for i in range(4)], axis=0
        ).astype(BF)
        nk_s[span, :] = jnp.concatenate(
            [nk_ref[4 * b + i].astype(F32) for i in range(4)], axis=0
        ).astype(BF)

    token_r = lax.broadcasted_iota(jnp.int32, (tokens, tokens), 0)
    token_c = lax.broadcasted_iota(jnp.int32, (tokens, tokens), 1)
    diagonal = token_r == token_c
    same = (token_r // STEPS == token_c // STEPS) & (token_c <= token_r)
    fresh = lax.dot_general(q_s[...], nk_s[...], NT, preferred_element_type=F32)
    new_s[...] = jnp.where(same, fresh * score_scale, -1e30)

    which = lax.broadcasted_iota(jnp.int32, (16, 1), 0) // STEPS
    position = lax.broadcasted_iota(jnp.int32, (16, cache_ref.shape[2]), 1)
    rope = cache_ref.shape[1] - latent

    def attend(b):
        span = pl.ds(pl.multiple_of(b * 16, 16), 16)
        first = b * 4
        q16 = q_s[span, :]

        def score(row):
            return matmul(q16[:, :latent], dense[row, :, : position.shape[1]]) + matmul(
                q16[:, latent:], dense[row, :rope, position.shape[1] :]
            )

        scores = score(first)
        length = jnp.full(position.shape, len_ref[first])
        for n in range(1, 4):
            scores = jnp.where(which == n, score(first + n), scores)
            length = jnp.where(which == n, len_ref[first + n], length)
        scores = jnp.where(position < length, scores * score_scale, -1e30)
        new = new_s[span, :]
        highest = jnp.maximum(jnp.max(scores, -1, keepdims=True), jnp.max(new, -1, keepdims=True))
        cache_exp = jnp.exp(scores - highest)
        new_exp = jnp.exp(new - highest)
        total = jnp.sum(cache_exp, -1, keepdims=True) + jnp.sum(new_exp, -1, keepdims=True)
        cache_w = (cache_exp / total).astype(BF)
        new_w = (new_exp / total).astype(BF)

        def mix(row):
            return lax.dot_general(
                cache_w, dense[row, :, : position.shape[1]], NT, preferred_element_type=F32
            )

        context = mix(first)
        for n in range(1, 4):
            context = jnp.where(which == n, mix(first + n), context)
        context = context + matmul(new_w, nk_s[:, :latent])
        ctx_s[span, :] = context.astype(BF)

    def meta_copy(d):
        tile = meta_v.at[fs, me]
        return remote(tile, tile, meta_sem.at[0], meta_sem.at[1], place.plus(d))

    def all_copies(buffer, sem):
        tiles = buffer.at[pl.ds(0, peers - 1)]
        return remote(tiles, tiles, sem.at[0], sem.at[1], me)

    for i, route in enumerate(ROUTES):
        for n in range(2):
            cache_copy(i, n).wait()
        each(route.first // 16, (route.first + route.count) // 16, attend)
        if i == 0:
            for n in range(3):
                weight_copy(n).start()

    out_copy.wait()
    for c in range(wo_v.shape[1] // 128):
        span = slice(c * 128, c * 128 + 128)
        wo_t[span, :] = wo_v[:, span].T
    gain = jnp.zeros((1, depth), F32)
    for j in range(peers):
        part = slice(j * depth, (j + 1) * depth)
        res_s[j, :, :depth] = res_ref[0, :, part].astype(F32)
        gain = jnp.where(me == j, gain_ref[:, part], gain)
    gain = jnp.concatenate([gain, jnp.zeros((1, WIDE - depth), F32)], axis=1)
    lane = lax.broadcasted_iota(jnp.int32, (1, rows), 1)
    here = lane // (STEPS * TOP) == lax.rem(me, 4)
    own_ids = jnp.where(here, spread(ids_ref[0].astype(F32), rows), 0.0)
    own_gates = jnp.where(here, spread(gates_ref[0], rows), 0.0)
    meta_v[fs, me] = jnp.concatenate([own_ids, own_gates, jnp.zeros((6, rows), F32)], axis=0)
    values = matmul(ctx_s[...], wv_ref[...]).astype(BF)
    pl.semaphore_wait(barrier, peers - 1 + groups - 1)

    def project(n):
        offsets = [offset_of(4 * n + k) for k in range(4)]
        for offset in offsets:
            j = place.plus(offset)
            span = pl.ds(pl.multiple_of(j * depth, 16), depth)
            part = lax.dot_general(wo_t[span, :], values, NT, preferred_element_type=F32)
            send_v[j] = part.astype(BF)
        for offset in offsets:
            for h in heads:
                h.send(offset)

    each(0, peers // 4, project)

    def res_copy(d):
        peer = place.plus(d)
        return remote(res_s.at[peer], res_r.at[me], res_sem.at[0], res_sem.at[1], peer)

    for d in FAR_FIRST:
        meta_copy(d).start()
        res_copy(d).start()
    res_r[me] = res_s[me]

    for h in heads:
        each(h.route.n[2], h.route.plane, h.step)
    for h in heads:
        each(0, h.route.n[2], h.step)
    pair_lane = lax.broadcasted_iota(jnp.int32, (1, rows), 1)
    slot_c = lax.broadcasted_iota(jnp.int32, (rows, experts * block), 1)
    slot_r = lax.broadcasted_iota(jnp.int32, (experts * block, rows), 0)

    def read_meta(q):
        piece = from_group(q)

        def one(n):
            info = meta_v[piece, 4 * n]
            for i in range(1, 4):
                info = info + meta_v[piece, 4 * n + i]
            j = piece * per + n
            code = info[0:1, :].astype(jnp.int32) * block + pair_lane // TOP
            code_s[j] = code
            code = jnp.sum(jnp.where(diagonal, code, 0), 1, keepdims=True)
            part_v[j] = (code == slot_c).astype(F32).astype(BF)
            gate_s[j] = info[1:2, :]

        each(0, per, one)

    for h in heads:
        h.turns()
    all_copies(meta_v.at[fs], meta_sem).wait_recv()
    for d in range(1, groups):
        group_copy(0, d, meta_v.at[fs]).start()
    read_meta(0)
    for h in heads:
        h.add(att_t)
    all_copies(res_s, res_sem).wait_recv()

    attended = jnp.concatenate([att_t[...], jnp.zeros((WIDE - depth, tokens), F32)], axis=0).T
    own_res = jnp.concatenate([res_r[n][:, :depth] for n in range(peers)], axis=0)
    own_res = jnp.concatenate([own_res, jnp.zeros((tokens, WIDE - depth), F32)], axis=1)
    attended = attended + own_res
    att[...] = attended
    x_v[fs] = (attended * gain).astype(BF)
    for d in range(1, groups):
        group_copy(1, d, x_v.at[fs]).start()
    column = jnp.sum(attended * attended, -1, keepdims=True)
    row = jnp.sum(jnp.where(diagonal, column, 0.0), 0, keepdims=True)
    ssq_s[...] = jnp.broadcast_to(row, ssq_s.shape)

    def ssq_copy(d):
        return remote(ssq_s, ssq_r.at[d], ssq_sem.at[0], ssq_sem.at[1], lax.rem(me + d, peers))

    ssq_r[0] = ssq_s[...]
    each(1, peers, lambda d: ssq_copy(d).start())

    def multiply(first, count, x):
        def some(n):
            for e in [4 * n + k for k in range(4)]:
                spot = pl.ds(pl.multiple_of(e * block, block), block)
                gate = matmul(x, wg_v[e]).astype(BF)
                up = matmul(x, wu_v[e]).astype(BF)
                dense[first : first + count, spot, :half] = gate.reshape(count, block, half)
                dense[first : first + count, spot, half:] = up.reshape(count, block, half)

        each(0, experts // 4, some)

    def pick(i):
        found = []
        for k in range(2):
            q = (2 * i + k) // per
            n = lax.rem((2 * i + k) // NY, 2) * NY + lax.rem(place.y + 2 * i + k, NY)
            j = from_group(q) * per + n
            found.append((j, matmul(part_v[j], dense[q * per + n]).astype(BF)))
        for j, part in found:
            part_v[j] = part
        for j, _ in found:
            offset = (
                lax.rem(j // (NZ * NY) + NX - place.x, NX),
                lax.rem(lax.rem(j // NY, NZ) + NZ - place.z, NZ),
                lax.rem(lax.rem(j, NY) + NY - place.y, NY),
            )
            for s in sums:
                s.send(offset)

    def pick_group(q):
        each(q * per // 2, (q + 1) * per // 2, pick)

    def relay(q):
        p = from_group(q)
        x_off = lax.rem(p // 2 + NX - place.x, NX)
        z_low = 2 * lax.rem(p, 2)

        def z_off(i):
            return lax.rem(z_low + i + NZ - place.z, NZ)

        @pl.when(lax.rem(p, 2) == place.z // 2)
        def _():
            each(0, NY, lambda i: sums[0].step(i * NX + x_off))

        each(0, 2, lambda i: sums[1].step(x_off * NZ + z_off(i)))

        @pl.when(x_off == 0)
        def _():
            each(0, 2 * NY, lambda i: sums[2].step(z_off(i // NY) * NY + lax.rem(i, NY)))

    weight_copy(0).wait()
    weight_copy(1).wait()
    multiply(0, per, x_v[fs][:, :depth])
    pick_group(0)

    for q in range(1, groups):
        group_copy(0, q, meta_v.at[from_group(q)]).wait_recv()
        group_copy(1, q, x_v.at[from_group(q)]).wait_recv()
        read_meta(q)
    others = [x_v[from_group(q)][:, :depth] for q in range(1, groups)]
    multiply(per, peers - per, jnp.concatenate(others, axis=0))
    pick_group(1)
    relay(0)
    pick_group(2)
    relay(1)
    pick_group(3)
    all_copies(ssq_r.at[pl.ds(1, peers - 1)], ssq_sem).wait_recv()
    sum_v[fs] = jnp.sum(ssq_r[...], axis=0)
    for d in range(1, groups):
        group_copy(2, d, sum_v.at[fs]).start()
    relay(2)
    relay(3)

    for s in sums:
        s.turns()

    def build(n):
        for j in (2 * n, 2 * n + 1):
            spread_s[j] = (code_s[j] == slot_r).astype(F32).astype(BF)

    each(0, peers // 2, build)
    for s in sums:
        s.add(acc)

    for d in range(1, groups):
        group_copy(2, d, sum_v.at[from_group(d)]).wait_recv()
    token = block * lax.rem(me, per) + token_r // TOP
    squares = jnp.sum(jnp.where(token == token_c, sum_v[me // per][:1, :], 0.0), 1, keepdims=True)
    scale = lax.rsqrt(squares / (depth * peers) + 1e-06)
    weight = jnp.sum(jnp.where(diagonal, gate_s[me], 0.0), 1, keepdims=True)
    gate = acc[:, :half] * scale
    up = acc[:, half:] * scale
    hid_v[me] = (gate / (1.0 + jnp.exp(-gate)) * up * weight).astype(BF)

    for g in gathers:
        g.begin()
    for g in gathers:
        g.push2(0)
    for g in gathers:
        g.push1(0, 0)
    for g in gathers:
        for d3 in range(1, g.route.n[2]):
            g.relay_last(d3)
    for g in gathers:
        each(g.route.n[2], g.route.plane, g.relay_middle)

    def expand(n):
        offsets = [offset_of(2 * n), offset_of(2 * n + 1)]
        for offset in offsets:
            for g in gathers:
                g.arrive(offset)
        blocks = [place.minus(offset) for offset in offsets]
        full = [matmul(spread_s[j], hid_v[j]).astype(BF) for j in blocks]
        for j, rows_of in zip(blocks, full):
            spot = pl.ds(pl.multiple_of(j * block, block), block)
            dense[:, spot, :half] = rows_of.reshape(experts, block, half)

    each(0, peers // 2, expand)
    weight_copy(2).wait()

    def shares(pieces):
        spots = [pl.ds(pl.multiple_of(p * tokens, tokens), tokens) for p in pieces]

        def some(n, total):
            for k in range(4):
                e = 4 * n + k
                both = jnp.concatenate([dense[e, spot, :half] for spot in spots], axis=0)
                total = total + lax.dot_general(both, wd_v[e], NT, preferred_element_type=F32)
            return total

        start = jnp.zeros((len(pieces) * tokens, depth), F32)
        return lax.fori_loop(0, experts // 4, some, start)

    def routed_copy(d):
        peer = lax.rem(fs + d, groups)
        return pltpu.make_async_remote_copy(
            src_ref=routed_v.at[peer],
            dst_ref=routed_r.at[d],
            send_sem=g_send.at[3, d],
            recv_sem=g_recv.at[3, d],
            device_id={"fsdp": peer},
            device_id_type=MESH,
        )

    mixed = att[:, :depth]
    for pair in ((2, 3), (1, 0)):
        both = shares([lax.rem(fs + d, groups) for d in pair])
        for k, d in enumerate(pair):
            share = both[k * tokens : (k + 1) * tokens]
            if d > 0:
                routed_v[lax.rem(fs + d, groups), :, :depth] = share.astype(BF)
                routed_copy(d).start()
            else:
                mixed = mixed + share
    for d in range(1, groups):
        routed_copy(d).wait_recv()
        mixed = mixed + routed_r[d][:, :depth].astype(F32)
    for j in range(peers):
        home_s[j, :, :depth] = mixed[j * own_rows : (j + 1) * own_rows, :]

    def home_copy(d):
        peer = place.plus(d)
        return remote(home_s.at[peer], home_r.at[me], home_sem.at[0], home_sem.at[1], peer)

    for d in FAR_FIRST:
        home_copy(d).start()
    home_r[me] = home_s[me]
    for s in heads + sums + gathers:
        s.finish()
    for d in range(1, groups):
        routed_copy(d).wait_send()
        group_copy(0, d, meta_v.at[fs]).wait_send()
        group_copy(1, d, x_v.at[fs]).wait_send()
        group_copy(2, d, sum_v.at[fs]).wait_send()

    all_copies(ssq_r, ssq_sem).wait_send()
    all_copies(meta_v.at[fs], meta_sem).wait_send()
    all_copies(res_s, res_sem).wait_send()
    all_copies(home_s, home_sem).wait_recv()
    for j in range(peers):
        out_ref[0, :, j * depth : (j + 1) * depth] = home_r[j][:, :depth]
    all_copies(home_s, home_sem).wait_send()


def shards(
    residual,
    gain,
    queries,
    new_keys,
    cache,
    lengths,
    w_value,
    w_out,
    w_gate,
    w_up,
    w_down,
    expert_ids,
    gates,
):
    peers = lax.axis_size("exp")
    groups = lax.axis_size("fsdp")
    group_rows, steps, _, key = queries.shape
    tokens = group_rows * steps
    experts, depth, half = w_gate.shape
    block = tokens * groups // peers
    rows = block * TOP
    smem, dma = pl.BlockSpec(memory_space=pltpu.SMEM), pltpu.SemaphoreType.DMA
    scratch = [
        pltpu.VMEM((peers, experts * block, 2 * half), BF),
        pltpu.VMEM(w_out.shape[1:], BF),
        pltpu.VMEM((w_out.shape[2], w_out.shape[1]), BF),
        pltpu.VMEM((peers, steps, WIDE), F32),
        pltpu.VMEM((peers, steps, WIDE), F32),
        pltpu.VMEM((tokens, key), BF),
        pltpu.VMEM((tokens, key), BF),
        pltpu.VMEM((tokens, tokens), F32),
        pltpu.VMEM((tokens, w_value.shape[1]), BF),
        pltpu.VMEM((peers, depth, tokens), BF),
        pltpu.VMEM((depth, tokens), F32),
        pltpu.VMEM((tokens, WIDE), F32),
        pltpu.VMEM((8, tokens), F32),
        pltpu.VMEM((peers, 8, tokens), F32),
        pltpu.VMEM((groups, 8, tokens), F32),
        pltpu.VMEM((groups, tokens, WIDE), BF),
        pltpu.VMEM((groups, peers, 8, rows), F32),
        pltpu.VMEM(w_gate.shape, BF),
        pltpu.VMEM(w_gate.shape, BF),
        pltpu.VMEM(w_gate.shape, BF),
        pltpu.VMEM((peers, rows, 2 * half), BF),
        pltpu.VMEM((rows, 2 * half), F32),
        pltpu.VMEM((peers, rows, half), BF),
        pltpu.VMEM((peers, experts * block, rows), BF),
        pltpu.VMEM((peers, 1, rows), jnp.int32),
        pltpu.VMEM((peers, 1, rows), F32),
        pltpu.VMEM((groups, tokens, WIDE), BF),
        pltpu.VMEM((groups, tokens, WIDE), BF),
        pltpu.VMEM((peers, steps, WIDE), F32),
        pltpu.VMEM((peers, steps, WIDE), F32),
        dma((len(ROUTES), 2)),
        dma,
        dma((3,)),
        dma((2,)),
        dma((2,)),
        dma((2,)),
        dma((2,)),
        dma((4, groups)),
        dma((4, groups)),
    ]
    for route in HEAD_ROUTES:
        scratch += reduce_scratch(route, tokens)
    for route in ROUTES:
        scratch += reduce_scratch(route, 2 * half)
    for route in ROUTES:
        scratch += gather_scratch(route)
    return pl.pallas_call(
        functools.partial(layer_kernel, peers, groups),
        out_shape=jax.ShapeDtypeStruct(residual.shape, F32),
        in_specs=[smem, vmem(), vmem(), anywhere(), vmem(), anywhere()]
        + [vmem()] * 4
        + [anywhere()] * 3,
        out_specs=vmem(),
        scratch_shapes=scratch,
        compiler_params=pltpu.CompilerParams(
            collective_id=0, has_side_effects=True, vmem_limit_bytes=HIGH
        ),
        name="layer",
    )(
        lengths,
        queries[:, :, 0, :],
        new_keys,
        cache,
        w_value[0],
        w_out[0],
        residual,
        gain.reshape(1, -1),
        expert_ids,
        gates,
        w_gate,
        w_up,
        w_down,
    )


def solution(mesh):
    return jax.shard_map(
        shards,
        mesh=mesh,
        in_specs=(
            P(("fsdp", "exp"), None, None),
            P(),
            P("fsdp", None, "exp", None),
            P("fsdp", None, None),
            P("fsdp", None, None),
            P("fsdp"),
            P("exp", None, None),
            P("exp", None, None),
            P(None, "exp", "fsdp"),
            P(None, "exp", "fsdp"),
            P(None, "exp", "fsdp"),
            P(("fsdp", "exp"), None, None),
            P(("fsdp", "exp"), None, None),
        ),
        out_specs=P(("fsdp", "exp"), None, None),
        check_vma=False,
    )
```
